128 devices in a mesh: gx: 16 (over x, z), gy: 8 (over y, core).
Axes of the slice: x: 4, y: 4, z: 4, core: 2. Of those that a mesh axis runs over, the one named last changes fastest.
Arguments:
- swath_bands: bfloat16 [131072, 6, 128], P(('gx', 'gy')), may hold values from 0 to 1
- clear_weight: bfloat16 [131072, 128], P(('gx', 'gy')), may hold values from 0.049804688 to 1
- owners: int32 [131072, 1], P(('gx', 'gy')), may hold values from 0 to 127; in each aligned block of 1024 rows (0 to 1023, 1024 to 2047, ...) at most 12 rows name the same one
- tile_row: int32 [131072], P(('gx', 'gy')), may hold values from 0 to 255
- columns: int32 [131072, 128], P(('gx', 'gy')), may hold values from 0 to 255
- counts: int32 [128], P(('gx', 'gy')), may hold values from 1 to 1024, 98304 in all
- conduct_x: float32 [2048, 4096], P('gy', 'gx'), may hold values from 0.02 to 0.2
- conduct_y: float32 [2048, 4096], P('gy', 'gx'), may hold values from 0.02 to 0.2
Outputs:
- gridded: float32 [6, 2048, 4096], P(None, 'gy', 'gx')
- coverage: float32 [2048, 4096], P('gy', 'gx')
The draws below stay inside these ranges and needn't reach their ends.
Inputs may be any that keep to these rules, and one draw needn't show every extreme that they name: `owners`: within the rows of one device no owner is named by more than 12 blocks, a bound that some block reaches. The counts sum to 98304, and some device's count is 1024.
All inputs are finite; a program needn't handle non-finite values.
Results may differ from the reference program's by a relative error of at most 0.0017.
Values may be sent and summed in bfloat16 or wider, within the bound.
No kernel may reach another device: no remote copies, remote signals or barrier semaphores. Data moves between devices by JAX's collectives and lax.ppermute only.
A program may use at most 64 MiB of HBM per device.

```python
import math
import jax
import jax.numpy as jnp
import numpy as np

BANDS = 6
PIX = 128
BLK_DEV = 1024
TH = 256
TW = 256
CAP = 12
BLOCKS = 131072
NROWS = 2048
NCOLS = 4096
N_GX = 16
N_GY = 8


def set_ends(values, key, low, top_value):
    place = [jax.random.randint(jax.random.fold_in(key, axis), (), 0, length) for axis, length in enumerate(values.shape)]
    widest = values.shape.index(max(values.shape))
    beside = place[:widest] + [(place[widest] + 1) % values.shape[widest]] + place[widest + 1:]
    return values.at[tuple(place)].set(low).at[tuple(beside)].set(top_value)


def level_of(key, dims, cuts, smallest, high):
    loudness = 1.0
    for axis_at, blocks in cuts:
        heights = jax.random.uniform(jax.random.fold_in(jax.random.fold_in(key, 6), axis_at), (blocks,), jnp.float32, smallest / len(cuts), high / len(cuts))
        loudness = loudness * jnp.repeat(jnp.exp(heights), dims[axis_at] // blocks).reshape((-1,) + (1,) * (len(dims) - 1 - axis_at))
    return loudness


def profile(count, total, bound, lean):
    portions = [(1 << 20) // math.isqrt(rank ** lean) + 1 for rank in range(2, count + 1)]
    spare, given = total - bound - (count - 1), [1] * (count - 1)
    while spare > 0:
        movable = [i for i in range(count - 1) if given[i] < bound]
        pool, remaining = sum([portions[i] for i in movable]), spare
        for i in movable:
            more = min(bound - given[i], max(1, remaining * portions[i] // pool), spare)
            given[i] = given[i] + more
            spare = spare - more
    return np.array([bound] + given)


def uneven_parts(own_key, number_of, total, most, slope):
    if number_of == 2:
        one = jax.random.randint(own_key, (), max(1, total - most), min(most, total - 1) + 1)
        return jnp.stack([one, total - one])
    sizes = jnp.asarray(profile(number_of, total, most, slope), jnp.int32)
    pairs = (number_of - 1) // 2
    donor, receiver = sizes[1:1 + 2 * pairs:2], sizes[2:2 + 2 * pairs:2]
    slack = jnp.minimum(donor - 1, most - receiver)
    moved = jax.random.randint(jax.random.fold_in(own_key, 1), (pairs,), 0, 1 << 20) % (slack + 1)
    sizes = sizes.at[1:1 + 2 * pairs:2].set(donor - moved).at[2:2 + 2 * pairs:2].set(receiver + moved)
    return sizes[jax.random.permutation(jax.random.fold_in(own_key, 2), number_of)]


def shared_out(own_key, own, number, rows, count, top, bound, slope):
    ranking = jax.random.permutation(own_key, count)
    heavy_load, usual = shares(count, rows * top, bound, slope, True), shares(count, rows * top, bound, slope, False)
    places = jnp.arange(count)

    def named(lengths, rotation):
        used = int((lengths > 0).sum())
        fixed = max(1, used // 4)
        passed = fixed + (places - fixed + rotation * (used - fixed)) % max(1, count - fixed)
        return jnp.zeros((count,), jnp.int32).at[ranking[jnp.where(places < fixed, places, passed)]].set(jnp.asarray(lengths, jnp.int32))

    lengths = jnp.where(number % 4 == 0, named(heavy_load, number // 4), named(usual, number - number // 4 - 1))
    mixed = jax.random.permutation(jax.random.fold_in(own, 3), count)
    giver, receiver = mixed[0:count // 2 * 2:2], mixed[1:count // 2 * 2:2]
    slack = jnp.minimum(lengths[giver] - 1, bound - lengths[receiver]) // 2
    slack = jnp.where((giver == ranking[0]) | (receiver == ranking[0]) | (lengths[receiver] == 0), 0, jnp.maximum(slack, 0))
    passed = jax.random.randint(jax.random.fold_in(own, 4), (count // 2,), 0, 1 << 20) % (slack + 1)
    lengths = lengths.at[giver].add(-passed).at[receiver].add(passed)
    labels = jnp.searchsorted(jnp.cumsum(lengths), jnp.arange(rows * top), side="right").astype(jnp.int32)
    grid = labels.reshape(top, rows).T
    grid = grid[jax.random.permutation(jax.random.fold_in(own, 1), rows)]
    rotation = jax.random.randint(jax.random.fold_in(own, 2), (rows, 1), 0, top)
    return jnp.take_along_axis(grid, (jnp.arange(top)[None, :] + rotation) % top, axis=1)


def shares(amount, total, most, lean, full):
    loads = [(1 << 20) // math.isqrt(grade ** lean) + 1 for grade in range(1, amount + 1)]
    largest = most if full else min(most, max(-(-total // amount), total * loads[0] // sum(loads)))
    least = 1 if total - largest >= amount - 1 else 0
    given, surplus = [largest] + [least] * (amount - 1), total - largest - least * (amount - 1)
    while surplus > 0:
        free = [i for i in range(1, amount) if given[i] < largest] or [i for i in range(1, amount) if given[i] < most]
        whole, budget = sum([loads[i] for i in free]), surplus
        for i in free:
            addition = min(most - given[i], max(1, budget * loads[i] // whole), surplus)
            given[i] = given[i] + addition
            surplus = surplus - addition
    return np.array(given)


def setup_inputs(seed: int = 0) -> dict:
    splits = jax.random.split(jax.random.key(seed), 9)
    swath_bands = jnp.clip(1.0 * jax.random.uniform(splits[0], (BLOCKS, BANDS, PIX), jnp.float32) ** level_of(splits[0], (BLOCKS, BANDS, PIX), ((0, 128),), -0.2, 0.2), 0.0, 1.0).astype(jnp.bfloat16)
    clear_weight = jnp.clip(jnp.exp(math.log(1.0) - 2.9996462 * jax.random.uniform(splits[1], (BLOCKS, PIX), jnp.float32) ** level_of(splits[1], (BLOCKS, PIX), ((0, 128),), -0.2, 0.2)), 0.049804688, 1.0).astype(jnp.bfloat16)
    owners_keys = jax.random.split(jax.random.fold_in(splits[2], 1), BLOCKS // BLK_DEV)
    owners_turns = jax.random.permutation(jax.random.fold_in(splits[2], 3), BLOCKS // BLK_DEV)
    owners = jax.vmap(lambda own, number: shared_out(jax.random.fold_in(splits[2], 2), own, number, BLK_DEV, N_GX * N_GY, 1, CAP, 2))(owners_keys, owners_turns).reshape((BLOCKS, 1))
    tile_row = set_ends(jax.random.randint(splits[3], (BLOCKS,), 0, TH), jax.random.fold_in(splits[3], 1), 0, TH - 1).astype(jnp.int32)
    columns = set_ends(jax.random.randint(splits[4], (BLOCKS, PIX), 0, TW), jax.random.fold_in(splits[4], 1), 0, TW - 1).astype(jnp.int32)
    counts = uneven_parts(splits[5], N_GX * N_GY, 3 * BLOCKS // 4, BLK_DEV, 2).astype(jnp.int32)
    conduct_x = jnp.clip(jnp.exp(math.log(0.2) - 2.3025851 * jax.random.uniform(splits[6], (NROWS, NCOLS), jnp.float32) ** level_of(splits[6], (NROWS, NCOLS), ((0, 8), (1, 16)), -0.2, 0.2)), 0.02, 0.2)
    conduct_y = jnp.clip(jnp.exp(math.log(0.2) - 2.3025851 * jax.random.uniform(splits[7], (NROWS, NCOLS), jnp.float32) ** level_of(splits[7], (NROWS, NCOLS), ((0, 8), (1, 16)), -0.2, 0.2)), 0.02, 0.2)
    return {"swath_bands": swath_bands, "clear_weight": clear_weight, "owners": owners, "tile_row": tile_row, "columns": columns, "counts": counts, "conduct_x": conduct_x, "conduct_y": conduct_y}


def smooth_once(current, along_x, along_y):
    padded = jnp.pad(current, ((0, 0), (1, 1), (1, 1)))
    east_west = padded[:, 1:-1, 2:] + padded[:, 1:-1, :-2] - 2.0 * current
    north_south = padded[:, 2:, 1:-1] + padded[:, :-2, 1:-1] - 2.0 * current
    return current + along_x[None] * east_west + along_y[None] * north_south


def reference(swath_bands, clear_weight, owners, tile_row, columns, counts, conduct_x, conduct_y):
    position = jnp.arange(BLK_DEV * N_GX * N_GY, dtype=jnp.int32)
    device_of = (position // BLK_DEV).astype(jnp.int32)
    is_live = ((position % BLK_DEV) < counts[device_of]).astype(jnp.float32)
    pixel_weight = clear_weight.astype(jnp.float32) * is_live[:, None]
    weighted_bands = (swath_bands.astype(jnp.float32) * pixel_weight[:, None, :]).astype(jnp.bfloat16)
    weighted = jnp.concatenate([weighted_bands, pixel_weight.astype(jnp.bfloat16)[:, None, :]], axis=1)
    target = owners[:, 0].astype(jnp.int32)
    grid_row = ((target % N_GY) * TH + tile_row).astype(jnp.int32)
    grid_col = ((target // N_GY)[:, None] * TW + columns).astype(jnp.int32)
    flat_bin = (grid_row[:, None] * (TW * N_GX) + grid_col).astype(jnp.int32)
    values = jnp.transpose(weighted.astype(jnp.float32), (0, 2, 1)).reshape(-1, BANDS + 1)
    summed = jax.ops.segment_sum(values, flat_bin.reshape(-1), num_segments=TH * N_GY * TW * N_GX)
    fields = jnp.transpose(summed).reshape(BANDS + 1, TH * N_GY, TW * N_GX)
    for step_index in range(2):
        fields = smooth_once(fields, conduct_x, conduct_y)
    coverage = fields[BANDS]
    gridded = fields[:BANDS] / jnp.maximum(coverage, 0.15)[None]
    return gridded, coverage
```

```python
import functools

import jax
import jax.numpy as jnp
from jax import lax
from jax.experimental import pallas as pl
from jax.experimental.pallas import tpu as pltpu
from jax.sharding import PartitionSpec as P

CAPACITY = 12
SLOTS = CAPACITY + 1
FLOOR = 0.15
HALO = 2

f32 = jnp.float32
bf16 = jnp.bfloat16
i32 = jnp.int32


def iota(shape, dim):
    return lax.broadcasted_iota(i32, shape, dim)


def ring(count, step):
    return [(i, (i + step) % count) for i in range(count)]


def pack_kernel(
    count_ref,
    owner_ref,
    row_ref,
    swath_ref,
    weight_ref,
    cols_ref,
    out_ref,
    weight_f,
    cols_f,
    codes_f,
    slot_v,
    slot_s,
    sem,
):
    blocks = swath_ref.shape[0]
    devices = out_ref.shape[0] // SLOTS
    live_count = count_ref[0]
    owner = owner_ref[...]
    live = iota((1, blocks), 1) < live_count
    owner = jnp.where(live, owner, -1)
    named = (iota((devices, blocks), 0) == owner).astype(f32)
    named16 = named.astype(bf16)
    earlier = (iota((blocks, blocks), 0) < iota((blocks, blocks), 1)).astype(f32).astype(bf16)
    before = jnp.dot(named16, earlier, preferred_element_type=f32)
    rank = jnp.sum(named * before, axis=0, keepdims=True).astype(i32)
    slot_v[...] = jnp.where(live, owner * SLOTS + rank, CAPACITY)
    copy = pltpu.make_async_copy(slot_v, slot_s, sem)
    copy.start()
    place = jnp.where(
        iota((128, blocks), 0) == rank, (row_ref[...] + 1).astype(f32), 0.0
    ).astype(bf16)
    codes_f[...] = lax.dot_general(
        named16, place, (((1,), (1,)), ((), ())), preferred_element_type=f32
    )
    weight_f[...] = weight_ref[...].astype(f32)
    cols_f[...] = cols_ref[...].astype(f32)

    @pl.loop(0, devices)
    def _(t):
        out_ref[pl.ds(t * SLOTS, SLOTS)] = jnp.zeros((SLOTS, 8, 128), bf16)

    copy.wait()

    @pl.loop(0, (live_count + 7) // 8)
    def _(group):
        for i in range(8):
            b = group * 8 + i
            slot = slot_s[0, b]
            w = weight_f[pl.ds(b, 1), :]
            c = cols_f[pl.ds(b, 1), :]
            bands = swath_ref[b].astype(f32) * w
            out_ref[slot] = jnp.concatenate([bands, w, c], axis=0).astype(bf16)

    @pl.loop(0, devices, unroll=4)
    def _(t):
        code = codes_f[pl.ds(t, 1), :]
        out_ref[t * SLOTS + CAPACITY] = jnp.broadcast_to(code, (8, 128)).astype(bf16)


def pack(counts, owners, tile_row, swath, weight, columns, devices):
    blocks = swath.shape[0]
    vmem = pl.BlockSpec(memory_space=pltpu.VMEM)
    return pl.pallas_call(
        pack_kernel,
        out_shape=jax.ShapeDtypeStruct((devices * SLOTS, 8, 128), bf16),
        in_specs=[pl.BlockSpec(memory_space=pltpu.SMEM)] + [vmem] * 5,
        out_specs=vmem,
        scratch_shapes=[
            pltpu.VMEM((blocks, 128), f32),
            pltpu.VMEM((blocks, 128), f32),
            pltpu.VMEM((devices, 128), f32),
            pltpu.VMEM((1, blocks), i32),
            pltpu.SMEM((1, blocks), i32),
            pltpu.SemaphoreType.DMA,
        ],
        compiler_params=pltpu.CompilerParams(vmem_limit_bytes=48 << 20),
        name="pack",
    )(counts, owners, tile_row, swath, weight, columns)


def bin_kernel(
    msg_ref, acc_ref, top_ref, bottom_ref, left_ref, right_ref, codes_v, codes_s, sem
):
    sources = msg_ref.shape[0] // SLOTS
    height, _, width = acc_ref.shape

    @pl.loop(0, sources, unroll=4)
    def _(s):
        tile = msg_ref[s * SLOTS + CAPACITY].astype(f32)
        codes_v[pl.ds(s, 1), :] = tile[0:1, :].astype(i32)

    copy = pltpu.make_async_copy(codes_v, codes_s, sem)
    copy.start()

    @pl.loop(0, height // 8)
    def _(g):
        acc_ref[pl.ds(g * 8, 8)] = jnp.zeros((8, 8, width), f32)

    copy.wait()
    lanes = iota((width, 128), 0).astype(f32).astype(bf16)
    one = jnp.ones((width, 128), bf16)
    zero = jnp.zeros((width, 128), bf16)
    empty = jnp.zeros((8, 128), bf16)

    @pl.loop(0, sources)
    def _(s):
        for k in range(0, CAPACITY, 2):
            first = msg_ref[s * SLOTS + k]
            second = msg_ref[s * SLOTS + k + 1]
            hits = jnp.concatenate(
                [
                    jnp.where(lanes == first[7:8, :], one, zero),
                    jnp.where(lanes == second[7:8, :], one, zero),
                ],
                axis=1,
            )
            values = jnp.concatenate(
                [
                    jnp.concatenate([first, empty], axis=1),
                    jnp.concatenate([empty, second], axis=1),
                ],
                axis=0,
            )
            sums = lax.dot_general(
                values, hits, (((1,), (1,)), ((), ())), preferred_element_type=f32
            )
            for j in range(2):
                row = jnp.maximum(codes_s[s, k + j] - 1, 0)
                acc_ref[row] += sums[8 * j : 8 * j + 8]

    top_ref[...] = acc_ref[0:HALO]
    bottom_ref[...] = acc_ref[height - HALO : height]
    lane = iota((8, 128), 1)
    blank = jnp.zeros((8, 128), f32)

    def edges(j, carry):
        here = lane // 2 == j
        result = []
        for q in range(4):
            near = pltpu.roll(acc_ref[q * 64 + j, :, 0:128], 2 * j, 1)
            result.append(jnp.where(here, near, carry[2 * q]))
            far = pltpu.roll(acc_ref[q * 64 + j, :, width - 128 : width], 2 * j + 2, 1)
            result.append(jnp.where(here, far, carry[2 * q + 1]))
        return tuple(result)

    strips = lax.fori_loop(0, 64, edges, (blank,) * 8)
    for q in range(4):
        left_ref[q] = strips[2 * q]
        right_ref[q] = strips[2 * q + 1]


def bin_blocks(message, height, width):
    sources = message.shape[0] // SLOTS
    vmem = pl.BlockSpec(memory_space=pltpu.VMEM)
    shape = lambda *dims: jax.ShapeDtypeStruct(dims, f32)
    return pl.pallas_call(
        bin_kernel,
        out_shape=(
            shape(height, 8, width),
            shape(HALO, 8, width),
            shape(HALO, 8, width),
            shape(height // 64, 8, 128),
            shape(height // 64, 8, 128),
        ),
        in_specs=[vmem],
        out_specs=(vmem,) * 5,
        scratch_shapes=[
            pltpu.VMEM((sources, 128), i32),
            pltpu.SMEM((sources, 128), i32),
            pltpu.SemaphoreType.DMA,
        ],
        compiler_params=pltpu.CompilerParams(vmem_limit_bytes=48 << 20),
        name="bin",
    )(message)


def smooth_row(above, current, below, along_x, along_y):
    total = current.shape[1]
    east = pltpu.roll(current, total - 1, 1)
    west = pltpu.roll(current, 1, 1)
    east_west = east + west - 2.0 * current
    north_south = below + above - 2.0 * current
    return current + along_x * east_west + along_y * north_south


def smooth_kernel(
    flags_ref,
    acc_ref,
    up_ref,
    down_ref,
    west_ref,
    east_ref,
    cx_ref,
    cy_ref,
    gridded_ref,
    coverage_ref,
    ext,
    once,
    twice,
):
    height, _, width = acc_ref.shape
    has_up, has_down = flags_ref[0], flags_ref[1]
    has_west, has_east = flags_ref[2], flags_ref[3]
    lane = iota((8, 128), 1)
    blank = jnp.zeros((8, 128), f32)

    ext[HALO : HALO + height, :, 0:width] = acc_ref[...]
    ext[0:HALO, :, 0:width] = jnp.where(has_up > 0, up_ref[...], 0.0)
    ext[HALO + height :, :, 0:width] = jnp.where(has_down > 0, down_ref[...], 0.0)

    @pl.loop(0, 64)
    def _(j):
        for q in range(4):
            east = pltpu.roll(east_ref[q], 128 - 2 * j, 1)
            west = pltpu.roll(west_ref[q], 126 - 2 * j, 1)
            east = jnp.where((lane < 2) & (has_east > 0), east, 0.0)
            side = jnp.where((lane >= 126) & (has_west > 0), west, east)
            ext[HALO + q * 64 + j, :, width:] = side

    for tile, row, flag in ((4, HALO - 1, has_up), (5, HALO + height, has_down)):
        east = jnp.where((lane < 1) & (has_east > 0), east_ref[tile], 0.0)
        side = jnp.where((lane >= 127) & (has_west > 0), west_ref[tile], east)
        ext[row, :, width:] = jnp.where(flag > 0, side, 0.0)
    ext[0, :, width:] = blank
    ext[HALO + height + 1, :, width:] = blank

    @pl.loop(0, height + 2)
    def _(r):
        once[r] = smooth_row(
            ext[r], ext[r + 1], ext[r + 2], cx_ref[pl.ds(r, 1), :], cy_ref[pl.ds(r, 1), :]
        )

    @pl.loop(0, height)
    def _(r):
        along_x = cx_ref[pl.ds(r + 1, 1), :]
        along_y = cy_ref[pl.ds(r + 1, 1), :]
        fresh = smooth_row(once[r], once[r + 1], once[r + 2], along_x, along_y)
        for half in range(width // 128):
            twice[half, pl.ds(pl.multiple_of(r * 8, 8), 8), :] = fresh[
                :, half * 128 : half * 128 + 128
            ]

    @pl.loop(0, height // 8)
    def _(g):
        rows = pl.ds(pl.multiple_of(g * 8, 8), 8)
        for half in range(width // 128):
            cols = pl.ds(half * 128, 128)
            coverage = twice[half, pl.ds(g * 64 + 6, 8, stride=8), :]
            coverage_ref[rows, cols] = coverage
            scale = 1.0 / jnp.maximum(coverage, FLOOR)
            for c in range(6):
                gridded_ref[c, rows, cols] = twice[half, pl.ds(g * 64 + c, 8, stride=8), :] * scale


def smooth(flags, acc, up, down, west, east, cx, cy):
    height, _, width = acc.shape
    vmem = pl.BlockSpec(memory_space=pltpu.VMEM)
    return pl.pallas_call(
        smooth_kernel,
        out_shape=(
            jax.ShapeDtypeStruct((6, height, width), f32),
            jax.ShapeDtypeStruct((height, width), f32),
        ),
        in_specs=[pl.BlockSpec(memory_space=pltpu.SMEM)] + [vmem] * 7,
        out_specs=(vmem, vmem),
        scratch_shapes=[
            pltpu.VMEM((height + 2 * HALO, 8, width + 128), f32),
            pltpu.VMEM((height + 2, 8, width + 128), f32),
            pltpu.VMEM((width // 128, height * 8, 128), f32),
        ],
        compiler_params=pltpu.CompilerParams(vmem_limit_bytes=48 << 20),
        name="smooth",
    )(flags, acc, up, down, west, east, cx, cy)


def extend(block, up, down, west, east, flags):
    height, width = block.shape
    up = jnp.where(flags[0] > 0, up, 0.0)
    down = jnp.where(flags[1] > 0, down, 0.0)
    west = jnp.where(flags[2] > 0, west, 0.0)
    east = jnp.where(flags[3] > 0, east, 0.0)
    core = jnp.concatenate([up[None], block, down[None]], axis=0)
    middle = jnp.zeros((height, 126), f32)
    side = jnp.concatenate([east[:, None], middle, west[:, None]], axis=1)
    side = jnp.pad(side, ((1, 1), (0, 0)))
    return jnp.concatenate([core, side], axis=1)


def body(swath_bands, clear_weight, owners, tile_row, columns, counts, conduct_x, conduct_y):
    blocks = swath_bands.shape[0]
    height, width = conduct_x.shape
    across, along = lax.axis_size("gx"), lax.axis_size("gy")
    devices = across * along
    gx, gy = lax.axis_index("gx"), lax.axis_index("gy")
    flags = jnp.stack([gy > 0, gy < along - 1, gx > 0, gx < across - 1]).astype(i32)
    message = pack(
        counts,
        owners.reshape(1, blocks),
        tile_row.reshape(1, blocks),
        swath_bands,
        clear_weight,
        columns,
        devices,
    )
    arrived = lax.all_to_all(
        message.reshape(devices, SLOTS, 8, 128),
        ("gx", "gy"),
        split_axis=0,
        concat_axis=0,
        tiled=True,
    ).reshape(devices * SLOTS, 8, 128)

    both = jnp.stack([conduct_x, conduct_y])
    from_up = lax.ppermute(both[:, height - 1, :], "gy", ring(along, 1))
    from_down = lax.ppermute(both[:, 0, :], "gy", ring(along, -1))
    from_west = lax.ppermute(both[:, :, width - 1], "gx", ring(across, 1))
    from_east = lax.ppermute(both[:, :, 0], "gx", ring(across, -1))
    cx, cy = (
        extend(both[i], from_up[i], from_down[i], from_west[i], from_east[i], flags)
        for i in range(2)
    )

    acc, top, bottom, left, right = bin_blocks(arrived, height, width)
    up = lax.ppermute(bottom, "gy", ring(along, 1))
    down = lax.ppermute(top, "gy", ring(along, -1))
    near = jnp.concatenate([left, up[1:2, :, 0:128], down[0:1, :, 0:128]], axis=0)
    far = jnp.concatenate([right, up[1:2, :, width - 128 :], down[0:1, :, width - 128 :]], axis=0)
    west = lax.ppermute(far, "gx", ring(across, 1))
    east = lax.ppermute(near, "gx", ring(across, -1))
    return smooth(flags, acc, up, down, west, east, cx, cy)


def solution(mesh):
    return jax.shard_map(
        body,
        mesh=mesh,
        in_specs=(
            P(("gx", "gy"), None, None),
            P(("gx", "gy"), None),
            P(("gx", "gy"), None),
            P(("gx", "gy")),
            P(("gx", "gy"), None),
            P(("gx", "gy")),
            P("gy", "gx"),
            P("gy", "gx"),
        ),
        out_specs=(P(None, "gy", "gx"), P("gy", "gx")),
        check_vma=False,
    )
```

```python
import functools

import jax
import jax.numpy as jnp
from jax import lax
from jax.experimental import pallas as pl
from jax.experimental.pallas import tpu as pltpu
from jax.sharding import PartitionSpec as P

CAPACITY = 12
SLOTS = CAPACITY + 1
COUNT_LANE = 16
GROUP = 64
ROWS = 16
FLOOR = 0.15
HALO = 2

f32 = jnp.float32
bf16 = jnp.bfloat16
i32 = jnp.int32


def iota(shape, dim):
    return lax.broadcasted_iota(i32, shape, dim)


def ring(count, step):
    return [(i, (i + step) % count) for i in range(count)]


def pack_kernel(
    count_ref,
    owner_ref,
    row_ref,
    swath_ref,
    weight_ref,
    cols_ref,
    out_ref,
    done_ref,
    owner_v,
    row_v,
    swath_v,
    weight_v,
    cols_v,
    rows_f,
    codes_f,
    slot_v,
    slot_s,
    sem,
    load_sems,
):
    bands, blocks, _ = swath_ref.shape
    loads = [
        pltpu.make_async_copy(source, target, load_sems.at[i])
        for i, (source, target) in enumerate(
            (
                (owner_ref, owner_v),
                (row_ref, row_v),
                (weight_ref, weight_v),
                (cols_ref, cols_v),
                (swath_ref, swath_v),
            )
        )
    ]
    for load in loads:
        load.start()
    done_ref[...] = jnp.zeros((8, 128), f32)
    devices = out_ref.shape[0] // SLOTS
    live_count = count_ref[0]
    loads[0].wait()
    owner = owner_v[...]
    live = iota((1, blocks), 1) < live_count
    owner = jnp.where(live, owner, -1)
    named = (iota((devices, blocks), 0) == owner).astype(f32)
    named16 = named.astype(bf16)
    earlier = (iota((blocks, blocks), 0) < iota((blocks, blocks), 1)).astype(f32).astype(bf16)
    before = jnp.dot(named16, earlier, preferred_element_type=f32)
    rank = jnp.sum(named * before, axis=0, keepdims=True).astype(i32)
    slot_v[...] = jnp.where(live, owner * SLOTS + rank, CAPACITY)
    copy = pltpu.make_async_copy(slot_v, slot_s, sem)
    copy.start()
    entry = iota((128, blocks), 0)
    loads[1].wait()
    place = jnp.where(entry == rank, (row_v[...] + 1).astype(f32), 0.0)
    place = jnp.where(entry == COUNT_LANE, 1.0, place).astype(bf16)
    codes_f[...] = lax.dot_general(
        named16, place, (((1,), (1,)), ((), ())), preferred_element_type=f32
    )

    @pl.loop(0, devices)
    def _(t):
        out_ref[pl.ds(t * SLOTS, SLOTS)] = jnp.zeros((SLOTS, 8, 128), bf16)

    for load in loads[2:]:
        load.wait()

    @pl.loop(0, blocks // 16, unroll=4)
    def _(g):
        near = pl.ds(pl.multiple_of(g * 16, 16), 16)
        weight = weight_v[near, :].astype(f32)
        for c in range(bands):
            rows_f[pl.ds(g * 128 + c, 16, stride=8), :] = swath_v[c, near, :].astype(f32) * weight
        rows_f[pl.ds(g * 128 + bands, 16, stride=8), :] = weight
        rows_f[pl.ds(g * 128 + bands + 1, 16, stride=8), :] = cols_v[near, :].astype(f32)

    copy.wait()

    @pl.loop(0, (live_count + 15) // 16)
    def _(group):
        for i in range(16):
            b = group * 16 + i
            out_ref[slot_s[0, b]] = rows_f[pl.ds(pl.multiple_of(b * 8, 8), 8), :].astype(bf16)

    @pl.loop(0, devices, unroll=4)
    def _(t):
        code = codes_f[pl.ds(t, 1), :]
        out_ref[t * SLOTS + CAPACITY] = jnp.broadcast_to(code, (8, 128)).astype(bf16)


def pack(counts, owners, tile_row, swath, weight, columns, devices):
    blocks = weight.shape[0]
    vmem = pl.BlockSpec(memory_space=pltpu.VMEM)
    return pl.pallas_call(
        pack_kernel,
        out_shape=(
            jax.ShapeDtypeStruct((devices * SLOTS, 8, 128), bf16),
            jax.ShapeDtypeStruct((8, 128), f32),
        ),
        in_specs=[pl.BlockSpec(memory_space=pltpu.SMEM)]
        + [pl.BlockSpec(memory_space=pltpu.HBM)] * 5,
        out_specs=(vmem, vmem),
        scratch_shapes=[
            pltpu.VMEM((1, blocks), i32),
            pltpu.VMEM((1, blocks), i32),
            pltpu.VMEM(swath.shape, bf16),
            pltpu.VMEM(weight.shape, bf16),
            pltpu.VMEM(columns.shape, i32),
            pltpu.VMEM((blocks * 8, 128), f32),
            pltpu.VMEM((devices, 128), f32),
            pltpu.VMEM((1, blocks), i32),
            pltpu.SMEM((1, blocks), i32),
            pltpu.SemaphoreType.DMA,
            pltpu.SemaphoreType.DMA((5,)),
        ],
        compiler_params=pltpu.CompilerParams(vmem_limit_bytes=60 << 20),
        name="pack",
    )(counts, owners, tile_row, swath, weight, columns)


def bin_kernel(
    msg_ref,
    after_ref,
    acc_ref,
    top_ref,
    bottom_ref,
    left_ref,
    right_ref,
    codes_v,
    codes_s,
    pairs_s,
    sem,
):
    sources = msg_ref.shape[0] // SLOTS
    height, width = acc_ref.shape[0] - 1, acc_ref.shape[2]

    @pl.loop(0, sources // 8)
    def _(g):
        for i in range(8):
            s = g * 8 + i
            tile = msg_ref[s * SLOTS + CAPACITY].astype(f32)
            codes_v[pl.ds(s, 1), :] = tile[0:1, :].astype(i32)

    copy = pltpu.make_async_copy(codes_v, codes_s, sem)
    copy.start()

    @pl.loop(0, height // 16)
    def _(g):
        acc_ref[pl.ds(g * 16, 16)] = jnp.zeros((16, 8, width), f32)

    acc_ref[height] = jnp.zeros((8, width), f32)
    copy.wait()

    def note_source(s, total):
        for p in range(CAPACITY // 2):
            pairs_s[total + p] = s * 128 + 2 * p
        return total + (codes_s[s, COUNT_LANE] + 1) // 2

    total = lax.fori_loop(0, sources, note_source, 0)

    @pl.loop(0, GROUP // 8)
    def _(g):
        for i in range(8):
            pairs_s[total + g * 8 + i] = CAPACITY

    low_ids = iota((64, 128), 0).astype(f32)
    quarter_ids = (iota((32, 128), 0) // 8).astype(f32)
    empty = jnp.zeros((32, 128), bf16)

    @pl.loop(0, (total + GROUP - 1) // GROUP)
    def _(group):
        for j in range(GROUP):
            pair = pairs_s[group * GROUP + j]
            source, first = pair // 128, pair % 128
            slot = source * SLOTS + first
            values, hits = [], []
            for i in range(2):
                block = msg_ref[slot + i].astype(f32)
                col = block[7:8, :]
                quarter = jnp.where(
                    col >= 128.0,
                    jnp.where(col >= 192.0, 3.0, 2.0),
                    jnp.where(col >= 64.0, 1.0, 0.0),
                )
                low = col - 64.0 * quarter
                block4 = jnp.concatenate([block] * 4, axis=0)
                values.append(jnp.where(quarter_ids == quarter, block4, 0.0).astype(bf16))
                hits.append(jnp.where(low_ids == low, 1.0, 0.0).astype(bf16))
            values = jnp.concatenate(
                [
                    jnp.concatenate([values[0], empty], axis=1),
                    jnp.concatenate([empty, values[1]], axis=1),
                ],
                axis=0,
            )
            sums = lax.dot_general(
                values,
                jnp.concatenate(hits, axis=1),
                (((1,), (1,)), ((), ())),
                preferred_element_type=f32,
            )
            for i in range(2):
                code = codes_s[source, first + i]
                row = jnp.where(code > 0, code - 1, height)
                for h in range(2):
                    o = 32 * i + 16 * h
                    acc_ref[row, :, 128 * h : 128 * h + 128] += jnp.concatenate(
                        [sums[o : o + 8], sums[o + 8 : o + 16]], axis=1
                    )

    top_ref[...] = acc_ref[0:HALO]
    bottom_ref[...] = acc_ref[height - HALO : height]
    lane = iota((8, 128), 1)
    blank = jnp.zeros((8, 128), f32)

    def edges(j, carry):
        here = lane // 2 == j
        result = []
        for q in range(4):
            near = pltpu.roll(acc_ref[q * 64 + j, :, 0:128], 2 * j, 1)
            result.append(jnp.where(here, near, carry[2 * q]))
            far = pltpu.roll(acc_ref[q * 64 + j, :, width - 128 : width], 2 * j + 2, 1)
            result.append(jnp.where(here, far, carry[2 * q + 1]))
        return tuple(result)

    strips = lax.fori_loop(0, 64, edges, (blank,) * 8, unroll=8)
    for q in range(4):
        left_ref[q] = strips[2 * q]
        right_ref[q] = strips[2 * q + 1]


def bin_blocks(message, after, height, width):
    sources = message.shape[0] // SLOTS
    vmem = pl.BlockSpec(memory_space=pltpu.VMEM)
    shape = lambda *dims: jax.ShapeDtypeStruct(dims, f32)
    return pl.pallas_call(
        bin_kernel,
        out_shape=(
            shape(height + 1, 8, width),
            shape(HALO, 8, width),
            shape(HALO, 8, width),
            shape(height // 64, 8, 128),
            shape(height // 64, 8, 128),
        ),
        in_specs=[vmem, pl.BlockSpec(memory_space=pl.ANY)],
        out_specs=(vmem,) * 5,
        scratch_shapes=[
            pltpu.VMEM((sources, 128), i32),
            pltpu.SMEM((sources, 128), i32),
            pltpu.SMEM((sources * CAPACITY // 2 + GROUP + 8,), i32),
            pltpu.SemaphoreType.DMA,
        ],
        compiler_params=pltpu.CompilerParams(vmem_limit_bytes=48 << 20),
        name="bin",
    )(message, after)


def smooth_row(above, current, below, along_x, along_y):
    total = current.shape[1]
    east = pltpu.roll(current, total - 1, 1)
    west = pltpu.roll(current, 1, 1)
    east_west = east + west - 2.0 * current
    north_south = below + above - 2.0 * current
    return current + along_x * east_west + along_y * north_south


def smooth_kernel(
    flags_ref,
    acc_ref,
    up_ref,
    down_ref,
    west_ref,
    east_ref,
    cx_ref,
    cy_ref,
    gridded_ref,
    coverage_ref,
    ext,
    once,
    twice,
):
    height, width = acc_ref.shape[0] - 1, acc_ref.shape[2]
    has_up, has_down = flags_ref[0], flags_ref[1]
    has_west, has_east = flags_ref[2], flags_ref[3]
    lane = iota((8, 128), 1)
    blank = jnp.zeros((8, 128), f32)

    ext[HALO : HALO + height, :, 0:width] = acc_ref[0:height]
    ext[0:HALO, :, 0:width] = jnp.where(has_up > 0, up_ref[...], 0.0)
    ext[HALO + height :, :, 0:width] = jnp.where(has_down > 0, down_ref[...], 0.0)

    @pl.loop(0, 64, unroll=16)
    def _(j):
        for q in range(4):
            east = pltpu.roll(east_ref[q], 128 - 2 * j, 1)
            west = pltpu.roll(west_ref[q], 126 - 2 * j, 1)
            east = jnp.where((lane < 2) & (has_east > 0), east, 0.0)
            side = jnp.where((lane >= 126) & (has_west > 0), west, east)
            ext[HALO + q * 64 + j, :, width:] = side

    for tile, row, flag in ((4, HALO - 1, has_up), (5, HALO + height, has_down)):
        east = jnp.where((lane < 1) & (has_east > 0), east_ref[tile], 0.0)
        side = jnp.where((lane >= 127) & (has_west > 0), west_ref[tile], east)
        ext[row, :, width:] = jnp.where(flag > 0, side, 0.0)
    ext[0, :, width:] = blank
    ext[HALO + height + 1, :, width:] = blank

    def pass_rows(source, start, count, shift):
        rows = [source[start + i] for i in range(count + 2)]
        for i in range(count):
            along_x = cx_ref[pl.ds(start + i + shift, 1), :]
            along_y = cy_ref[pl.ds(start + i + shift, 1), :]
            yield i, smooth_row(rows[i], rows[i + 1], rows[i + 2], along_x, along_y)

    for r in (0, height + 1):
        for _, fresh in pass_rows(ext, r, 1, 0):
            once[r] = fresh

    @pl.loop(0, height // ROWS)
    def _(g):
        start = g * ROWS + 1
        for i, fresh in pass_rows(ext, start, ROWS, 0):
            once[start + i] = fresh

    @pl.loop(0, height // ROWS)
    def _(g):
        start = g * ROWS
        for i, fresh in pass_rows(once, start, ROWS, 1):
            for half in range(width // 128):
                twice[half, pl.ds(pl.multiple_of((start + i) * 8, 8), 8), :] = fresh[
                    :, half * 128 : half * 128 + 128
                ]

    @pl.loop(0, height // 8, unroll=2)
    def _(g):
        rows = pl.ds(pl.multiple_of(g * 8, 8), 8)
        for half in range(width // 128):
            cols = pl.ds(half * 128, 128)
            coverage = twice[half, pl.ds(g * 64 + 6, 8, stride=8), :]
            coverage_ref[rows, cols] = coverage
            scale = 1.0 / jnp.maximum(coverage, FLOOR)
            for c in range(6):
                gridded_ref[c, rows, cols] = twice[half, pl.ds(g * 64 + c, 8, stride=8), :] * scale


def smooth(flags, acc, up, down, west, east, cx, cy):
    height, width = acc.shape[0] - 1, acc.shape[2]
    vmem = pl.BlockSpec(memory_space=pltpu.VMEM)
    return pl.pallas_call(
        smooth_kernel,
        out_shape=(
            jax.ShapeDtypeStruct((6, height, width), f32),
            jax.ShapeDtypeStruct((height, width), f32),
        ),
        in_specs=[pl.BlockSpec(memory_space=pltpu.SMEM)] + [vmem] * 7,
        out_specs=(vmem, vmem),
        scratch_shapes=[
            pltpu.VMEM((height + 2 * HALO, 8, width + 128), f32),
            pltpu.VMEM((height + 2, 8, width + 128), f32),
            pltpu.VMEM((width // 128, height * 8, 128), f32),
        ],
        compiler_params=pltpu.CompilerParams(vmem_limit_bytes=48 << 20),
        name="smooth",
    )(flags, acc, up, down, west, east, cx, cy)


def edge_kernel(after_ref, cx_ref, cy_ref, top_ref, bottom_ref, left_ref, right_ref):
    height, width = cx_ref.shape
    for i, block in enumerate((cx_ref, cy_ref)):
        top_ref[i : i + 1, :] = block[0:1, :]
        bottom_ref[i : i + 1, :] = block[height - 1 : height, :]
        left_ref[i : i + 1, :] = block[:, 0:128].T[0:1, :]
        right_ref[i : i + 1, :] = block[:, width - 128 : width].T[127:128, :]


def coefficient_edges(after, cx, cy):
    height, width = cx.shape
    vmem = pl.BlockSpec(memory_space=pltpu.VMEM)
    row = jax.ShapeDtypeStruct((2, width), f32)
    column = jax.ShapeDtypeStruct((2, height), f32)
    return pl.pallas_call(
        edge_kernel,
        out_shape=(row, row, column, column),
        in_specs=[vmem] * 3,
        out_specs=(vmem,) * 4,
        name="coefficient_edges",
    )(after, cx, cy)


def extend_kernel(
    flags_ref, cx_ref, cy_ref, up_ref, down_ref, west_ref, east_ref, ext_x, ext_y, done_ref
):
    done_ref[...] = jnp.zeros((8, 128), f32)
    height, width = cx_ref.shape
    lane = iota((height, 128), 1)
    for i, (block, ext) in enumerate(((cx_ref, ext_x), (cy_ref, ext_y))):
        up = jnp.where(flags_ref[0] > 0, up_ref[i : i + 1, :], 0.0)
        down = jnp.where(flags_ref[1] > 0, down_ref[i : i + 1, :], 0.0)
        west = jnp.where(flags_ref[2] > 0, west_ref[i : i + 1, :], 0.0)
        east = jnp.where(flags_ref[3] > 0, east_ref[i : i + 1, :], 0.0)
        ext[0:1, 0:width] = up
        ext[1 : height + 1, 0:width] = block[...]
        ext[height + 1 : height + 2, 0:width] = down
        west = jnp.broadcast_to(west, (128, height)).T
        east = jnp.broadcast_to(east, (128, height)).T
        side = jnp.where(lane == 0, east, jnp.where(lane == 127, west, 0.0))
        ext[0:1, width:] = jnp.zeros((1, 128), f32)
        ext[1 : height + 1, width:] = side
        ext[height + 1 : height + 2, width:] = jnp.zeros((1, 128), f32)


def extend(flags, cx, cy, up, down, west, east):
    height, width = cx.shape
    vmem = pl.BlockSpec(memory_space=pltpu.VMEM)
    wide = jax.ShapeDtypeStruct((height + 2, width + 128), f32)
    return pl.pallas_call(
        extend_kernel,
        out_shape=(wide, wide, jax.ShapeDtypeStruct((8, 128), f32)),
        in_specs=[pl.BlockSpec(memory_space=pltpu.SMEM)] + [vmem] * 6,
        out_specs=(vmem,) * 3,
        name="extend",
    )(flags, cx, cy, up, down, west, east)


def body(swath_bands, clear_weight, owners, tile_row, columns, counts, conduct_x, conduct_y):
    blocks = swath_bands.shape[0]
    height, width = conduct_x.shape
    across, along = lax.axis_size("gx"), lax.axis_size("gy")
    devices = across * along
    gx, gy = lax.axis_index("gx"), lax.axis_index("gy")
    flags = jnp.stack([gy > 0, gy < along - 1, gx > 0, gx < across - 1]).astype(i32)
    message, packed = pack(
        counts,
        owners.reshape(1, blocks),
        tile_row.reshape(1, blocks),
        jnp.transpose(swath_bands, (1, 0, 2)),
        clear_weight,
        columns,
        devices,
    )
    arrived = lax.all_to_all(
        message.reshape(devices, SLOTS, 8, 128),
        ("gx", "gy"),
        split_axis=0,
        concat_axis=0,
        tiled=True,
    ).reshape(devices * SLOTS, 8, 128)

    first_rows, last_rows, first_cols, last_cols = coefficient_edges(packed, conduct_x, conduct_y)
    cx, cy, extended = extend(
        flags,
        conduct_x,
        conduct_y,
        lax.ppermute(last_rows, "gy", ring(along, 1)),
        lax.ppermute(first_rows, "gy", ring(along, -1)),
        lax.ppermute(last_cols, "gx", ring(across, 1)),
        lax.ppermute(first_cols, "gx", ring(across, -1)),
    )

    acc, top, bottom, left, right = bin_blocks(arrived, extended, height, width)
    up = lax.ppermute(bottom, "gy", ring(along, 1))
    down = lax.ppermute(top, "gy", ring(along, -1))
    near = jnp.concatenate([left, up[1:2, :, 0:128], down[0:1, :, 0:128]], axis=0)
    far = jnp.concatenate([right, up[1:2, :, width - 128 :], down[0:1, :, width - 128 :]], axis=0)
    west = lax.ppermute(far, "gx", ring(across, 1))
    east = lax.ppermute(near, "gx", ring(across, -1))
    return smooth(flags, acc, up, down, west, east, cx, cy)


def solution(mesh):
    return jax.shard_map(
        body,
        mesh=mesh,
        in_specs=(
            P(("gx", "gy"), None, None),
            P(("gx", "gy"), None),
            P(("gx", "gy"), None),
            P(("gx", "gy")),
            P(("gx", "gy"), None),
            P(("gx", "gy")),
            P("gy", "gx"),
            P("gy", "gx"),
        ),
        out_specs=(P(None, "gy", "gx"), P("gy", "gx")),
        check_vma=False,
    )
```

```python
import functools

import jax
import jax.numpy as jnp
from jax import lax
from jax.experimental import pallas as pl
from jax.experimental.pallas import tpu as pltpu
from jax.sharding import PartitionSpec as P

CAPACITY = 12
SLOTS = CAPACITY + 1
COUNT_LANE = 14
CODES = 16
GROUP = 64
ROWS = 16
FLOOR = 0.15
HALO = 2

f32 = jnp.float32
bf16 = jnp.bfloat16
i32 = jnp.int32


def iota(shape, dim):
    return lax.broadcasted_iota(i32, shape, dim)


def ring(count, step):
    return [(i, (i + step) % count) for i in range(count)]


def pack_kernel(
    count_ref,
    owner_ref,
    row_ref,
    swath_ref,
    weight_ref,
    cols_ref,
    out_ref,
    done_ref,
    owner_v,
    row_v,
    swath_v,
    weight_v,
    cols_v,
    rows_f,
    codes_f,
    slot_v,
    slot_s,
    sem,
    load_sems,
):
    bands, blocks, _ = swath_ref.shape
    loads = [
        pltpu.make_async_copy(source, target, load_sems.at[i])
        for i, (source, target) in enumerate(
            (
                (owner_ref, owner_v),
                (row_ref, row_v),
                (weight_ref, weight_v),
                (cols_ref, cols_v),
                (swath_ref, swath_v),
            )
        )
    ]
    for load in loads:
        load.start()
    done_ref[...] = jnp.zeros((8, 128), f32)
    devices = out_ref.shape[0] // SLOTS
    live_count = count_ref[0]
    earlier = (iota((blocks, blocks), 0) < iota((blocks, blocks), 1)).astype(f32).astype(bf16)

    @pl.loop(0, devices // 2)
    def _(t):
        out_ref[pl.ds(t * 2 * SLOTS, 2 * SLOTS)] = jnp.zeros((2 * SLOTS, 8, 128), bf16)

    loads[0].wait()
    owner = owner_v[...]
    live = iota((1, blocks), 1) < live_count
    owner = jnp.where(live, owner, -1)
    named = (iota((devices, blocks), 0) == owner).astype(f32)
    named16 = named.astype(bf16)
    before = jnp.dot(named16, earlier, preferred_element_type=f32)
    rank = jnp.sum(named * before, axis=0, keepdims=True).astype(i32)
    slot_v[...] = jnp.where(live, owner * SLOTS + rank, CAPACITY)
    copy = pltpu.make_async_copy(slot_v, slot_s, sem)
    copy.start()
    entry = iota((128, blocks), 0)
    loads[1].wait()
    place = jnp.where(entry == rank, (row_v[...] + 1).astype(f32), 0.0)
    place = jnp.where(entry == COUNT_LANE, 1.0, place).astype(bf16)
    codes_f[...] = lax.dot_general(
        named16, place, (((1,), (1,)), ((), ())), preferred_element_type=f32
    )

    for load in loads[2:]:
        load.wait()

    @pl.loop(0, blocks // 16, unroll=4)
    def _(g):
        near = pl.ds(pl.multiple_of(g * 16, 16), 16)
        weight = weight_v[near, :].astype(f32)
        for c in range(bands):
            rows_f[pl.ds(g * 128 + c, 16, stride=8), :] = swath_v[c, near, :].astype(f32) * weight
        rows_f[pl.ds(g * 128 + bands, 16, stride=8), :] = weight
        rows_f[pl.ds(g * 128 + bands + 1, 16, stride=8), :] = cols_v[near, :].astype(f32)

    copy.wait()

    @pl.loop(0, (live_count + 15) // 16)
    def _(group):
        for i in range(16):
            b = group * 16 + i
            out_ref[slot_s[0, b]] = rows_f[pl.ds(pl.multiple_of(b * 8, 8), 8), :].astype(bf16)

    @pl.loop(0, devices, unroll=4)
    def _(t):
        code = codes_f[pl.ds(t, 1), :]
        out_ref[t * SLOTS + CAPACITY] = jnp.broadcast_to(code, (8, 128)).astype(bf16)


def pack(counts, owners, tile_row, swath, weight, columns, devices):
    blocks = weight.shape[0]
    vmem = pl.BlockSpec(memory_space=pltpu.VMEM)
    return pl.pallas_call(
        pack_kernel,
        out_shape=(
            jax.ShapeDtypeStruct((devices * SLOTS, 8, 128), bf16),
            jax.ShapeDtypeStruct((8, 128), f32),
        ),
        in_specs=[pl.BlockSpec(memory_space=pltpu.SMEM)]
        + [pl.BlockSpec(memory_space=pltpu.HBM)] * 5,
        out_specs=(vmem, vmem),
        scratch_shapes=[
            pltpu.VMEM((1, blocks), i32),
            pltpu.VMEM((1, blocks), i32),
            pltpu.VMEM(swath.shape, bf16),
            pltpu.VMEM(weight.shape, bf16),
            pltpu.VMEM(columns.shape, i32),
            pltpu.VMEM((blocks * 8, 128), f32),
            pltpu.VMEM((devices, 128), f32),
            pltpu.VMEM((1, blocks), i32),
            pltpu.SMEM((1, blocks), i32),
            pltpu.SemaphoreType.DMA,
            pltpu.SemaphoreType.DMA((5,)),
        ],
        compiler_params=pltpu.CompilerParams(vmem_limit_bytes=60 << 20),
        name="pack",
    )(counts, owners, tile_row, swath, weight, columns)


def bin_kernel(
    msg_ref,
    edge_top,
    edge_bottom,
    edge_left,
    edge_right,
    acc_ref,
    top_ref,
    bottom_ref,
    left_ref,
    right_ref,
    codes_v,
    codes_t,
    codes_s,
    pairs_s,
    sem,
):
    sources = msg_ref.shape[0] // SLOTS
    height, width = acc_ref.shape[0] - 1, acc_ref.shape[2]

    @pl.loop(0, sources // 8)
    def _(g):
        for i in range(8):
            s = g * 8 + i
            tile = msg_ref[s * SLOTS + CAPACITY].astype(f32)
            codes_v[pl.ds(s, 1), :] = tile[0:1, :]

    codes_t[...] = codes_v[...].T[0:CODES, :].astype(i32)
    copy = pltpu.make_async_copy(codes_t, codes_s, sem)
    copy.start()

    @pl.loop(0, height // 16)
    def _(g):
        acc_ref[pl.ds(g * 16, 16)] = jnp.zeros((16, 8, width), f32)

    acc_ref[height] = jnp.zeros((8, width), f32)
    copy.wait()

    def note_source(s, total):
        for p in range(CAPACITY // 2):
            pairs_s[total + p] = s * 128 + 2 * p
        return total + (codes_s[COUNT_LANE, s] + 1) // 2

    total = lax.fori_loop(0, sources, note_source, 0, unroll=8)

    @pl.loop(0, GROUP // 8)
    def _(g):
        for i in range(8):
            pairs_s[total + g * 8 + i] = CAPACITY

    low_ids = iota((64, 128), 0).astype(f32)
    quarter_ids = (iota((32, 128), 0) // 8).astype(f32)
    empty = jnp.zeros((32, 128), bf16)

    @pl.loop(0, (total + GROUP - 1) // GROUP)
    def _(group):
        for j in range(GROUP):
            pair = pairs_s[group * GROUP + j]
            source, first = pair // 128, pair % 128
            slot = source * SLOTS + first
            values, hits = [], []
            for i in range(2):
                block = msg_ref[slot + i].astype(f32)
                col = block[7:8, :]
                quarter = jnp.where(
                    col >= 128.0,
                    jnp.where(col >= 192.0, 3.0, 2.0),
                    jnp.where(col >= 64.0, 1.0, 0.0),
                )
                low = col - 64.0 * quarter
                block4 = jnp.concatenate([block] * 4, axis=0)
                values.append(jnp.where(quarter_ids == quarter, block4, 0.0).astype(bf16))
                hits.append(jnp.where(low_ids == low, 1.0, 0.0).astype(bf16))
            values = jnp.concatenate(
                [
                    jnp.concatenate([values[0], empty], axis=1),
                    jnp.concatenate([empty, values[1]], axis=1),
                ],
                axis=0,
            )
            sums = lax.dot_general(
                values,
                jnp.concatenate(hits, axis=1),
                (((1,), (1,)), ((), ())),
                preferred_element_type=f32,
            )
            for i in range(2):
                code = codes_s[first + i, source]
                row = jnp.where(code > 0, code - 1, height)
                for h in range(2):
                    o = 32 * i + 16 * h
                    acc_ref[row, :, 128 * h : 128 * h + 128] += jnp.concatenate(
                        [sums[o : o + 8], sums[o + 8 : o + 16]], axis=1
                    )

    top_ref[0:HALO] = acc_ref[0:HALO]
    bottom_ref[0:HALO] = acc_ref[height - HALO : height]
    top_ref[HALO] = edge_top[...]
    bottom_ref[HALO] = edge_bottom[...]
    left_ref[4] = edge_left[...]
    right_ref[4] = edge_right[...]
    lane = iota((8, 128), 1)
    blank = jnp.zeros((8, 128), f32)

    def edges(j, carry):
        here = lane // 2 == j
        result = []
        for q in range(4):
            near = pltpu.roll(acc_ref[q * 64 + j, :, 0:128], 2 * j, 1)
            result.append(jnp.where(here, near, carry[2 * q]))
            far = pltpu.roll(acc_ref[q * 64 + j, :, width - 128 : width], 2 * j + 2, 1)
            result.append(jnp.where(here, far, carry[2 * q + 1]))
        return tuple(result)

    strips = lax.fori_loop(0, 64, edges, (blank,) * 8, unroll=8)
    for q in range(4):
        left_ref[q] = strips[2 * q]
        right_ref[q] = strips[2 * q + 1]


def bin_blocks(message, edges, height, width):
    sources = message.shape[0] // SLOTS
    vmem = pl.BlockSpec(memory_space=pltpu.VMEM)
    shape = lambda *dims: jax.ShapeDtypeStruct(dims, f32)
    return pl.pallas_call(
        bin_kernel,
        out_shape=(
            shape(height + 1, 8, width),
            shape(HALO + 1, 8, width),
            shape(HALO + 1, 8, width),
            shape(height // 64 + 1, 8, 128),
            shape(height // 64 + 1, 8, 128),
        ),
        in_specs=[vmem] * 5,
        out_specs=(vmem,) * 5,
        scratch_shapes=[
            pltpu.VMEM((sources, 128), f32),
            pltpu.VMEM((CODES, sources), i32),
            pltpu.SMEM((CODES, sources), i32),
            pltpu.SMEM((sources * CAPACITY // 2 + GROUP + 8,), i32),
            pltpu.SemaphoreType.DMA,
        ],
        compiler_params=pltpu.CompilerParams(vmem_limit_bytes=16 << 20),
        name="bin",
    )(message, *edges)


def relax(current, east_west, north_south, along_x, along_y):
    return current + along_x * (east_west - 2.0 * current) + along_y * (north_south - 2.0 * current)


def smooth_row(above, current, below, near, along_x, along_y):
    lane = iota((8, 128), 1)
    ahead = [pltpu.roll(half, 1, 1) for half in current]
    back = [pltpu.roll(half, 127, 1) for half in current]
    west = [jnp.where(lane == 0, near, ahead[0]), jnp.where(lane == 0, ahead[0], ahead[1])]
    east = [jnp.where(lane == 127, back[1], back[0]), jnp.where(lane == 127, near, back[1])]
    return [
        relax(current[h], east[h] + west[h], below[h] + above[h], along_x[h], along_y[h])
        for h in range(2)
    ]


def smooth_kernel(
    flags_ref,
    acc_ref,
    up_ref,
    down_ref,
    west_ref,
    east_ref,
    cx_ref,
    cy_ref,
    gridded_ref,
    coverage_ref,
    mix_near,
    mix_far,
    near,
    far,
    once,
    once_near,
    twice,
    side_x,
    side_y,
):
    height, width = acc_ref.shape[0] - 1, acc_ref.shape[2]
    has_up, has_down = flags_ref[0] > 0, flags_ref[1] > 0
    has_west, has_east = flags_ref[2] > 0, flags_ref[3] > 0
    lane = iota((8, 128), 1)

    def halves(ref, row):
        return [ref[row, :, 0:128], ref[row, :, 128:256]]

    def keep(flag, parts):
        return [jnp.where(flag, part, 0.0) for part in parts]

    def along(ref, row):
        line = ref[pl.ds(row, 1), :]
        return [line[:, i : i + 128] for i in (0, 128)]

    for q in range(4):
        west = jnp.where(has_west, west_ref[q], 0.0)
        east = jnp.where(has_east, east_ref[q], 0.0)
        even = lane % 2 == 0
        mix_near[q] = jnp.where(even, pltpu.roll(west, 127, 1), pltpu.roll(east, 127, 1))
        mix_far[q] = jnp.where(even, west, pltpu.roll(east, 126, 1))

    @pl.loop(0, 64, unroll=16)
    def _(j):
        for q in range(4):
            near[q * 64 + j + 1] = pltpu.roll(mix_near[q], 128 - 2 * j, 1)
            far[q * 64 + j] = pltpu.roll(mix_far[q], 128 - 2 * j, 1)

    for tile, row, flag in ((5, 0, has_up), (6, height + 1, has_down)):
        west = jnp.where(has_west & flag, west_ref[tile], 0.0)
        east = jnp.where(has_east & flag, east_ref[tile], 0.0)
        near[row] = jnp.where(lane < 64, pltpu.roll(west, 1, 1), pltpu.roll(east, 127, 1))

    upper = iota((128, 128), 0) < 64
    for i, side in enumerate((side_x, side_y)):
        for half in range(2):
            at = slice(2 * i + half, 2 * i + half + 1)
            west = jnp.where(has_west, west_ref[4, at, :], 0.0)
            east = jnp.where(has_east, east_ref[4, at, :], 0.0)
            both = jnp.where(
                upper, jnp.broadcast_to(west, (128, 128)), jnp.broadcast_to(east, (128, 128))
            )
            side[half * 128 : half * 128 + 128, :] = both.T

    up = [keep(has_up, halves(up_ref, i)) for i in range(2)]
    down = [keep(has_down, halves(down_ref, i)) for i in range(2)]

    def store(ref, row, parts):
        ref[row, :, 0:128] = parts[0]
        ref[row, :, 128:256] = parts[1]

    def coefficients(row):
        return along(cx_ref, row), along(cy_ref, row)

    def beyond(ref, flag):
        return [
            keep(flag, [ref[HALO, i : i + 1, h * 128 : h * 128 + 128] for h in range(2)])
            for i in range(2)
        ]

    store(
        once,
        0,
        smooth_row(up[0], up[1], halves(acc_ref, 0), near[0], *beyond(up_ref, has_up)),
    )
    store(
        once,
        height + 1,
        smooth_row(
            halves(acc_ref, height - 1),
            down[0],
            down[1],
            near[height + 1],
            *beyond(down_ref, has_down),
        ),
    )
    steps = height // ROWS

    @pl.loop(0, steps + 3)
    def _(g):
        block = jnp.clip(g - 3, 0, steps - 1)
        for part in range(ROWS // 8):
            base = block * ROWS + part * 8
            rows = pl.ds(pl.multiple_of(base, 8), 8)
            for half in range(width // 128):
                cols = pl.ds(half * 128, 128)
                coverage = twice[half, pl.ds(base * 8 + 6, 8, stride=8), :]
                coverage_ref[rows, cols] = coverage
                scale = 1.0 / jnp.maximum(coverage, FLOOR)
                for c in range(6):
                    gridded_ref[c, rows, cols] = (
                        twice[half, pl.ds(base * 8 + c, 8, stride=8), :] * scale
                    )
        start = jnp.clip(g - 2, 0, steps - 1) * ROWS
        lines = [halves(once, start + i) for i in range(ROWS + 2)]
        for i in range(ROWS):
            fresh = smooth_row(
                *lines[i : i + 3], once_near[start + i], *coefficients(start + i)
            )
            for half in range(2):
                twice[half, pl.ds(pl.multiple_of((start + i) * 8, 8), 8), :] = fresh[half]
        block = jnp.minimum(g, steps - 1)
        start = block * ROWS
        lines = [halves(acc_ref, start + i) for i in range(ROWS)]
        before = halves(acc_ref, jnp.maximum(start - 1, 0))
        after = halves(acc_ref, jnp.minimum(start + ROWS, height - 1))
        before = [jnp.where(block == 0, up[1][h], before[h]) for h in range(2)]
        after = [jnp.where(block == steps - 1, down[0][h], after[h]) for h in range(2)]
        lines = [before] + lines + [after]
        for i in range(ROWS):
            row = start + i + 1
            along_x, along_y = coefficients(start + i)
            store(once, row, smooth_row(*lines[i : i + 3], near[row], along_x, along_y))
            inner = jnp.where(lane < 64, lines[i + 1][0], lines[i + 1][1])
            once_near[start + i] = relax(
                near[row],
                inner + far[start + i],
                near[row + 1] + near[row - 1],
                side_x[pl.ds(start + i, 1), :],
                side_y[pl.ds(start + i, 1), :],
            )


def smooth(flags, acc, up, down, west, east, cx, cy):
    height, width = acc.shape[0] - 1, acc.shape[2]
    vmem = pl.BlockSpec(memory_space=pltpu.VMEM)
    return pl.pallas_call(
        smooth_kernel,
        out_shape=(
            jax.ShapeDtypeStruct((6, height, width), f32),
            jax.ShapeDtypeStruct((height, width), f32),
        ),
        in_specs=[pl.BlockSpec(memory_space=pltpu.SMEM)] + [vmem] * 7,
        out_specs=(vmem, vmem),
        scratch_shapes=[
            pltpu.VMEM((4, 8, 128), f32),
            pltpu.VMEM((4, 8, 128), f32),
            pltpu.VMEM((height + 2, 8, 128), f32),
            pltpu.VMEM((height, 8, 128), f32),
            pltpu.VMEM((height + 2, 8, width), f32),
            pltpu.VMEM((height, 8, 128), f32),
            pltpu.VMEM((width // 128, height * 8, 128), f32),
            pltpu.VMEM((height, 128), f32),
            pltpu.VMEM((height, 128), f32),
        ],
        compiler_params=pltpu.CompilerParams(vmem_limit_bytes=24 << 20),
        name="smooth",
    )(flags, acc, up, down, west, east, cx, cy)


def edge_kernel(after_ref, flags_ref, cx_ref, cy_ref, top_ref, bottom_ref, left_ref, right_ref):
    height, width = cx_ref.shape
    for ref in (top_ref, bottom_ref, left_ref, right_ref):
        ref[...] = jnp.zeros_like(ref)
    for i, block in enumerate((cx_ref, cy_ref)):
        top_ref[i : i + 1, :] = block[0:1, :]
        bottom_ref[i : i + 1, :] = block[height - 1 : height, :]
        first = block[:, 0:128].T
        last = block[:, width - 128 : width].T
        for half in range(2):
            at = slice(2 * i + half, 2 * i + half + 1)
            left_ref[at, :] = first[0:1, half * 128 : half * 128 + 128]
            right_ref[at, :] = last[127:128, half * 128 : half * 128 + 128]


def coefficient_edges(after, flags, cx, cy):
    width = cx.shape[1]
    vmem = pl.BlockSpec(memory_space=pltpu.VMEM)
    row = jax.ShapeDtypeStruct((8, width), f32)
    column = jax.ShapeDtypeStruct((8, 128), f32)
    return pl.pallas_call(
        edge_kernel,
        out_shape=(row, row, column, column),
        in_specs=[vmem, pl.BlockSpec(memory_space=pltpu.SMEM), vmem, vmem],
        out_specs=(vmem,) * 4,
        compiler_params=pltpu.CompilerParams(vmem_limit_bytes=8 << 20),
        name="coefficient_edges",
    )(after, flags, cx, cy)


def body(swath_bands, clear_weight, owners, tile_row, columns, counts, conduct_x, conduct_y):
    blocks = swath_bands.shape[0]
    height, width = conduct_x.shape
    across, along = lax.axis_size("gx"), lax.axis_size("gy")
    devices = across * along
    gx, gy = lax.axis_index("gx"), lax.axis_index("gy")
    flags = jnp.stack([gy > 0, gy < along - 1, gx > 0, gx < across - 1]).astype(i32)
    message, packed = pack(
        counts,
        owners.reshape(1, blocks),
        tile_row.reshape(1, blocks),
        jnp.transpose(swath_bands, (1, 0, 2)),
        clear_weight,
        columns,
        devices,
    )
    arrived = lax.all_to_all(
        message.reshape(devices, SLOTS, 8, 128),
        ("gx", "gy"),
        split_axis=0,
        concat_axis=0,
        tiled=True,
    ).reshape(devices * SLOTS, 8, 128)

    edges = coefficient_edges(packed, flags, conduct_x, conduct_y)
    acc, top, bottom, left, right = bin_blocks(arrived, edges, height, width)
    up = lax.ppermute(bottom, "gy", ring(along, 1))
    down = lax.ppermute(top, "gy", ring(along, -1))
    near = jnp.concatenate([left, up[1:2, :, 0:128], down[0:1, :, 0:128]], axis=0)
    far = jnp.concatenate([right, up[1:2, :, width - 128 :], down[0:1, :, width - 128 :]], axis=0)
    west = lax.ppermute(far, "gx", ring(across, 1))
    east = lax.ppermute(near, "gx", ring(across, -1))
    return smooth(flags, acc, up, down, west, east, conduct_x, conduct_y)


def solution(mesh):
    return jax.shard_map(
        body,
        mesh=mesh,
        in_specs=(
            P(("gx", "gy"), None, None),
            P(("gx", "gy"), None),
            P(("gx", "gy"), None),
            P(("gx", "gy")),
            P(("gx", "gy"), None),
            P(("gx", "gy")),
            P("gy", "gx"),
            P("gy", "gx"),
        ),
        out_specs=(P(None, "gy", "gx"), P("gy", "gx")),
        check_vma=False,
    )
```

```python
import functools

import jax
import jax.numpy as jnp
from jax import lax
from jax.experimental import pallas as pl
from jax.experimental.pallas import tpu as pltpu
from jax.sharding import PartitionSpec as P

CAPACITY = 12
SLOTS = CAPACITY + 1
COUNT_LANE = 14
CODES = 16
ENTRIES = 896
GROUP = 64
ROWS = 16
FLOOR = 0.15
HALO = 2

f32 = jnp.float32
bf16 = jnp.bfloat16
i32 = jnp.int32


def iota(shape, dim):
    return lax.broadcasted_iota(i32, shape, dim)


def ring(count, step):
    return [(i, (i + step) % count) for i in range(count)]


def pack_kernel(
    count_ref,
    owner_ref,
    row_ref,
    swath_ref,
    weight_ref,
    cols_ref,
    out_ref,
    done_ref,
    owner_v,
    row_v,
    swath_v,
    weight_v,
    cols_v,
    rows_f,
    codes_f,
    slot_v,
    slot_s,
    sem,
    load_sems,
):
    bands, blocks, _ = swath_ref.shape
    loads = [
        pltpu.make_async_copy(source, target, load_sems.at[i])
        for i, (source, target) in enumerate(
            (
                (owner_ref, owner_v),
                (row_ref, row_v),
                (weight_ref, weight_v),
                (cols_ref, cols_v),
                (swath_ref, swath_v),
            )
        )
    ]
    for load in loads:
        load.start()
    done_ref[...] = jnp.zeros((8, 128), f32)
    devices = out_ref.shape[0] // SLOTS
    live_count = count_ref[0]
    earlier = (iota((blocks, blocks), 0) < iota((blocks, blocks), 1)).astype(f32).astype(bf16)

    @pl.loop(0, devices // 2)
    def _(t):
        out_ref[pl.ds(t * 2 * SLOTS, 2 * SLOTS)] = jnp.zeros((2 * SLOTS, 8, 128), bf16)

    loads[0].wait()
    owner = owner_v[...]
    live = iota((1, blocks), 1) < live_count
    owner = jnp.where(live, owner, -1)
    named = (iota((devices, blocks), 0) == owner).astype(f32)
    named16 = named.astype(bf16)
    before = jnp.dot(named16, earlier, preferred_element_type=f32)
    rank = jnp.sum(named * before, axis=0, keepdims=True).astype(i32)
    slot_v[...] = jnp.where(live, owner * SLOTS + rank, CAPACITY)
    copy = pltpu.make_async_copy(slot_v, slot_s, sem)
    copy.start()
    entry = iota((128, blocks), 0)
    loads[1].wait()
    place = jnp.where(entry == rank, (row_v[...] + 1).astype(f32), 0.0)
    place = jnp.where(entry == COUNT_LANE, 1.0, place).astype(bf16)
    codes_f[...] = lax.dot_general(
        named16, place, (((1,), (1,)), ((), ())), preferred_element_type=f32
    )

    for load in loads[2:]:
        load.wait()

    @pl.loop(0, blocks // 16, unroll=4)
    def _(g):
        near = pl.ds(pl.multiple_of(g * 16, 16), 16)
        weight = weight_v[near, :].astype(f32)
        for c in range(bands):
            rows_f[pl.ds(g * 128 + c, 16, stride=8), :] = swath_v[c, near, :].astype(f32) * weight
        rows_f[pl.ds(g * 128 + bands, 16, stride=8), :] = weight
        rows_f[pl.ds(g * 128 + bands + 1, 16, stride=8), :] = cols_v[near, :].astype(f32)

    copy.wait()

    @pl.loop(0, (live_count + 15) // 16)
    def _(group):
        for i in range(16):
            b = group * 16 + i
            out_ref[slot_s[0, b]] = rows_f[pl.ds(pl.multiple_of(b * 8, 8), 8), :].astype(bf16)

    @pl.loop(0, devices, unroll=4)
    def _(t):
        code = codes_f[pl.ds(t, 1), :]
        out_ref[t * SLOTS + CAPACITY] = jnp.broadcast_to(code, (8, 128)).astype(bf16)


def pack(counts, owners, tile_row, swath, weight, columns, devices):
    blocks = weight.shape[0]
    vmem = pl.BlockSpec(memory_space=pltpu.VMEM)
    return pl.pallas_call(
        pack_kernel,
        out_shape=(
            jax.ShapeDtypeStruct((devices * SLOTS, 8, 128), bf16),
            jax.ShapeDtypeStruct((8, 128), f32),
        ),
        in_specs=[pl.BlockSpec(memory_space=pltpu.SMEM)]
        + [pl.BlockSpec(memory_space=pltpu.HBM)] * 5,
        out_specs=(vmem, vmem),
        scratch_shapes=[
            pltpu.VMEM((1, blocks), i32),
            pltpu.VMEM((1, blocks), i32),
            pltpu.VMEM(swath.shape, bf16),
            pltpu.VMEM(weight.shape, bf16),
            pltpu.VMEM(columns.shape, i32),
            pltpu.VMEM((blocks * 8, 128), f32),
            pltpu.VMEM((devices, 128), f32),
            pltpu.VMEM((1, blocks), i32),
            pltpu.SMEM((1, blocks), i32),
            pltpu.SemaphoreType.DMA,
            pltpu.SemaphoreType.DMA((5,)),
        ],
        compiler_params=pltpu.CompilerParams(vmem_limit_bytes=60 << 20),
        name="pack",
    )(counts, owners, tile_row, swath, weight, columns)


def bin_kernel(
    msg_ref,
    edge_top,
    edge_bottom,
    acc_ref,
    top_ref,
    bottom_ref,
    codes_v,
    lists_v,
    lists_s,
    sem,
):
    sources = msg_ref.shape[0] // SLOTS
    height = acc_ref.shape[0] - 1

    @pl.loop(0, sources // 8)
    def _(g):
        for i in range(8):
            s = g * 8 + i
            tile = msg_ref[s * SLOTS + CAPACITY].astype(f32)
            codes_v[pl.ds(s, 1), :] = tile[0:1, :]

    codes = codes_v[...].T[0:CODES, :]
    pairs = jnp.floor((codes[COUNT_LANE : COUNT_LANE + 1, :] + 1.0) * 0.5)
    earlier = (iota((sources, sources), 0) < iota((sources, sources), 1)).astype(f32).astype(bf16)
    before = jnp.dot(
        jnp.broadcast_to(pairs, (8, sources)).astype(bf16), earlier, preferred_element_type=f32
    )[0:1, :]
    total = (before + pairs)[:, sources - 1 : sources]
    entry = iota((ENTRIES, sources), 0).astype(f32)
    source = iota((1, sources), 1).astype(f32)
    facts, places = [], []
    for p in range(CAPACITY // 2):
        facts.append(
            jnp.concatenate(
                [
                    codes[2 * p : 2 * p + 2, :],
                    source,
                    jnp.full((1, sources), 2.0 * p, f32),
                    jnp.zeros((4, sources), f32),
                ],
                axis=0,
            ).astype(bf16)
        )
        place = jnp.where(pairs > p, before + p, -1.0)
        places.append(jnp.where(entry == place, 1.0, 0.0).astype(bf16))
    found = lax.dot_general(
        jnp.concatenate(facts, axis=1),
        jnp.concatenate(places, axis=1),
        (((1,), (1,)), ((), ())),
        preferred_element_type=f32,
    )
    rows = jnp.where(found[0:2] > 0.0, found[0:2] - 1.0, float(height))
    slots = found[2:3] * SLOTS + found[3:4]
    lists_v[0:1, :] = slots.astype(i32)
    lists_v[1:3, :] = rows.astype(i32)
    lists_v[3:4, :] = jnp.broadcast_to(total, (1, ENTRIES)).astype(i32)
    copy = pltpu.make_async_copy(lists_v, lists_s, sem)
    copy.start()

    @pl.loop(0, height // 16)
    def _(g):
        acc_ref[pl.ds(g * 16, 16)] = jnp.zeros((16, 32, 128), f32)

    acc_ref[height] = jnp.zeros((32, 128), f32)
    copy.wait()
    low_ids = iota((64, 128), 0).astype(f32)
    quarter_ids = (iota((32, 128), 0) // 8).astype(f32)
    empty = jnp.zeros((32, 128), bf16)

    @pl.loop(0, (lists_s[3, 0] + GROUP - 1) // GROUP)
    def _(group):
        for j in range(GROUP):
            slot = lists_s[0, group * GROUP + j]
            values, hits = [], []
            for i in range(2):
                block = msg_ref[slot + i].astype(f32)
                col = block[7:8, :]
                quarter = jnp.where(
                    col >= 128.0,
                    jnp.where(col >= 192.0, 3.0, 2.0),
                    jnp.where(col >= 64.0, 1.0, 0.0),
                )
                low = col - 64.0 * quarter
                block4 = jnp.concatenate([block] * 4, axis=0)
                values.append(jnp.where(quarter_ids == quarter, block4, 0.0).astype(bf16))
                hits.append(jnp.where(low_ids == low, 1.0, 0.0).astype(bf16))
            values = jnp.concatenate(
                [
                    jnp.concatenate([values[0], empty], axis=1),
                    jnp.concatenate([empty, values[1]], axis=1),
                ],
                axis=0,
            )
            sums = lax.dot_general(
                values,
                jnp.concatenate(hits, axis=1),
                (((1,), (1,)), ((), ())),
                preferred_element_type=f32,
            )
            row_0 = lists_s[1, group * GROUP + j]
            row_1 = lists_s[2, group * GROUP + j]
            shared = jnp.where(row_0 == row_1, sums[0:32], 0.0)
            sum_0 = acc_ref[row_0, :, 0:64] + sums[0:32]
            sum_1 = acc_ref[row_1, :, 0:64] + (sums[32:64] + shared)
            acc_ref[row_0, :, 0:64] = sum_0
            acc_ref[row_1, :, 0:64] = sum_1

    for ref, first, edge in ((top_ref, 0, edge_top), (bottom_ref, height - HALO, edge_bottom)):
        for i in range(HALO):
            for h, half in enumerate(join_quarters(acc_ref[first + i])):
                ref[i, :, 128 * h : 128 * h + 128] = half
        ref[HALO] = edge[...]


def join_quarters(tile):
    quarters = [tile[8 * q : 8 * q + 8] for q in range(4)]
    return [quarters[2 * h] + pltpu.roll(quarters[2 * h + 1], 64, 1) for h in range(2)]


def bin_blocks(message, edge_top, edge_bottom, height, width):
    sources = message.shape[0] // SLOTS
    vmem = pl.BlockSpec(memory_space=pltpu.VMEM)
    shape = lambda *dims: jax.ShapeDtypeStruct(dims, f32)
    return pl.pallas_call(
        bin_kernel,
        out_shape=(
            shape(height + 1, 32, 128),
            shape(HALO + 1, 8, width),
            shape(HALO + 1, 8, width),
        ),
        in_specs=[vmem] * 3,
        out_specs=(vmem,) * 3,
        scratch_shapes=[
            pltpu.VMEM((sources, 128), f32),
            pltpu.VMEM((8, ENTRIES), i32),
            pltpu.SMEM((8, ENTRIES), i32),
            pltpu.SemaphoreType.DMA,
        ],
        compiler_params=pltpu.CompilerParams(vmem_limit_bytes=16 << 20),
        name="bin",
    )(message, edge_top, edge_bottom)


def join_kernel(acc_ref, edge_left, edge_right, fields_ref, left_ref, right_ref):
    lane = iota((8, 128), 1)
    blank = jnp.zeros((8, 128), f32)

    def join_rows(j, carry):
        here = lane // 2 == j
        result = []
        for q in range(4):
            row = q * 64 + j
            first, last = join_quarters(acc_ref[row])
            fields_ref[row, :, 0:128] = first
            fields_ref[row, :, 128:256] = last
            result.append(jnp.where(here, pltpu.roll(first, 2 * j, 1), carry[2 * q]))
            result.append(jnp.where(here, pltpu.roll(last, 2 * j + 2, 1), carry[2 * q + 1]))
        return tuple(result)

    strips = lax.fori_loop(0, 64, join_rows, (blank,) * 8, unroll=8)
    for q in range(4):
        left_ref[q] = strips[2 * q]
        right_ref[q] = strips[2 * q + 1]
    left_ref[4] = edge_left[...]
    right_ref[4] = edge_right[...]


def join(acc, edge_left, edge_right, height, width):
    vmem = pl.BlockSpec(memory_space=pltpu.VMEM)
    shape = lambda *dims: jax.ShapeDtypeStruct(dims, f32)
    return pl.pallas_call(
        join_kernel,
        out_shape=(
            shape(height, 8, width),
            shape(height // 64 + 1, 8, 128),
            shape(height // 64 + 1, 8, 128),
        ),
        in_specs=[vmem] * 3,
        out_specs=(vmem,) * 3,
        compiler_params=pltpu.CompilerParams(vmem_limit_bytes=12 << 20),
        name="join",
    )(acc, edge_left, edge_right)


def relax(current, east_west, north_south, along_x, along_y):
    return current + along_x * (east_west - 2.0 * current) + along_y * (north_south - 2.0 * current)


def smooth_row(above, current, below, near, along_x, along_y):
    lane = iota((8, 128), 1)
    ahead = [pltpu.roll(half, 1, 1) for half in current]
    back = [pltpu.roll(half, 127, 1) for half in current]
    west = [jnp.where(lane == 0, near, ahead[0]), jnp.where(lane == 0, ahead[0], ahead[1])]
    east = [jnp.where(lane == 127, back[1], back[0]), jnp.where(lane == 127, near, back[1])]
    return [
        relax(current[h], east[h] + west[h], below[h] + above[h], along_x[h], along_y[h])
        for h in range(2)
    ]


def smooth_kernel(
    flags_ref,
    acc_ref,
    up_ref,
    down_ref,
    west_ref,
    east_ref,
    cx_ref,
    cy_ref,
    gridded_ref,
    coverage_ref,
    mix_near,
    mix_far,
    near,
    far,
    once,
    once_near,
    twice,
    side_x,
    side_y,
):
    height, _, width = acc_ref.shape
    has_up, has_down = flags_ref[0] > 0, flags_ref[1] > 0
    has_west, has_east = flags_ref[2] > 0, flags_ref[3] > 0
    lane = iota((8, 128), 1)

    def halves(ref, row):
        return [ref[row, :, 0:128], ref[row, :, 128:256]]

    def keep(flag, parts):
        return [jnp.where(flag, part, 0.0) for part in parts]

    def along(ref, row):
        line = ref[pl.ds(row, 1), :]
        return [line[:, i : i + 128] for i in (0, 128)]

    for q in range(4):
        west = jnp.where(has_west, west_ref[q], 0.0)
        east = jnp.where(has_east, east_ref[q], 0.0)
        even = lane % 2 == 0
        mix_near[q] = jnp.where(even, pltpu.roll(west, 127, 1), pltpu.roll(east, 127, 1))
        mix_far[q] = jnp.where(even, west, pltpu.roll(east, 126, 1))

    @pl.loop(0, 64, unroll=16)
    def _(j):
        for q in range(4):
            near[q * 64 + j + 1] = pltpu.roll(mix_near[q], 128 - 2 * j, 1)
            far[q * 64 + j] = pltpu.roll(mix_far[q], 128 - 2 * j, 1)

    for tile, row, flag in ((5, 0, has_up), (6, height + 1, has_down)):
        west = jnp.where(has_west & flag, west_ref[tile], 0.0)
        east = jnp.where(has_east & flag, east_ref[tile], 0.0)
        near[row] = jnp.where(lane < 64, pltpu.roll(west, 1, 1), pltpu.roll(east, 127, 1))

    upper = iota((128, 128), 0) < 64
    for i, side in enumerate((side_x, side_y)):
        for half in range(2):
            at = slice(2 * i + half, 2 * i + half + 1)
            west = jnp.where(has_west, west_ref[4, at, :], 0.0)
            east = jnp.where(has_east, east_ref[4, at, :], 0.0)
            both = jnp.where(
                upper, jnp.broadcast_to(west, (128, 128)), jnp.broadcast_to(east, (128, 128))
            )
            side[half * 128 : half * 128 + 128, :] = both.T

    up = [keep(has_up, halves(up_ref, i)) for i in range(2)]
    down = [keep(has_down, halves(down_ref, i)) for i in range(2)]

    def store(ref, row, parts):
        ref[row, :, 0:128] = parts[0]
        ref[row, :, 128:256] = parts[1]

    def coefficients(row):
        return along(cx_ref, row), along(cy_ref, row)

    def beyond(ref, flag):
        return [
            keep(flag, [ref[HALO, i : i + 1, h * 128 : h * 128 + 128] for h in range(2)])
            for i in range(2)
        ]

    store(
        once,
        0,
        smooth_row(up[0], up[1], halves(acc_ref, 0), near[0], *beyond(up_ref, has_up)),
    )
    store(
        once,
        height + 1,
        smooth_row(
            halves(acc_ref, height - 1),
            down[0],
            down[1],
            near[height + 1],
            *beyond(down_ref, has_down),
        ),
    )
    steps = height // ROWS

    @pl.loop(0, steps + 3)
    def _(g):
        block = jnp.clip(g - 3, 0, steps - 1)
        for part in range(ROWS // 8):
            base = block * ROWS + part * 8
            rows = pl.ds(pl.multiple_of(base, 8), 8)
            for half in range(width // 128):
                cols = pl.ds(half * 128, 128)
                coverage = twice[half, pl.ds(base * 8 + 6, 8, stride=8), :]
                coverage_ref[rows, cols] = coverage
                scale = 1.0 / jnp.maximum(coverage, FLOOR)
                for c in range(6):
                    gridded_ref[c, rows, cols] = (
                        twice[half, pl.ds(base * 8 + c, 8, stride=8), :] * scale
                    )
        start = jnp.clip(g - 2, 0, steps - 1) * ROWS
        lines = [halves(once, start + i) for i in range(ROWS + 2)]
        for i in range(ROWS):
            fresh = smooth_row(
                *lines[i : i + 3], once_near[start + i], *coefficients(start + i)
            )
            for half in range(2):
                twice[half, pl.ds(pl.multiple_of((start + i) * 8, 8), 8), :] = fresh[half]
        block = jnp.minimum(g, steps - 1)
        start = block * ROWS
        lines = [halves(acc_ref, start + i) for i in range(ROWS)]
        before = halves(acc_ref, jnp.maximum(start - 1, 0))
        after = halves(acc_ref, jnp.minimum(start + ROWS, height - 1))
        before = [jnp.where(block == 0, up[1][h], before[h]) for h in range(2)]
        after = [jnp.where(block == steps - 1, down[0][h], after[h]) for h in range(2)]
        lines = [before] + lines + [after]
        for i in range(ROWS):
            row = start + i + 1
            along_x, along_y = coefficients(start + i)
            store(once, row, smooth_row(*lines[i : i + 3], near[row], along_x, along_y))
            inner = jnp.where(lane < 64, lines[i + 1][0], lines[i + 1][1])
            once_near[start + i] = relax(
                near[row],
                inner + far[start + i],
                near[row + 1] + near[row - 1],
                side_x[pl.ds(start + i, 1), :],
                side_y[pl.ds(start + i, 1), :],
            )


def smooth(flags, acc, up, down, west, east, cx, cy):
    height, _, width = acc.shape
    vmem = pl.BlockSpec(memory_space=pltpu.VMEM)
    return pl.pallas_call(
        smooth_kernel,
        out_shape=(
            jax.ShapeDtypeStruct((6, height, width), f32),
            jax.ShapeDtypeStruct((height, width), f32),
        ),
        in_specs=[pl.BlockSpec(memory_space=pltpu.SMEM)] + [vmem] * 7,
        out_specs=(vmem, vmem),
        scratch_shapes=[
            pltpu.VMEM((4, 8, 128), f32),
            pltpu.VMEM((4, 8, 128), f32),
            pltpu.VMEM((height + 2, 8, 128), f32),
            pltpu.VMEM((height, 8, 128), f32),
            pltpu.VMEM((height + 2, 8, width), f32),
            pltpu.VMEM((height, 8, 128), f32),
            pltpu.VMEM((width // 128, height * 8, 128), f32),
            pltpu.VMEM((height, 128), f32),
            pltpu.VMEM((height, 128), f32),
        ],
        compiler_params=pltpu.CompilerParams(vmem_limit_bytes=24 << 20),
        name="smooth",
    )(flags, acc, up, down, west, east, cx, cy)


def edge_kernel(after_ref, flags_ref, cx_ref, cy_ref, top_ref, bottom_ref, left_ref, right_ref):
    height, width = cx_ref.shape
    for ref in (top_ref, bottom_ref, left_ref, right_ref):
        ref[...] = jnp.zeros_like(ref)
    for i, block in enumerate((cx_ref, cy_ref)):
        top_ref[i : i + 1, :] = block[0:1, :]
        bottom_ref[i : i + 1, :] = block[height - 1 : height, :]
        first = block[:, 0:128].T
        last = block[:, width - 128 : width].T
        for half in range(2):
            at = slice(2 * i + half, 2 * i + half + 1)
            left_ref[at, :] = first[0:1, half * 128 : half * 128 + 128]
            right_ref[at, :] = last[127:128, half * 128 : half * 128 + 128]


def coefficient_edges(after, flags, cx, cy):
    width = cx.shape[1]
    vmem = pl.BlockSpec(memory_space=pltpu.VMEM)
    row = jax.ShapeDtypeStruct((8, width), f32)
    column = jax.ShapeDtypeStruct((8, 128), f32)
    return pl.pallas_call(
        edge_kernel,
        out_shape=(row, row, column, column),
        in_specs=[vmem, pl.BlockSpec(memory_space=pltpu.SMEM), vmem, vmem],
        out_specs=(vmem,) * 4,
        compiler_params=pltpu.CompilerParams(vmem_limit_bytes=8 << 20),
        name="coefficient_edges",
    )(after, flags, cx, cy)


def body(swath_bands, clear_weight, owners, tile_row, columns, counts, conduct_x, conduct_y):
    blocks = swath_bands.shape[0]
    height, width = conduct_x.shape
    across, along = lax.axis_size("gx"), lax.axis_size("gy")
    devices = across * along
    gx, gy = lax.axis_index("gx"), lax.axis_index("gy")
    flags = jnp.stack([gy > 0, gy < along - 1, gx > 0, gx < across - 1]).astype(i32)
    message, packed = pack(
        counts,
        owners.reshape(1, blocks),
        tile_row.reshape(1, blocks),
        jnp.transpose(swath_bands, (1, 0, 2)),
        clear_weight,
        columns,
        devices,
    )
    arrived = lax.all_to_all(
        message.reshape(devices, SLOTS, 8, 128),
        ("gx", "gy"),
        split_axis=0,
        concat_axis=0,
        tiled=True,
    ).reshape(devices * SLOTS, 8, 128)

    edges = coefficient_edges(packed, flags, conduct_x, conduct_y)
    acc, top, bottom = bin_blocks(arrived, edges[0], edges[1], height, width)
    fields, left, right = join(acc, edges[2], edges[3], height, width)
    up = lax.ppermute(bottom, "gy", ring(along, 1))
    down = lax.ppermute(top, "gy", ring(along, -1))
    near = jnp.concatenate([left, up[1:2, :, 0:128], down[0:1, :, 0:128]], axis=0)
    far = jnp.concatenate([right, up[1:2, :, width - 128 :], down[0:1, :, width - 128 :]], axis=0)
    west = lax.ppermute(far, "gx", ring(across, 1))
    east = lax.ppermute(near, "gx", ring(across, -1))
    return smooth(flags, fields, up, down, west, east, conduct_x, conduct_y)


def solution(mesh):
    return jax.shard_map(
        body,
        mesh=mesh,
        in_specs=(
            P(("gx", "gy"), None, None),
            P(("gx", "gy"), None),
            P(("gx", "gy"), None),
            P(("gx", "gy")),
            P(("gx", "gy"), None),
            P(("gx", "gy")),
            P("gy", "gx"),
            P("gy", "gx"),
        ),
        out_specs=(P(None, "gy", "gx"), P("gy", "gx")),
        check_vma=False,
    )
```

```python
import functools

import jax
import jax.numpy as jnp
from jax import lax
from jax.experimental import pallas as pl
from jax.experimental.pallas import tpu as pltpu
from jax.sharding import PartitionSpec as P

CAPACITY = 12
SLOTS = CAPACITY + 1
COUNT_LANE = 14
CODES = 16
ENTRIES = 896
GROUP = 64
ROWS = 16
FLOOR = 0.15
HALO = 2

f32 = jnp.float32
bf16 = jnp.bfloat16
i32 = jnp.int32


def iota(shape, dim):
    return lax.broadcasted_iota(i32, shape, dim)


def ring(count, step):
    return [(i, (i + step) % count) for i in range(count)]


def pack_kernel(
    count_ref,
    owner_ref,
    row_ref,
    swath_ref,
    weight_ref,
    cols_ref,
    out_ref,
    done_ref,
    owner_v,
    row_v,
    swath_v,
    weight_v,
    cols_v,
    rows_f,
    codes_f,
    slot_v,
    slot_s,
    sem,
    load_sems,
):
    bands, blocks, _ = swath_ref.shape
    loads = [
        pltpu.make_async_copy(source, target, load_sems.at[i])
        for i, (source, target) in enumerate(
            (
                (owner_ref, owner_v),
                (row_ref, row_v),
                (weight_ref, weight_v),
                (cols_ref, cols_v),
                (swath_ref, swath_v),
            )
        )
    ]
    for load in loads:
        load.start()
    done_ref[...] = jnp.zeros((8, 128), f32)
    devices = out_ref.shape[0] // SLOTS
    live_count = count_ref[0]
    chunk = iota((128, 256), 1)
    earlier = ((iota((128, 256), 0) < chunk) | (chunk >= 128)).astype(f32).astype(bf16)

    @pl.loop(0, devices // 2)
    def _(t):
        out_ref[pl.ds(t * 2 * SLOTS, 2 * SLOTS)] = jnp.zeros((2 * SLOTS, 8, 128), bf16)

    loads[0].wait()
    owner = owner_v[...]
    live = iota((1, blocks), 1) < live_count
    owner = jnp.where(live, owner, -1)
    named = (iota((devices, blocks), 0) == owner).astype(f32)
    named16 = named.astype(bf16)
    before, seen = [], jnp.zeros((devices, 128), f32)
    for first in range(0, blocks, 128):
        found = jnp.dot(
            named16[:, first : first + 128], earlier, preferred_element_type=f32
        )
        before.append(seen + found[:, 0:128])
        seen = seen + found[:, 128:256]
    before = jnp.concatenate(before, axis=1)
    rank = jnp.sum(named * before, axis=0, keepdims=True).astype(i32)
    slot_v[...] = jnp.where(live, owner * SLOTS + rank, CAPACITY)
    copy = pltpu.make_async_copy(slot_v, slot_s, sem)
    copy.start()
    entry = iota((128, blocks), 0)
    loads[1].wait()
    place = jnp.where(entry == rank, (row_v[...] + 1).astype(f32), 0.0)
    place = jnp.where(entry == COUNT_LANE, 1.0, place).astype(bf16)
    codes_f[...] = lax.dot_general(
        named16, place, (((1,), (1,)), ((), ())), preferred_element_type=f32
    )

    for load in loads[2:]:
        load.wait()

    @pl.loop(0, blocks // 16, unroll=4)
    def _(g):
        near = pl.ds(pl.multiple_of(g * 16, 16), 16)
        weight = weight_v[near, :].astype(f32)
        for c in range(bands):
            rows_f[pl.ds(g * 128 + c, 16, stride=8), :] = swath_v[c, near, :].astype(f32) * weight
        rows_f[pl.ds(g * 128 + bands, 16, stride=8), :] = weight
        rows_f[pl.ds(g * 128 + bands + 1, 16, stride=8), :] = cols_v[near, :].astype(f32)

    copy.wait()

    @pl.loop(0, (live_count + 15) // 16)
    def _(group):
        for i in range(16):
            b = group * 16 + i
            out_ref[slot_s[0, b]] = rows_f[pl.ds(pl.multiple_of(b * 8, 8), 8), :].astype(bf16)

    @pl.loop(0, devices, unroll=4)
    def _(t):
        code = codes_f[pl.ds(t, 1), :]
        out_ref[t * SLOTS + CAPACITY] = jnp.broadcast_to(code, (8, 128)).astype(bf16)


def pack(counts, owners, tile_row, swath, weight, columns, devices):
    blocks = weight.shape[0]
    vmem = pl.BlockSpec(memory_space=pltpu.VMEM)
    return pl.pallas_call(
        pack_kernel,
        out_shape=(
            jax.ShapeDtypeStruct((devices * SLOTS, 8, 128), bf16),
            jax.ShapeDtypeStruct((8, 128), f32),
        ),
        in_specs=[pl.BlockSpec(memory_space=pltpu.SMEM)]
        + [pl.BlockSpec(memory_space=pltpu.HBM)] * 5,
        out_specs=(vmem, vmem),
        scratch_shapes=[
            pltpu.VMEM((1, blocks), i32),
            pltpu.VMEM((1, blocks), i32),
            pltpu.VMEM(swath.shape, bf16),
            pltpu.VMEM(weight.shape, bf16),
            pltpu.VMEM(columns.shape, i32),
            pltpu.VMEM((blocks * 8, 128), f32),
            pltpu.VMEM((devices, 128), f32),
            pltpu.VMEM((1, blocks), i32),
            pltpu.SMEM((1, blocks), i32),
            pltpu.SemaphoreType.DMA,
            pltpu.SemaphoreType.DMA((5,)),
        ],
        compiler_params=pltpu.CompilerParams(vmem_limit_bytes=60 << 20),
        name="pack",
    )(counts, owners, tile_row, swath, weight, columns)


def bin_kernel(
    msg_ref,
    edge_top,
    edge_bottom,
    acc_ref,
    top_ref,
    bottom_ref,
    codes_v,
    lists_v,
    lists_s,
    sem,
):
    sources = msg_ref.shape[0] // SLOTS
    height = acc_ref.shape[0] - 1

    @pl.loop(0, sources // 8)
    def _(g):
        for i in range(8):
            s = g * 8 + i
            tile = msg_ref[s * SLOTS + CAPACITY].astype(f32)
            codes_v[pl.ds(s, 1), :] = tile[0:1, :]

    codes = codes_v[...].T[0:CODES, :]
    pairs = jnp.floor((codes[COUNT_LANE : COUNT_LANE + 1, :] + 1.0) * 0.5)
    earlier = (iota((sources, sources), 0) < iota((sources, sources), 1)).astype(f32).astype(bf16)
    before = jnp.dot(
        jnp.broadcast_to(pairs, (8, sources)).astype(bf16), earlier, preferred_element_type=f32
    )[0:1, :]
    total = (before + pairs)[:, sources - 1 : sources]
    entry = iota((ENTRIES, sources), 0).astype(f32)
    source = iota((1, sources), 1).astype(f32)
    facts, places = [], []
    for p in range(CAPACITY // 2):
        facts.append(
            jnp.concatenate(
                [
                    codes[2 * p : 2 * p + 2, :],
                    source,
                    jnp.full((1, sources), 2.0 * p, f32),
                    jnp.zeros((4, sources), f32),
                ],
                axis=0,
            ).astype(bf16)
        )
        place = jnp.where(pairs > p, before + p, -1.0)
        places.append(jnp.where(entry == place, 1.0, 0.0).astype(bf16))
    found = lax.dot_general(
        jnp.concatenate(facts, axis=1),
        jnp.concatenate(places, axis=1),
        (((1,), (1,)), ((), ())),
        preferred_element_type=f32,
    )
    rows = jnp.where(found[0:2] > 0.0, found[0:2] - 1.0, float(height))
    slots = found[2:3] * SLOTS + found[3:4]
    lists_v[0:1, :] = slots.astype(i32)
    lists_v[1:3, :] = rows.astype(i32)
    lists_v[3:4, :] = jnp.broadcast_to(total, (1, ENTRIES)).astype(i32)
    copy = pltpu.make_async_copy(lists_v, lists_s, sem)
    copy.start()

    @pl.loop(0, height // 16)
    def _(g):
        acc_ref[pl.ds(g * 16, 16)] = jnp.zeros((16, 32, 128), f32)

    acc_ref[height] = jnp.zeros((32, 128), f32)
    copy.wait()
    ids = iota((16, 128), 0).astype(f32)
    low_ids = [(ids + 16.0 * k).astype(bf16) for k in range(4)]
    quarter_ids = [(2.0 * k + jnp.floor(ids * 0.125)).astype(bf16) for k in range(2)]
    one = jnp.ones((16, 128), bf16)
    zero = jnp.zeros((16, 128), bf16)
    empty = jnp.zeros((32, 128), bf16)

    @pl.loop(0, (lists_s[3, 0] + GROUP - 1) // GROUP)
    def _(group):
        for j in range(GROUP):
            slot = lists_s[0, group * GROUP + j]
            values, hits = [], []
            for i in range(2):
                block = msg_ref[slot + i].astype(f32)
                col = jnp.broadcast_to(block[7:8, :], (8, 128))
                quarter = jnp.floor(col * (1.0 / 64.0))
                low = col - 64.0 * quarter
                block, quarter, low = (
                    jnp.concatenate([x, x], axis=0).astype(bf16) for x in (block, quarter, low)
                )
                values.append(
                    jnp.concatenate([jnp.where(q == quarter, block, zero) for q in quarter_ids], axis=0)
                )
                hits.append(
                    jnp.concatenate([jnp.where(k == low, one, zero) for k in low_ids], axis=0)
                )
            values = jnp.concatenate(
                [
                    jnp.concatenate([values[0], empty], axis=1),
                    jnp.concatenate([empty, values[1]], axis=1),
                ],
                axis=0,
            )
            sums = lax.dot_general(
                values,
                jnp.concatenate(hits, axis=1),
                (((1,), (1,)), ((), ())),
                preferred_element_type=f32,
            )
            row_0 = lists_s[1, group * GROUP + j]
            row_1 = lists_s[2, group * GROUP + j]
            shared = jnp.where(row_0 == row_1, sums[0:32], 0.0)
            sum_0 = acc_ref[row_0, :, 0:64] + sums[0:32]
            sum_1 = acc_ref[row_1, :, 0:64] + (sums[32:64] + shared)
            acc_ref[row_0, :, 0:64] = sum_0
            acc_ref[row_1, :, 0:64] = sum_1

    for ref, first, edge in ((top_ref, 0, edge_top), (bottom_ref, height - HALO, edge_bottom)):
        for i in range(HALO):
            for h, half in enumerate(join_quarters(acc_ref[first + i])):
                ref[i, :, 128 * h : 128 * h + 128] = half
        ref[HALO] = edge[...]


def join_quarters(tile):
    quarters = [tile[8 * q : 8 * q + 8] for q in range(4)]
    return [quarters[2 * h] + pltpu.roll(quarters[2 * h + 1], 64, 1) for h in range(2)]


def bin_blocks(message, edge_top, edge_bottom, height, width):
    sources = message.shape[0] // SLOTS
    vmem = pl.BlockSpec(memory_space=pltpu.VMEM)
    shape = lambda *dims: jax.ShapeDtypeStruct(dims, f32)
    return pl.pallas_call(
        bin_kernel,
        out_shape=(
            shape(height + 1, 32, 128),
            shape(HALO + 1, 8, width),
            shape(HALO + 1, 8, width),
        ),
        in_specs=[vmem] * 3,
        out_specs=(vmem,) * 3,
        scratch_shapes=[
            pltpu.VMEM((sources, 128), f32),
            pltpu.VMEM((8, ENTRIES), i32),
            pltpu.SMEM((8, ENTRIES), i32),
            pltpu.SemaphoreType.DMA,
        ],
        compiler_params=pltpu.CompilerParams(vmem_limit_bytes=16 << 20),
        name="bin",
    )(message, edge_top, edge_bottom)


def join_kernel(acc_ref, edge_left, edge_right, fields_ref, left_ref, right_ref):
    lane = iota((8, 128), 1)
    blank = jnp.zeros((8, 128), f32)

    def join_rows(j, carry):
        here = lane // 2 == j
        result = []
        for q in range(4):
            row = q * 64 + j
            first, last = join_quarters(acc_ref[row])
            fields_ref[row, :, 0:128] = first
            fields_ref[row, :, 128:256] = last
            result.append(jnp.where(here, pltpu.roll(first, 2 * j, 1), carry[2 * q]))
            result.append(jnp.where(here, pltpu.roll(last, 2 * j + 2, 1), carry[2 * q + 1]))
        return tuple(result)

    strips = lax.fori_loop(0, 64, join_rows, (blank,) * 8, unroll=8)
    for q in range(4):
        left_ref[q] = strips[2 * q]
        right_ref[q] = strips[2 * q + 1]
    left_ref[4] = edge_left[...]
    right_ref[4] = edge_right[...]


def join(acc, edge_left, edge_right, height, width):
    vmem = pl.BlockSpec(memory_space=pltpu.VMEM)
    shape = lambda *dims: jax.ShapeDtypeStruct(dims, f32)
    return pl.pallas_call(
        join_kernel,
        out_shape=(
            shape(height, 8, width),
            shape(height // 64 + 1, 8, 128),
            shape(height // 64 + 1, 8, 128),
        ),
        in_specs=[vmem] * 3,
        out_specs=(vmem,) * 3,
        compiler_params=pltpu.CompilerParams(vmem_limit_bytes=12 << 20),
        name="join",
    )(acc, edge_left, edge_right)


def relax(current, east_west, north_south, along_x, along_y):
    return current + along_x * (east_west - 2.0 * current) + along_y * (north_south - 2.0 * current)


def smooth_row(above, current, below, near, along_x, along_y):
    lane = iota((8, 128), 1)
    ahead = [pltpu.roll(half, 1, 1) for half in current]
    back = [pltpu.roll(half, 127, 1) for half in current]
    west = [jnp.where(lane == 0, near, ahead[0]), jnp.where(lane == 0, ahead[0], ahead[1])]
    east = [jnp.where(lane == 127, back[1], back[0]), jnp.where(lane == 127, near, back[1])]
    return [
        relax(current[h], east[h] + west[h], below[h] + above[h], along_x[h], along_y[h])
        for h in range(2)
    ]


def smooth_kernel(
    flags_ref,
    acc_ref,
    up_ref,
    down_ref,
    west_ref,
    east_ref,
    cx_ref,
    cy_ref,
    gridded_ref,
    coverage_ref,
    mix_near,
    mix_far,
    near,
    far,
    once,
    once_near,
    twice,
    side_x,
    side_y,
):
    height, _, width = acc_ref.shape
    has_up, has_down = flags_ref[0] > 0, flags_ref[1] > 0
    has_west, has_east = flags_ref[2] > 0, flags_ref[3] > 0
    lane = iota((8, 128), 1)

    def halves(ref, row):
        return [ref[row, :, 0:128], ref[row, :, 128:256]]

    def keep(flag, parts):
        return [jnp.where(flag, part, 0.0) for part in parts]

    def along(ref, row):
        line = ref[pl.ds(row, 1), :]
        return [line[:, i : i + 128] for i in (0, 128)]

    for q in range(4):
        west = jnp.where(has_west, west_ref[q], 0.0)
        east = jnp.where(has_east, east_ref[q], 0.0)
        even = lane % 2 == 0
        mix_near[q] = jnp.where(even, pltpu.roll(west, 127, 1), pltpu.roll(east, 127, 1))
        mix_far[q] = jnp.where(even, west, pltpu.roll(east, 126, 1))

    @pl.loop(0, 64, unroll=16)
    def _(j):
        for q in range(4):
            near[q * 64 + j + 1] = pltpu.roll(mix_near[q], 128 - 2 * j, 1)
            far[q * 64 + j] = pltpu.roll(mix_far[q], 128 - 2 * j, 1)

    for tile, row, flag in ((5, 0, has_up), (6, height + 1, has_down)):
        west = jnp.where(has_west & flag, west_ref[tile], 0.0)
        east = jnp.where(has_east & flag, east_ref[tile], 0.0)
        near[row] = jnp.where(lane < 64, pltpu.roll(west, 1, 1), pltpu.roll(east, 127, 1))

    upper = iota((128, 128), 0) < 64
    for i, side in enumerate((side_x, side_y)):
        for half in range(2):
            at = slice(2 * i + half, 2 * i + half + 1)
            west = jnp.where(has_west, west_ref[4, at, :], 0.0)
            east = jnp.where(has_east, east_ref[4, at, :], 0.0)
            both = jnp.where(
                upper, jnp.broadcast_to(west, (128, 128)), jnp.broadcast_to(east, (128, 128))
            )
            side[half * 128 : half * 128 + 128, :] = both.T

    up = [keep(has_up, halves(up_ref, i)) for i in range(2)]
    down = [keep(has_down, halves(down_ref, i)) for i in range(2)]

    def store(ref, row, parts):
        ref[row, :, 0:128] = parts[0]
        ref[row, :, 128:256] = parts[1]

    def coefficients(row):
        return along(cx_ref, row), along(cy_ref, row)

    def beyond(ref, flag):
        return [
            keep(flag, [ref[HALO, i : i + 1, h * 128 : h * 128 + 128] for h in range(2)])
            for i in range(2)
        ]

    store(
        once,
        0,
        smooth_row(up[0], up[1], halves(acc_ref, 0), near[0], *beyond(up_ref, has_up)),
    )
    store(
        once,
        height + 1,
        smooth_row(
            halves(acc_ref, height - 1),
            down[0],
            down[1],
            near[height + 1],
            *beyond(down_ref, has_down),
        ),
    )
    steps = height // ROWS

    @pl.loop(0, steps + 3)
    def _(g):
        block = jnp.clip(g - 3, 0, steps - 1)
        for part in range(ROWS // 8):
            base = block * ROWS + part * 8
            rows = pl.ds(pl.multiple_of(base, 8), 8)
            for half in range(width // 128):
                cols = pl.ds(half * 128, 128)
                coverage = twice[half, pl.ds(base * 8 + 6, 8, stride=8), :]
                coverage_ref[rows, cols] = coverage
                scale = 1.0 / jnp.maximum(coverage, FLOOR)
                for c in range(6):
                    gridded_ref[c, rows, cols] = (
                        twice[half, pl.ds(base * 8 + c, 8, stride=8), :] * scale
                    )
        start = jnp.clip(g - 2, 0, steps - 1) * ROWS
        lines = [halves(once, start + i) for i in range(ROWS + 2)]
        for i in range(ROWS):
            fresh = smooth_row(
                *lines[i : i + 3], once_near[start + i], *coefficients(start + i)
            )
            for half in range(2):
                twice[half, pl.ds(pl.multiple_of((start + i) * 8, 8), 8), :] = fresh[half]
        block = jnp.minimum(g, steps - 1)
        start = block * ROWS
        lines = [halves(acc_ref, start + i) for i in range(ROWS)]
        before = halves(acc_ref, jnp.maximum(start - 1, 0))
        after = halves(acc_ref, jnp.minimum(start + ROWS, height - 1))
        before = [jnp.where(block == 0, up[1][h], before[h]) for h in range(2)]
        after = [jnp.where(block == steps - 1, down[0][h], after[h]) for h in range(2)]
        lines = [before] + lines + [after]
        sides = [near[start + i] for i in range(ROWS + 2)]
        for i in range(ROWS):
            row = start + i + 1
            along_x, along_y = coefficients(start + i)
            store(once, row, smooth_row(*lines[i : i + 3], sides[i + 1], along_x, along_y))
            inner = jnp.where(lane < 64, lines[i + 1][0], lines[i + 1][1])
            once_near[start + i] = relax(
                sides[i + 1],
                inner + far[start + i],
                sides[i + 2] + sides[i],
                side_x[pl.ds(start + i, 1), :],
                side_y[pl.ds(start + i, 1), :],
            )


def smooth(flags, acc, up, down, west, east, cx, cy):
    height, _, width = acc.shape
    vmem = pl.BlockSpec(memory_space=pltpu.VMEM)
    return pl.pallas_call(
        smooth_kernel,
        out_shape=(
            jax.ShapeDtypeStruct((6, height, width), f32),
            jax.ShapeDtypeStruct((height, width), f32),
        ),
        in_specs=[pl.BlockSpec(memory_space=pltpu.SMEM)] + [vmem] * 7,
        out_specs=(vmem, vmem),
        scratch_shapes=[
            pltpu.VMEM((4, 8, 128), f32),
            pltpu.VMEM((4, 8, 128), f32),
            pltpu.VMEM((height + 2, 8, 128), f32),
            pltpu.VMEM((height, 8, 128), f32),
            pltpu.VMEM((height + 2, 8, width), f32),
            pltpu.VMEM((height, 8, 128), f32),
            pltpu.VMEM((width // 128, height * 8, 128), f32),
            pltpu.VMEM((height, 128), f32),
            pltpu.VMEM((height, 128), f32),
        ],
        compiler_params=pltpu.CompilerParams(vmem_limit_bytes=24 << 20),
        name="smooth",
    )(flags, acc, up, down, west, east, cx, cy)


def edge_kernel(after_ref, flags_ref, cx_ref, cy_ref, top_ref, bottom_ref, left_ref, right_ref):
    height, width = cx_ref.shape
    for ref in (top_ref, bottom_ref, left_ref, right_ref):
        ref[...] = jnp.zeros_like(ref)
    for i, block in enumerate((cx_ref, cy_ref)):
        top_ref[i : i + 1, :] = block[0:1, :]
        bottom_ref[i : i + 1, :] = block[height - 1 : height, :]
        first = block[:, 0:128].T
        last = block[:, width - 128 : width].T
        for half in range(2):
            at = slice(2 * i + half, 2 * i + half + 1)
            left_ref[at, :] = first[0:1, half * 128 : half * 128 + 128]
            right_ref[at, :] = last[127:128, half * 128 : half * 128 + 128]


def coefficient_edges(after, flags, cx, cy):
    width = cx.shape[1]
    vmem = pl.BlockSpec(memory_space=pltpu.VMEM)
    row = jax.ShapeDtypeStruct((8, width), f32)
    column = jax.ShapeDtypeStruct((8, 128), f32)
    return pl.pallas_call(
        edge_kernel,
        out_shape=(row, row, column, column),
        in_specs=[vmem, pl.BlockSpec(memory_space=pltpu.SMEM), vmem, vmem],
        out_specs=(vmem,) * 4,
        compiler_params=pltpu.CompilerParams(vmem_limit_bytes=8 << 20),
        name="coefficient_edges",
    )(after, flags, cx, cy)


def body(swath_bands, clear_weight, owners, tile_row, columns, counts, conduct_x, conduct_y):
    blocks = swath_bands.shape[0]
    height, width = conduct_x.shape
    across, along = lax.axis_size("gx"), lax.axis_size("gy")
    devices = across * along
    gx, gy = lax.axis_index("gx"), lax.axis_index("gy")
    flags = jnp.stack([gy > 0, gy < along - 1, gx > 0, gx < across - 1]).astype(i32)
    message, packed = pack(
        counts,
        owners.reshape(1, blocks),
        tile_row.reshape(1, blocks),
        jnp.transpose(swath_bands, (1, 0, 2)),
        clear_weight,
        columns,
        devices,
    )
    arrived = lax.all_to_all(
        message.reshape(devices, SLOTS, 8, 128),
        ("gx", "gy"),
        split_axis=0,
        concat_axis=0,
        tiled=True,
    ).reshape(devices * SLOTS, 8, 128)

    edges = coefficient_edges(packed, flags, conduct_x, conduct_y)
    acc, top, bottom = bin_blocks(arrived, edges[0], edges[1], height, width)
    fields, left, right = join(acc, edges[2], edges[3], height, width)
    up = lax.ppermute(bottom, "gy", ring(along, 1))
    down = lax.ppermute(top, "gy", ring(along, -1))
    near = jnp.concatenate([left, up[1:2, :, 0:128], down[0:1, :, 0:128]], axis=0)
    far = jnp.concatenate([right, up[1:2, :, width - 128 :], down[0:1, :, width - 128 :]], axis=0)
    west = lax.ppermute(far, "gx", ring(across, 1))
    east = lax.ppermute(near, "gx", ring(across, -1))
    return smooth(flags, fields, up, down, west, east, conduct_x, conduct_y)


def solution(mesh):
    return jax.shard_map(
        body,
        mesh=mesh,
        in_specs=(
            P(("gx", "gy"), None, None),
            P(("gx", "gy"), None),
            P(("gx", "gy"), None),
            P(("gx", "gy")),
            P(("gx", "gy"), None),
            P(("gx", "gy")),
            P("gy", "gx"),
            P("gy", "gx"),
        ),
        out_specs=(P(None, "gy", "gx"), P("gy", "gx")),
        check_vma=False,
    )
```

```python
import functools

import jax
import jax.numpy as jnp
from jax import lax
from jax.experimental import pallas as pl
from jax.experimental.pallas import tpu as pltpu
from jax.sharding import PartitionSpec as P

CAPACITY = 12
SLOTS = CAPACITY + 1
COUNT_LANE = 14
CODES = 16
ENTRIES = 896
GROUP = 64
ROWS = 16
FLOOR = 0.15
HALO = 2

f32 = jnp.float32
bf16 = jnp.bfloat16
i32 = jnp.int32


def iota(shape, dim):
    return lax.broadcasted_iota(i32, shape, dim)


def ring(count, step):
    return [(i, (i + step) % count) for i in range(count)]


def pack_kernel(
    count_ref,
    owner_ref,
    row_ref,
    swath_ref,
    weight_ref,
    cols_ref,
    out_ref,
    done_ref,
    owner_v,
    row_v,
    swath_v,
    weight_v,
    cols_v,
    rows_f,
    codes_f,
    slot_v,
    slot_s,
    sem,
    load_sems,
):
    bands, blocks, _ = swath_ref.shape
    loads = [
        pltpu.make_async_copy(source, target, load_sems.at[i])
        for i, (source, target) in enumerate(
            (
                (owner_ref, owner_v),
                (row_ref, row_v),
                (weight_ref, weight_v),
                (cols_ref, cols_v),
                (swath_ref, swath_v),
            )
        )
    ]
    for load in loads:
        load.start()
    done_ref[...] = jnp.zeros((8, 128), f32)
    devices = out_ref.shape[0] // SLOTS
    live_count = count_ref[0]
    chunk = iota((128, 256), 1)
    earlier = ((iota((128, 256), 0) < chunk) | (chunk >= 128)).astype(f32).astype(bf16)

    @pl.loop(0, devices // 2)
    def _(t):
        out_ref[pl.ds(t * 2 * SLOTS, 2 * SLOTS)] = jnp.zeros((2 * SLOTS, 8, 128), bf16)

    loads[0].wait()
    owner = owner_v[...]
    live = iota((1, blocks), 1) < live_count
    owner = jnp.where(live, owner, -1)
    named = (iota((devices, blocks), 0) == owner).astype(f32)
    named16 = named.astype(bf16)
    before, seen = [], jnp.zeros((devices, 128), f32)
    for first in range(0, blocks, 128):
        found = jnp.dot(
            named16[:, first : first + 128], earlier, preferred_element_type=f32
        )
        before.append(seen + found[:, 0:128])
        seen = seen + found[:, 128:256]
    before = jnp.concatenate(before, axis=1)
    rank = jnp.sum(named * before, axis=0, keepdims=True).astype(i32)
    slot_v[...] = jnp.where(live, owner * SLOTS + rank, CAPACITY)
    copy = pltpu.make_async_copy(slot_v, slot_s, sem)
    copy.start()
    entry = iota((128, blocks), 0)
    loads[1].wait()
    place = jnp.where(entry == rank, (row_v[...] + 1).astype(f32), 0.0)
    place = jnp.where(entry == COUNT_LANE, 1.0, place).astype(bf16)
    codes_f[...] = lax.dot_general(
        named16, place, (((1,), (1,)), ((), ())), preferred_element_type=f32
    )

    for load in loads[2:]:
        load.wait()

    @pl.loop(0, blocks // 16, unroll=4)
    def _(g):
        near = pl.ds(pl.multiple_of(g * 16, 16), 16)
        weight = weight_v[near, :].astype(f32)
        for c in range(bands):
            rows_f[pl.ds(g * 128 + c, 16, stride=8), :] = swath_v[c, near, :].astype(f32) * weight
        rows_f[pl.ds(g * 128 + bands, 16, stride=8), :] = weight
        rows_f[pl.ds(g * 128 + bands + 1, 16, stride=8), :] = cols_v[near, :].astype(f32)

    copy.wait()

    @pl.loop(0, (live_count + 15) // 16)
    def _(group):
        for i in range(16):
            b = group * 16 + i
            out_ref[slot_s[0, b]] = rows_f[pl.ds(pl.multiple_of(b * 8, 8), 8), :].astype(bf16)

    @pl.loop(0, devices, unroll=4)
    def _(t):
        code = codes_f[pl.ds(t, 1), :]
        out_ref[t * SLOTS + CAPACITY] = jnp.broadcast_to(code, (8, 128)).astype(bf16)


def pack(counts, owners, tile_row, swath, weight, columns, devices):
    blocks = weight.shape[0]
    vmem = pl.BlockSpec(memory_space=pltpu.VMEM)
    return pl.pallas_call(
        pack_kernel,
        out_shape=(
            jax.ShapeDtypeStruct((devices * SLOTS, 8, 128), bf16),
            jax.ShapeDtypeStruct((8, 128), f32),
        ),
        in_specs=[pl.BlockSpec(memory_space=pltpu.SMEM)]
        + [pl.BlockSpec(memory_space=pltpu.HBM)] * 5,
        out_specs=(vmem, vmem),
        scratch_shapes=[
            pltpu.VMEM((1, blocks), i32),
            pltpu.VMEM((1, blocks), i32),
            pltpu.VMEM(swath.shape, bf16),
            pltpu.VMEM(weight.shape, bf16),
            pltpu.VMEM(columns.shape, i32),
            pltpu.VMEM((blocks * 8, 128), f32),
            pltpu.VMEM((devices, 128), f32),
            pltpu.VMEM((1, blocks), i32),
            pltpu.SMEM((1, blocks), i32),
            pltpu.SemaphoreType.DMA,
            pltpu.SemaphoreType.DMA((5,)),
        ],
        compiler_params=pltpu.CompilerParams(vmem_limit_bytes=60 << 20),
        name="pack",
    )(counts, owners, tile_row, swath, weight, columns)


def bin_kernel(
    msg_ref,
    edge_top,
    edge_bottom,
    acc_ref,
    top_ref,
    bottom_ref,
    codes_v,
    lists_v,
    lists_s,
    sem,
):
    sources = msg_ref.shape[0] // SLOTS
    height = acc_ref.shape[0] - 1

    @pl.loop(0, sources // 8)
    def _(g):
        for i in range(8):
            s = g * 8 + i
            tile = msg_ref[s * SLOTS + CAPACITY].astype(f32)
            codes_v[pl.ds(s, 1), :] = tile[0:1, :]

    codes = codes_v[...].T[0:CODES, :]
    pairs = jnp.floor((codes[COUNT_LANE : COUNT_LANE + 1, :] + 1.0) * 0.5)
    earlier = (iota((sources, sources), 0) < iota((sources, sources), 1)).astype(f32).astype(bf16)
    before = jnp.dot(
        jnp.broadcast_to(pairs, (8, sources)).astype(bf16), earlier, preferred_element_type=f32
    )[0:1, :]
    total = (before + pairs)[:, sources - 1 : sources]
    entry = iota((ENTRIES, sources), 0).astype(f32)
    source = iota((1, sources), 1).astype(f32)
    facts, places = [], []
    for p in range(CAPACITY // 2):
        facts.append(
            jnp.concatenate(
                [
                    codes[2 * p : 2 * p + 2, :],
                    source,
                    jnp.full((1, sources), 2.0 * p, f32),
                    jnp.zeros((4, sources), f32),
                ],
                axis=0,
            ).astype(bf16)
        )
        place = jnp.where(pairs > p, before + p, -1.0)
        places.append(jnp.where(entry == place, 1.0, 0.0).astype(bf16))
    found = lax.dot_general(
        jnp.concatenate(facts, axis=1),
        jnp.concatenate(places, axis=1),
        (((1,), (1,)), ((), ())),
        preferred_element_type=f32,
    )
    rows = jnp.where(found[0:2] > 0.0, found[0:2] - 1.0, float(height))
    slots = found[2:3] * SLOTS + found[3:4]
    lists_v[0:1, :] = slots.astype(i32)
    lists_v[1:3, :] = rows.astype(i32)
    lists_v[3:4, :] = jnp.broadcast_to(total, (1, ENTRIES)).astype(i32)
    copy = pltpu.make_async_copy(lists_v, lists_s, sem)
    copy.start()

    @pl.loop(0, height // 16)
    def _(g):
        acc_ref[pl.ds(g * 16, 16)] = jnp.zeros((16, 32, 128), f32)

    acc_ref[height] = jnp.zeros((32, 128), f32)
    copy.wait()
    ids = iota((16, 128), 0).astype(f32)
    low_ids = [(ids + 16.0 * k).astype(bf16) for k in range(4)]
    quarter_ids = [(2.0 * k + jnp.floor(ids * 0.125)).astype(bf16) for k in range(2)]
    one = jnp.ones((16, 128), bf16)
    zero = jnp.zeros((16, 128), bf16)
    empty = jnp.zeros((32, 128), bf16)

    @pl.loop(0, (lists_s[3, 0] + GROUP - 1) // GROUP)
    def _(group):
        for j in range(GROUP):
            slot = lists_s[0, group * GROUP + j]
            values, hits = [], []
            for i in range(2):
                block = msg_ref[slot + i].astype(f32)
                col = jnp.broadcast_to(block[7:8, :], (8, 128))
                quarter = jnp.floor(col * (1.0 / 64.0))
                low = col - 64.0 * quarter
                block, quarter, low = (
                    jnp.concatenate([x, x], axis=0).astype(bf16) for x in (block, quarter, low)
                )
                values.append(
                    jnp.concatenate([jnp.where(q == quarter, block, zero) for q in quarter_ids], axis=0)
                )
                hits.append(
                    jnp.concatenate([jnp.where(k == low, one, zero) for k in low_ids], axis=0)
                )
            values = jnp.concatenate(
                [
                    jnp.concatenate([values[0], empty], axis=1),
                    jnp.concatenate([empty, values[1]], axis=1),
                ],
                axis=0,
            )
            sums = lax.dot_general(
                values,
                jnp.concatenate(hits, axis=1),
                (((1,), (1,)), ((), ())),
                preferred_element_type=f32,
            )
            row_0 = lists_s[1, group * GROUP + j]
            row_1 = lists_s[2, group * GROUP + j]
            shared = jnp.where(row_0 == row_1, sums[0:32], 0.0)
            sum_0 = acc_ref[row_0, :, 0:64] + sums[0:32]
            sum_1 = acc_ref[row_1, :, 0:64] + (sums[32:64] + shared)
            acc_ref[row_0, :, 0:64] = sum_0
            acc_ref[row_1, :, 0:64] = sum_1

    for ref, first, edge in ((top_ref, 0, edge_top), (bottom_ref, height - HALO, edge_bottom)):
        for i in range(HALO):
            for h, half in enumerate(join_quarters(acc_ref[first + i])):
                ref[i, :, 128 * h : 128 * h + 128] = half
        ref[HALO] = edge[...]


def join_quarters(tile):
    quarters = [tile[8 * q : 8 * q + 8] for q in range(4)]
    return [quarters[2 * h] + pltpu.roll(quarters[2 * h + 1], 64, 1) for h in range(2)]


def bin_blocks(message, edge_top, edge_bottom, height, width):
    sources = message.shape[0] // SLOTS
    vmem = pl.BlockSpec(memory_space=pltpu.VMEM)
    shape = lambda *dims: jax.ShapeDtypeStruct(dims, f32)
    return pl.pallas_call(
        bin_kernel,
        out_shape=(
            shape(height + 1, 32, 128),
            shape(HALO + 1, 8, width),
            shape(HALO + 1, 8, width),
        ),
        in_specs=[vmem] * 3,
        out_specs=(vmem,) * 3,
        scratch_shapes=[
            pltpu.VMEM((sources, 128), f32),
            pltpu.VMEM((8, ENTRIES), i32),
            pltpu.SMEM((8, ENTRIES), i32),
            pltpu.SemaphoreType.DMA,
        ],
        compiler_params=pltpu.CompilerParams(vmem_limit_bytes=16 << 20),
        name="bin",
    )(message, edge_top, edge_bottom)


def strip_kernel(acc_ref, edge_left, edge_right, left_ref, right_ref):
    lane = iota((8, 128), 1)
    blank = jnp.zeros((8, 128), f32)

    def take(j, carry):
        here = lane // 2 == j
        result = []
        for q in range(4):
            first = pltpu.roll(acc_ref[q * 64 + j, 0:8], 2 * j, 1)
            last = pltpu.roll(acc_ref[q * 64 + j, 24:32], (2 * j + 66) % 128, 1)
            result.append(jnp.where(here, first, carry[2 * q]))
            result.append(jnp.where(here, last, carry[2 * q + 1]))
        return tuple(result)

    strips = lax.fori_loop(0, 64, take, (blank,) * 8, unroll=8)
    for q in range(4):
        left_ref[q] = strips[2 * q]
        right_ref[q] = strips[2 * q + 1]
    left_ref[4] = edge_left[...]
    right_ref[4] = edge_right[...]


def column_strips(acc, edge_left, edge_right):
    vmem = pl.BlockSpec(memory_space=pltpu.VMEM)
    strip = jax.ShapeDtypeStruct(((acc.shape[0] - 1) // 64 + 1, 8, 128), f32)
    return pl.pallas_call(
        strip_kernel,
        out_shape=(strip, strip),
        in_specs=[vmem] * 3,
        out_specs=(vmem,) * 2,
        compiler_params=pltpu.CompilerParams(vmem_limit_bytes=12 << 20),
        name="column_strips",
    )(acc, edge_left, edge_right)


def relax(current, east_west, north_south, along_x, along_y):
    return current + along_x * (east_west - 2.0 * current) + along_y * (north_south - 2.0 * current)


def smooth_row(above, current, below, near, along_x, along_y):
    lane = iota((8, 128), 1)
    ahead = [pltpu.roll(half, 1, 1) for half in current]
    back = [pltpu.roll(half, 127, 1) for half in current]
    west = [jnp.where(lane == 0, near, ahead[0]), jnp.where(lane == 0, ahead[0], ahead[1])]
    east = [jnp.where(lane == 127, back[1], back[0]), jnp.where(lane == 127, near, back[1])]
    return [
        relax(current[h], east[h] + west[h], below[h] + above[h], along_x[h], along_y[h])
        for h in range(2)
    ]


def halves(ref, row):
    return [ref[row, :, 0:128], ref[row, :, 128:256]]


def keep(flag, parts):
    return [jnp.where(flag, part, 0.0) for part in parts]


def line(ref, row):
    both = ref[pl.ds(row, 1), :]
    return [both[:, 0:128], both[:, 128:256]]


def beyond(ref, flag):
    return [
        keep(flag, [ref[HALO, i : i + 1, h * 128 : h * 128 + 128] for h in range(2)])
        for i in range(2)
    ]


def first_kernel(flags_ref, acc_ref, up_ref, down_ref, cx_ref, cy_ref, once_ref, inner_ref):
    height = inner_ref.shape[0]
    has_up, has_down = flags_ref[0] > 0, flags_ref[1] > 0
    lane = iota((8, 128), 1)
    blank = jnp.zeros((8, 128), f32)
    up = [keep(has_up, halves(up_ref, i)) for i in range(2)]
    down = [keep(has_down, halves(down_ref, i)) for i in range(2)]

    def store(row, parts):
        once_ref[row, :, 0:128] = parts[0]
        once_ref[row, :, 128:256] = parts[1]

    store(0, smooth_row(up[0], up[1], join_quarters(acc_ref[0]), blank, *beyond(up_ref, has_up)))
    store(
        height + 1,
        smooth_row(
            join_quarters(acc_ref[height - 1]),
            down[0],
            down[1],
            blank,
            *beyond(down_ref, has_down),
        ),
    )
    steps = height // ROWS

    @pl.loop(0, steps)
    def _(block):
        start = block * ROWS
        before = join_quarters(acc_ref[jnp.maximum(start - 1, 0)])
        after = join_quarters(acc_ref[jnp.minimum(start + ROWS, height - 1)])
        before = [jnp.where(block == 0, up[1][h], before[h]) for h in range(2)]
        after = [jnp.where(block == steps - 1, down[0][h], after[h]) for h in range(2)]
        lines = [before] + [join_quarters(acc_ref[start + i]) for i in range(ROWS)] + [after]
        for i in range(ROWS):
            fresh = smooth_row(
                *lines[i : i + 3], blank, line(cx_ref, start + i), line(cy_ref, start + i)
            )
            store(start + i + 1, fresh)
            inner_ref[start + i] = jnp.where(lane < 64, lines[i + 1][0], lines[i + 1][1])


def first_pass(flags, acc, up, down, cx, cy):
    height, width = cx.shape
    vmem = pl.BlockSpec(memory_space=pltpu.VMEM)
    return pl.pallas_call(
        first_kernel,
        out_shape=(
            jax.ShapeDtypeStruct((height + 2, 8, width), f32),
            jax.ShapeDtypeStruct((height, 8, 128), f32),
        ),
        in_specs=[pl.BlockSpec(memory_space=pltpu.SMEM)] + [vmem] * 5,
        out_specs=(vmem, vmem),
        compiler_params=pltpu.CompilerParams(vmem_limit_bytes=20 << 20),
        name="first_pass",
    )(flags, acc, up, down, cx, cy)


def second_kernel(
    flags_ref,
    once_ref,
    inner_ref,
    up_ref,
    down_ref,
    west_ref,
    east_ref,
    cx_ref,
    cy_ref,
    gridded_ref,
    coverage_ref,
    mix_near,
    mix_far,
    near,
    far,
    twice,
    side_x,
    side_y,
):
    height, width = cx_ref.shape
    has_up, has_down = flags_ref[0] > 0, flags_ref[1] > 0
    has_west, has_east = flags_ref[2] > 0, flags_ref[3] > 0
    lane = iota((8, 128), 1)

    for q in range(4):
        west = jnp.where(has_west, west_ref[q], 0.0)
        east = jnp.where(has_east, east_ref[q], 0.0)
        even = lane % 2 == 0
        mix_near[q] = jnp.where(even, pltpu.roll(west, 127, 1), pltpu.roll(east, 127, 1))
        mix_far[q] = jnp.where(even, west, pltpu.roll(east, 126, 1))

    @pl.loop(0, 64, unroll=16)
    def _(j):
        for q in range(4):
            near[q * 64 + j + 1] = pltpu.roll(mix_near[q], 128 - 2 * j, 1)
            far[q * 64 + j] = pltpu.roll(mix_far[q], 128 - 2 * j, 1)

    for tile, row, flag in ((5, 0, has_up), (6, height + 1, has_down)):
        west = jnp.where(has_west & flag, west_ref[tile], 0.0)
        east = jnp.where(has_east & flag, east_ref[tile], 0.0)
        near[row] = jnp.where(lane < 64, pltpu.roll(west, 1, 1), pltpu.roll(east, 127, 1))

    upper = iota((128, 128), 0) < 64
    for i, side in enumerate((side_x, side_y)):
        for half in range(2):
            at = slice(2 * i + half, 2 * i + half + 1)
            west = jnp.where(has_west, west_ref[4, at, :], 0.0)
            east = jnp.where(has_east, east_ref[4, at, :], 0.0)
            both = jnp.where(
                upper, jnp.broadcast_to(west, (128, 128)), jnp.broadcast_to(east, (128, 128))
            )
            side[half * 128 : half * 128 + 128, :] = both.T

    above_x = beyond(up_ref, has_up)[0]
    below_x = beyond(down_ref, has_down)[0]
    steps = height // ROWS

    def completed(row, beside, along_x):
        first, last = halves(once_ref, row)
        return [
            first + jnp.where(lane == 0, along_x[0] * beside, 0.0),
            last + jnp.where(lane == 127, along_x[1] * beside, 0.0),
        ]

    @pl.loop(0, steps + 1)
    def _(g):
        block = jnp.maximum(g - 1, 0)
        for part in range(ROWS // 8):
            base = block * ROWS + part * 8
            rows = pl.ds(pl.multiple_of(base, 8), 8)
            for half in range(width // 128):
                cols = pl.ds(half * 128, 128)
                coverage = twice[half, pl.ds(base * 8 + 6, 8, stride=8), :]
                coverage_ref[rows, cols] = coverage
                scale = 1.0 / jnp.maximum(coverage, FLOOR)
                for c in range(6):
                    gridded_ref[c, rows, cols] = (
                        twice[half, pl.ds(base * 8 + c, 8, stride=8), :] * scale
                    )
        block = jnp.minimum(g, steps - 1)
        start = block * ROWS
        sides = [near[start + i] for i in range(ROWS + 2)]
        along_x = [line(cx_ref, start + i) for i in range(ROWS)]
        along_y = [line(cy_ref, start + i) for i in range(ROWS)]
        before = line(cx_ref, jnp.maximum(start - 1, 0))
        after = line(cx_ref, jnp.minimum(start + ROWS, height - 1))
        before = [jnp.where(block == 0, above_x[h], before[h]) for h in range(2)]
        after = [jnp.where(block == steps - 1, below_x[h], after[h]) for h in range(2)]
        factors = [before] + along_x + [after]
        lines = [completed(start + i, sides[i], factors[i]) for i in range(ROWS + 2)]
        for i in range(ROWS):
            beside = relax(
                sides[i + 1],
                inner_ref[start + i] + far[start + i],
                sides[i + 2] + sides[i],
                side_x[pl.ds(start + i, 1), :],
                side_y[pl.ds(start + i, 1), :],
            )
            fresh = smooth_row(*lines[i : i + 3], beside, along_x[i], along_y[i])
            for half in range(2):
                twice[half, pl.ds(pl.multiple_of((start + i) * 8, 8), 8), :] = fresh[half]


def second_pass(flags, once, inner, up, down, west, east, cx, cy):
    height, width = cx.shape
    vmem = pl.BlockSpec(memory_space=pltpu.VMEM)
    return pl.pallas_call(
        second_kernel,
        out_shape=(
            jax.ShapeDtypeStruct((6, height, width), f32),
            jax.ShapeDtypeStruct((height, width), f32),
        ),
        in_specs=[pl.BlockSpec(memory_space=pltpu.SMEM)] + [vmem] * 8,
        out_specs=(vmem, vmem),
        scratch_shapes=[
            pltpu.VMEM((4, 8, 128), f32),
            pltpu.VMEM((4, 8, 128), f32),
            pltpu.VMEM((height + 2, 8, 128), f32),
            pltpu.VMEM((height, 8, 128), f32),
            pltpu.VMEM((width // 128, height * 8, 128), f32),
            pltpu.VMEM((height, 128), f32),
            pltpu.VMEM((height, 128), f32),
        ],
        compiler_params=pltpu.CompilerParams(vmem_limit_bytes=24 << 20),
        name="second_pass",
    )(flags, once, inner, up, down, west, east, cx, cy)


def edge_kernel(after_ref, flags_ref, cx_ref, cy_ref, top_ref, bottom_ref, left_ref, right_ref):
    height, width = cx_ref.shape
    for ref in (top_ref, bottom_ref, left_ref, right_ref):
        ref[...] = jnp.zeros_like(ref)
    for i, block in enumerate((cx_ref, cy_ref)):
        top_ref[i : i + 1, :] = block[0:1, :]
        bottom_ref[i : i + 1, :] = block[height - 1 : height, :]
        first = block[:, 0:128].T
        last = block[:, width - 128 : width].T
        for half in range(2):
            at = slice(2 * i + half, 2 * i + half + 1)
            left_ref[at, :] = first[0:1, half * 128 : half * 128 + 128]
            right_ref[at, :] = last[127:128, half * 128 : half * 128 + 128]


def coefficient_edges(after, flags, cx, cy):
    width = cx.shape[1]
    vmem = pl.BlockSpec(memory_space=pltpu.VMEM)
    row = jax.ShapeDtypeStruct((8, width), f32)
    column = jax.ShapeDtypeStruct((8, 128), f32)
    return pl.pallas_call(
        edge_kernel,
        out_shape=(row, row, column, column),
        in_specs=[vmem, pl.BlockSpec(memory_space=pltpu.SMEM), vmem, vmem],
        out_specs=(vmem,) * 4,
        compiler_params=pltpu.CompilerParams(vmem_limit_bytes=8 << 20),
        name="coefficient_edges",
    )(after, flags, cx, cy)


def body(swath_bands, clear_weight, owners, tile_row, columns, counts, conduct_x, conduct_y):
    blocks = swath_bands.shape[0]
    height, width = conduct_x.shape
    across, along = lax.axis_size("gx"), lax.axis_size("gy")
    devices = across * along
    gx, gy = lax.axis_index("gx"), lax.axis_index("gy")
    flags = jnp.stack([gy > 0, gy < along - 1, gx > 0, gx < across - 1]).astype(i32)
    message, packed = pack(
        counts,
        owners.reshape(1, blocks),
        tile_row.reshape(1, blocks),
        jnp.transpose(swath_bands, (1, 0, 2)),
        clear_weight,
        columns,
        devices,
    )
    arrived = lax.all_to_all(
        message.reshape(devices, SLOTS, 8, 128),
        ("gx", "gy"),
        split_axis=0,
        concat_axis=0,
        tiled=True,
    ).reshape(devices * SLOTS, 8, 128)

    edges = coefficient_edges(packed, flags, conduct_x, conduct_y)
    acc, top, bottom = bin_blocks(arrived, edges[0], edges[1], height, width)
    left, right = column_strips(acc, edges[2], edges[3])
    up = lax.ppermute(bottom, "gy", ring(along, 1))
    down = lax.ppermute(top, "gy", ring(along, -1))
    near = jnp.concatenate([left, up[1:2, :, 0:128], down[0:1, :, 0:128]], axis=0)
    far = jnp.concatenate([right, up[1:2, :, width - 128 :], down[0:1, :, width - 128 :]], axis=0)
    west = lax.ppermute(far, "gx", ring(across, 1))
    east = lax.ppermute(near, "gx", ring(across, -1))
    once, inner = first_pass(flags, acc, up, down, conduct_x, conduct_y)
    return second_pass(flags, once, inner, up, down, west, east, conduct_x, conduct_y)


def solution(mesh):
    return jax.shard_map(
        body,
        mesh=mesh,
        in_specs=(
            P(("gx", "gy"), None, None),
            P(("gx", "gy"), None),
            P(("gx", "gy"), None),
            P(("gx", "gy")),
            P(("gx", "gy"), None),
            P(("gx", "gy")),
            P("gy", "gx"),
            P("gy", "gx"),
        ),
        out_specs=(P(None, "gy", "gx"), P("gy", "gx")),
        check_vma=False,
    )
```

```python
import functools

import jax
import jax.numpy as jnp
from jax import lax
from jax.experimental import pallas as pl
from jax.experimental.pallas import tpu as pltpu
from jax.sharding import PartitionSpec as P

CAPACITY = 12
SLOTS = CAPACITY + 1
COUNT_LANE = 14
CODES = 16
ENTRIES = 896
GROUP = 64
FIRST_ROWS = 64
ROWS = 32
FLOOR = 0.15
HALO = 2

f32 = jnp.float32
bf16 = jnp.bfloat16
i32 = jnp.int32


def iota(shape, dim):
    return lax.broadcasted_iota(i32, shape, dim)


def ring(count, step):
    return [(i, (i + step) % count) for i in range(count)]


def pack_kernel(
    count_ref,
    owner_ref,
    row_ref,
    swath_ref,
    weight_ref,
    cols_ref,
    out_ref,
    done_ref,
    owner_v,
    row_v,
    swath_v,
    weight_v,
    cols_v,
    rows_f,
    codes_f,
    slot_v,
    slot_s,
    sem,
    load_sems,
):
    bands, blocks, _ = swath_ref.shape
    loads = [
        pltpu.make_async_copy(source, target, load_sems.at[i])
        for i, (source, target) in enumerate(
            (
                (owner_ref, owner_v),
                (row_ref, row_v),
                (weight_ref, weight_v),
                (cols_ref, cols_v),
                (swath_ref, swath_v),
            )
        )
    ]
    for load in loads:
        load.start()
    done_ref[...] = jnp.zeros((8, 128), f32)
    devices = out_ref.shape[0] // SLOTS
    live_count = count_ref[0]
    chunk = iota((128, 256), 1)
    earlier = ((iota((128, 256), 0) < chunk) | (chunk >= 128)).astype(f32).astype(bf16)

    @pl.loop(0, devices // 2)
    def _(t):
        out_ref[pl.ds(t * 2 * SLOTS, 2 * SLOTS)] = jnp.zeros((2 * SLOTS, 8, 128), bf16)

    loads[0].wait()
    owner = owner_v[...]
    live = iota((1, blocks), 1) < live_count
    owner = jnp.where(live, owner, -1)
    named = (iota((devices, blocks), 0) == owner).astype(f32)
    named16 = named.astype(bf16)
    before, seen = [], jnp.zeros((devices, 128), f32)
    for first in range(0, blocks, 128):
        found = jnp.dot(
            named16[:, first : first + 128], earlier, preferred_element_type=f32
        )
        before.append(seen + found[:, 0:128])
        seen = seen + found[:, 128:256]
    before = jnp.concatenate(before, axis=1)
    rank = jnp.sum(named * before, axis=0, keepdims=True).astype(i32)
    slot_v[...] = jnp.where(live, owner * SLOTS + rank, CAPACITY)
    copy = pltpu.make_async_copy(slot_v, slot_s, sem)
    copy.start()
    entry = iota((128, blocks), 0)
    loads[1].wait()
    place = jnp.where(entry == rank, (row_v[...] + 1).astype(f32), 0.0)
    place = jnp.where(entry == COUNT_LANE, 1.0, place).astype(bf16)
    codes_f[...] = lax.dot_general(
        named16, place, (((1,), (1,)), ((), ())), preferred_element_type=f32
    )

    for load in loads[2:]:
        load.wait()

    @pl.loop(0, blocks // 16, unroll=4)
    def _(g):
        near = pl.ds(pl.multiple_of(g * 16, 16), 16)
        weight = weight_v[near, :].astype(f32)
        for c in range(bands):
            rows_f[pl.ds(g * 128 + c, 16, stride=8), :] = swath_v[c, near, :].astype(f32) * weight
        rows_f[pl.ds(g * 128 + bands, 16, stride=8), :] = weight
        rows_f[pl.ds(g * 128 + bands + 1, 16, stride=8), :] = cols_v[near, :].astype(f32)

    copy.wait()

    @pl.loop(0, (live_count + 15) // 16)
    def _(group):
        for i in range(16):
            b = group * 16 + i
            out_ref[slot_s[0, b]] = rows_f[pl.ds(pl.multiple_of(b * 8, 8), 8), :].astype(bf16)

    @pl.loop(0, devices, unroll=4)
    def _(t):
        code = codes_f[pl.ds(t, 1), :]
        out_ref[t * SLOTS + CAPACITY] = jnp.broadcast_to(code, (8, 128)).astype(bf16)


def pack(counts, owners, tile_row, swath, weight, columns, devices):
    blocks = weight.shape[0]
    vmem = pl.BlockSpec(memory_space=pltpu.VMEM)
    return pl.pallas_call(
        pack_kernel,
        out_shape=(
            jax.ShapeDtypeStruct((devices * SLOTS, 8, 128), bf16),
            jax.ShapeDtypeStruct((8, 128), f32),
        ),
        in_specs=[pl.BlockSpec(memory_space=pltpu.SMEM)]
        + [pl.BlockSpec(memory_space=pltpu.HBM)] * 5,
        out_specs=(vmem, vmem),
        scratch_shapes=[
            pltpu.VMEM((1, blocks), i32),
            pltpu.VMEM((1, blocks), i32),
            pltpu.VMEM(swath.shape, bf16),
            pltpu.VMEM(weight.shape, bf16),
            pltpu.VMEM(columns.shape, i32),
            pltpu.VMEM((blocks * 8, 128), f32),
            pltpu.VMEM((devices, 128), f32),
            pltpu.VMEM((1, blocks), i32),
            pltpu.SMEM((1, blocks), i32),
            pltpu.SemaphoreType.DMA,
            pltpu.SemaphoreType.DMA((5,)),
        ],
        compiler_params=pltpu.CompilerParams(vmem_limit_bytes=60 << 20),
        name="pack",
    )(counts, owners, tile_row, swath, weight, columns)


def bin_kernel(
    msg_ref,
    edge_top,
    edge_bottom,
    acc_ref,
    top_ref,
    bottom_ref,
    codes_v,
    lists_v,
    lists_s,
    sem,
):
    sources = msg_ref.shape[0] // SLOTS
    height = acc_ref.shape[0] - 1

    @pl.loop(0, sources // 8)
    def _(g):
        for i in range(8):
            s = g * 8 + i
            tile = msg_ref[s * SLOTS + CAPACITY].astype(f32)
            codes_v[pl.ds(s, 1), :] = tile[0:1, :]

    codes = codes_v[...].T[0:CODES, :]
    pairs = jnp.floor((codes[COUNT_LANE : COUNT_LANE + 1, :] + 1.0) * 0.5)
    earlier = (iota((sources, sources), 0) < iota((sources, sources), 1)).astype(f32).astype(bf16)
    before = jnp.dot(
        jnp.broadcast_to(pairs, (8, sources)).astype(bf16), earlier, preferred_element_type=f32
    )[0:1, :]
    total = (before + pairs)[:, sources - 1 : sources]
    entry = iota((ENTRIES, sources), 0).astype(f32)
    source = iota((1, sources), 1).astype(f32)
    facts, places = [], []
    for p in range(CAPACITY // 2):
        facts.append(
            jnp.concatenate(
                [
                    codes[2 * p : 2 * p + 2, :],
                    source,
                    jnp.full((1, sources), 2.0 * p, f32),
                    jnp.zeros((4, sources), f32),
                ],
                axis=0,
            ).astype(bf16)
        )
        place = jnp.where(pairs > p, before + p, -1.0)
        places.append(jnp.where(entry == place, 1.0, 0.0).astype(bf16))
    found = lax.dot_general(
        jnp.concatenate(facts, axis=1),
        jnp.concatenate(places, axis=1),
        (((1,), (1,)), ((), ())),
        preferred_element_type=f32,
    )
    rows = jnp.where(found[0:2] > 0.0, found[0:2] - 1.0, float(height))
    slots = found[2:3] * SLOTS + found[3:4]
    lists_v[0:1, :] = slots.astype(i32)
    lists_v[1:3, :] = rows.astype(i32)
    lists_v[3:4, :] = jnp.broadcast_to(total, (1, ENTRIES)).astype(i32)
    copy = pltpu.make_async_copy(lists_v, lists_s, sem)
    copy.start()

    @pl.loop(0, height // 16)
    def _(g):
        acc_ref[pl.ds(g * 16, 16)] = jnp.zeros((16, 32, 128), f32)

    acc_ref[height] = jnp.zeros((32, 128), f32)
    copy.wait()
    ids = iota((16, 128), 0).astype(f32)
    low_ids = [(ids + 16.0 * k).astype(bf16) for k in range(4)]
    quarter_ids = [(2.0 * k + jnp.floor(ids * 0.125)).astype(bf16) for k in range(2)]
    one = jnp.ones((16, 128), bf16)
    zero = jnp.zeros((16, 128), bf16)
    empty = jnp.zeros((32, 128), bf16)

    @pl.loop(0, (lists_s[3, 0] + GROUP - 1) // GROUP)
    def _(group):
        for j in range(GROUP):
            slot = lists_s[0, group * GROUP + j]
            values, hits = [], []
            for i in range(2):
                block = msg_ref[slot + i].astype(f32)
                col = jnp.broadcast_to(block[7:8, :], (8, 128))
                quarter = jnp.floor(col * (1.0 / 64.0))
                low = col - 64.0 * quarter
                block, quarter, low = (
                    jnp.concatenate([x, x], axis=0).astype(bf16) for x in (block, quarter, low)
                )
                values.append(
                    jnp.concatenate([jnp.where(q == quarter, block, zero) for q in quarter_ids], axis=0)
                )
                hits.append(
                    jnp.concatenate([jnp.where(k == low, one, zero) for k in low_ids], axis=0)
                )
            values = jnp.concatenate(
                [
                    jnp.concatenate([values[0], empty], axis=1),
                    jnp.concatenate([empty, values[1]], axis=1),
                ],
                axis=0,
            )
            sums = lax.dot_general(
                values,
                jnp.concatenate(hits, axis=1),
                (((1,), (1,)), ((), ())),
                preferred_element_type=f32,
            )
            row_0 = lists_s[1, group * GROUP + j]
            row_1 = lists_s[2, group * GROUP + j]
            shared = jnp.where(row_0 == row_1, sums[0:32], 0.0)
            sum_0 = acc_ref[row_0, :, 0:64] + sums[0:32]
            sum_1 = acc_ref[row_1, :, 0:64] + (sums[32:64] + shared)
            acc_ref[row_0, :, 0:64] = sum_0
            acc_ref[row_1, :, 0:64] = sum_1

    for ref, first, edge in ((top_ref, 0, edge_top), (bottom_ref, height - HALO, edge_bottom)):
        for i in range(HALO):
            for h, half in enumerate(join_quarters(acc_ref[first + i])):
                ref[i, :, 128 * h : 128 * h + 128] = half
        ref[HALO] = edge[...]


def join_quarters(tile):
    quarters = [tile[8 * q : 8 * q + 8] for q in range(4)]
    return [quarters[2 * h] + pltpu.roll(quarters[2 * h + 1], 64, 1) for h in range(2)]


def bin_blocks(message, edge_top, edge_bottom, height, width):
    sources = message.shape[0] // SLOTS
    vmem = pl.BlockSpec(memory_space=pltpu.VMEM)
    shape = lambda *dims: jax.ShapeDtypeStruct(dims, f32)
    return pl.pallas_call(
        bin_kernel,
        out_shape=(
            shape(height + 1, 32, 128),
            shape(HALO + 1, 8, width),
            shape(HALO + 1, 8, width),
        ),
        in_specs=[vmem] * 3,
        out_specs=(vmem,) * 3,
        scratch_shapes=[
            pltpu.VMEM((sources, 128), f32),
            pltpu.VMEM((8, ENTRIES), i32),
            pltpu.SMEM((8, ENTRIES), i32),
            pltpu.SemaphoreType.DMA,
        ],
        compiler_params=pltpu.CompilerParams(vmem_limit_bytes=16 << 20),
        name="bin",
    )(message, edge_top, edge_bottom)


def strip_kernel(acc_ref, edge_left, edge_right, left_ref, right_ref):
    lane = iota((8, 128), 1)
    blank = jnp.zeros((8, 128), f32)

    def take(j, carry):
        here = lane // 2 == j
        result = []
        for q in range(4):
            first = pltpu.roll(acc_ref[q * 64 + j, 0:8], 2 * j, 1)
            last = pltpu.roll(acc_ref[q * 64 + j, 24:32], (2 * j + 66) % 128, 1)
            result.append(jnp.where(here, first, carry[2 * q]))
            result.append(jnp.where(here, last, carry[2 * q + 1]))
        return tuple(result)

    strips = lax.fori_loop(0, 64, take, (blank,) * 8, unroll=8)
    for q in range(4):
        left_ref[q] = strips[2 * q]
        right_ref[q] = strips[2 * q + 1]
    left_ref[4] = edge_left[...]
    right_ref[4] = edge_right[...]


def column_strips(acc, edge_left, edge_right):
    vmem = pl.BlockSpec(memory_space=pltpu.VMEM)
    strip = jax.ShapeDtypeStruct(((acc.shape[0] - 1) // 64 + 1, 8, 128), f32)
    return pl.pallas_call(
        strip_kernel,
        out_shape=(strip, strip),
        in_specs=[vmem] * 3,
        out_specs=(vmem,) * 2,
        compiler_params=pltpu.CompilerParams(vmem_limit_bytes=12 << 20),
        name="column_strips",
    )(acc, edge_left, edge_right)


def relax(current, east_west, north_south, along_x, along_y):
    return current + along_x * (east_west - 2.0 * current) + along_y * (north_south - 2.0 * current)


def smooth_row(above, current, below, near, along_x, along_y):
    lane = iota((8, 128), 1)
    ahead = [pltpu.roll(half, 1, 1) for half in current]
    back = [pltpu.roll(half, 127, 1) for half in current]
    west = [jnp.where(lane == 0, near, ahead[0]), jnp.where(lane == 0, ahead[0], ahead[1])]
    east = [jnp.where(lane == 127, back[1], back[0]), jnp.where(lane == 127, near, back[1])]
    return [
        relax(current[h], east[h] + west[h], below[h] + above[h], along_x[h], along_y[h])
        for h in range(2)
    ]


def halves(ref, row):
    return [ref[row, :, 0:128], ref[row, :, 128:256]]


def keep(flag, parts):
    return [jnp.where(flag, part, 0.0) for part in parts]


def line(ref, row):
    both = ref[pl.ds(row, 1), :]
    return [both[:, 0:128], both[:, 128:256]]


def beyond(ref, flag):
    return [
        keep(flag, [ref[HALO, i : i + 1, h * 128 : h * 128 + 128] for h in range(2)])
        for i in range(2)
    ]


def first_kernel(flags_ref, acc_ref, up_ref, down_ref, cx_ref, cy_ref, once_ref, inner_ref):
    height = inner_ref.shape[0]
    has_up, has_down = flags_ref[0] > 0, flags_ref[1] > 0
    lane = iota((8, 128), 1)
    blank = jnp.zeros((8, 128), f32)
    up = [keep(has_up, halves(up_ref, i)) for i in range(2)]
    down = [keep(has_down, halves(down_ref, i)) for i in range(2)]

    def store(row, parts):
        once_ref[row, :, 0:128] = parts[0]
        once_ref[row, :, 128:256] = parts[1]

    store(0, smooth_row(up[0], up[1], join_quarters(acc_ref[0]), blank, *beyond(up_ref, has_up)))
    store(
        height + 1,
        smooth_row(
            join_quarters(acc_ref[height - 1]),
            down[0],
            down[1],
            blank,
            *beyond(down_ref, has_down),
        ),
    )
    steps = height // FIRST_ROWS

    @pl.loop(0, steps)
    def _(block):
        start = block * FIRST_ROWS
        before = join_quarters(acc_ref[jnp.maximum(start - 1, 0)])
        after = join_quarters(acc_ref[jnp.minimum(start + FIRST_ROWS, height - 1)])
        before = [jnp.where(block == 0, up[1][h], before[h]) for h in range(2)]
        after = [jnp.where(block == steps - 1, down[0][h], after[h]) for h in range(2)]
        lines = [before] + [join_quarters(acc_ref[start + i]) for i in range(FIRST_ROWS)] + [after]
        for i in range(FIRST_ROWS):
            fresh = smooth_row(
                *lines[i : i + 3], blank, line(cx_ref, start + i), line(cy_ref, start + i)
            )
            store(start + i + 1, fresh)
            inner_ref[start + i] = jnp.where(lane < 64, lines[i + 1][0], lines[i + 1][1])


def first_pass(flags, acc, up, down, cx, cy):
    height, width = cx.shape
    vmem = pl.BlockSpec(memory_space=pltpu.VMEM)
    return pl.pallas_call(
        first_kernel,
        out_shape=(
            jax.ShapeDtypeStruct((height + 2, 8, width), f32),
            jax.ShapeDtypeStruct((height, 8, 128), f32),
        ),
        in_specs=[pl.BlockSpec(memory_space=pltpu.SMEM)] + [vmem] * 5,
        out_specs=(vmem, vmem),
        compiler_params=pltpu.CompilerParams(vmem_limit_bytes=20 << 20),
        name="first_pass",
    )(flags, acc, up, down, cx, cy)


def second_kernel(
    flags_ref,
    once_ref,
    inner_ref,
    up_ref,
    down_ref,
    west_ref,
    east_ref,
    cx_ref,
    cy_ref,
    gridded_ref,
    coverage_ref,
    mix_near,
    mix_far,
    near,
    far,
    twice,
    side_x,
    side_y,
):
    height, width = cx_ref.shape
    has_up, has_down = flags_ref[0] > 0, flags_ref[1] > 0
    has_west, has_east = flags_ref[2] > 0, flags_ref[3] > 0
    lane = iota((8, 128), 1)

    for q in range(4):
        west = jnp.where(has_west, west_ref[q], 0.0)
        east = jnp.where(has_east, east_ref[q], 0.0)
        even = lane % 2 == 0
        mix_near[q] = jnp.where(even, pltpu.roll(west, 127, 1), pltpu.roll(east, 127, 1))
        mix_far[q] = jnp.where(even, west, pltpu.roll(east, 126, 1))

    @pl.loop(0, 64, unroll=16)
    def _(j):
        for q in range(4):
            near[q * 64 + j + 1] = pltpu.roll(mix_near[q], 128 - 2 * j, 1)
            far[q * 64 + j] = pltpu.roll(mix_far[q], 128 - 2 * j, 1)

    for tile, row, flag in ((5, 0, has_up), (6, height + 1, has_down)):
        west = jnp.where(has_west & flag, west_ref[tile], 0.0)
        east = jnp.where(has_east & flag, east_ref[tile], 0.0)
        near[row] = jnp.where(lane < 64, pltpu.roll(west, 1, 1), pltpu.roll(east, 127, 1))

    upper = iota((128, 128), 0) < 64
    for i, side in enumerate((side_x, side_y)):
        for half in range(2):
            at = slice(2 * i + half, 2 * i + half + 1)
            west = jnp.where(has_west, west_ref[4, at, :], 0.0)
            east = jnp.where(has_east, east_ref[4, at, :], 0.0)
            both = jnp.where(
                upper, jnp.broadcast_to(west, (128, 128)), jnp.broadcast_to(east, (128, 128))
            )
            side[half * 128 : half * 128 + 128, :] = both.T

    above_x = beyond(up_ref, has_up)[0]
    below_x = beyond(down_ref, has_down)[0]
    steps = height // ROWS

    def completed(row, beside, along_x):
        first, last = halves(once_ref, row)
        return [
            first + jnp.where(lane == 0, along_x[0] * beside, 0.0),
            last + jnp.where(lane == 127, along_x[1] * beside, 0.0),
        ]

    @pl.loop(0, steps + 1)
    def _(g):
        block = jnp.maximum(g - 1, 0)
        for part in range(ROWS // 8):
            base = block * ROWS + part * 8
            rows = pl.ds(pl.multiple_of(base, 8), 8)
            for half in range(width // 128):
                cols = pl.ds(half * 128, 128)
                coverage = twice[half, pl.ds(base * 8 + 6, 8, stride=8), :]
                coverage_ref[rows, cols] = coverage
                scale = 1.0 / jnp.maximum(coverage, FLOOR)
                for c in range(6):
                    gridded_ref[c, rows, cols] = (
                        twice[half, pl.ds(base * 8 + c, 8, stride=8), :] * scale
                    )
        block = jnp.minimum(g, steps - 1)
        start = block * ROWS
        sides = [near[start + i] for i in range(ROWS + 2)]
        along_x = [line(cx_ref, start + i) for i in range(ROWS)]
        along_y = [line(cy_ref, start + i) for i in range(ROWS)]
        before = line(cx_ref, jnp.maximum(start - 1, 0))
        after = line(cx_ref, jnp.minimum(start + ROWS, height - 1))
        before = [jnp.where(block == 0, above_x[h], before[h]) for h in range(2)]
        after = [jnp.where(block == steps - 1, below_x[h], after[h]) for h in range(2)]
        factors = [before] + along_x + [after]
        lines = [completed(start + i, sides[i], factors[i]) for i in range(ROWS + 2)]
        for i in range(ROWS):
            beside = relax(
                sides[i + 1],
                inner_ref[start + i] + far[start + i],
                sides[i + 2] + sides[i],
                side_x[pl.ds(start + i, 1), :],
                side_y[pl.ds(start + i, 1), :],
            )
            fresh = smooth_row(*lines[i : i + 3], beside, along_x[i], along_y[i])
            for half in range(2):
                twice[half, pl.ds(pl.multiple_of((start + i) * 8, 8), 8), :] = fresh[half]


def second_pass(flags, once, inner, up, down, west, east, cx, cy):
    height, width = cx.shape
    vmem = pl.BlockSpec(memory_space=pltpu.VMEM)
    return pl.pallas_call(
        second_kernel,
        out_shape=(
            jax.ShapeDtypeStruct((6, height, width), f32),
            jax.ShapeDtypeStruct((height, width), f32),
        ),
        in_specs=[pl.BlockSpec(memory_space=pltpu.SMEM)] + [vmem] * 8,
        out_specs=(vmem, vmem),
        scratch_shapes=[
            pltpu.VMEM((4, 8, 128), f32),
            pltpu.VMEM((4, 8, 128), f32),
            pltpu.VMEM((height + 2, 8, 128), f32),
            pltpu.VMEM((height, 8, 128), f32),
            pltpu.VMEM((width // 128, height * 8, 128), f32),
            pltpu.VMEM((height, 128), f32),
            pltpu.VMEM((height, 128), f32),
        ],
        compiler_params=pltpu.CompilerParams(vmem_limit_bytes=24 << 20),
        name="second_pass",
    )(flags, once, inner, up, down, west, east, cx, cy)


def edge_kernel(after_ref, flags_ref, cx_ref, cy_ref, top_ref, bottom_ref, left_ref, right_ref):
    height, width = cx_ref.shape
    for ref in (top_ref, bottom_ref, left_ref, right_ref):
        ref[...] = jnp.zeros_like(ref)
    for i, block in enumerate((cx_ref, cy_ref)):
        top_ref[i : i + 1, :] = block[0:1, :]
        bottom_ref[i : i + 1, :] = block[height - 1 : height, :]
        first = block[:, 0:128].T
        last = block[:, width - 128 : width].T
        for half in range(2):
            at = slice(2 * i + half, 2 * i + half + 1)
            left_ref[at, :] = first[0:1, half * 128 : half * 128 + 128]
            right_ref[at, :] = last[127:128, half * 128 : half * 128 + 128]


def coefficient_edges(after, flags, cx, cy):
    width = cx.shape[1]
    vmem = pl.BlockSpec(memory_space=pltpu.VMEM)
    row = jax.ShapeDtypeStruct((8, width), f32)
    column = jax.ShapeDtypeStruct((8, 128), f32)
    return pl.pallas_call(
        edge_kernel,
        out_shape=(row, row, column, column),
        in_specs=[vmem, pl.BlockSpec(memory_space=pltpu.SMEM), vmem, vmem],
        out_specs=(vmem,) * 4,
        compiler_params=pltpu.CompilerParams(vmem_limit_bytes=8 << 20),
        name="coefficient_edges",
    )(after, flags, cx, cy)


def body(swath_bands, clear_weight, owners, tile_row, columns, counts, conduct_x, conduct_y):
    blocks = swath_bands.shape[0]
    height, width = conduct_x.shape
    across, along = lax.axis_size("gx"), lax.axis_size("gy")
    devices = across * along
    gx, gy = lax.axis_index("gx"), lax.axis_index("gy")
    flags = jnp.stack([gy > 0, gy < along - 1, gx > 0, gx < across - 1]).astype(i32)
    message, packed = pack(
        counts,
        owners.reshape(1, blocks),
        tile_row.reshape(1, blocks),
        jnp.transpose(swath_bands, (1, 0, 2)),
        clear_weight,
        columns,
        devices,
    )
    arrived = lax.all_to_all(
        message.reshape(devices, SLOTS, 8, 128),
        ("gx", "gy"),
        split_axis=0,
        concat_axis=0,
        tiled=True,
    ).reshape(devices * SLOTS, 8, 128)

    edges = coefficient_edges(packed, flags, conduct_x, conduct_y)
    acc, top, bottom = bin_blocks(arrived, edges[0], edges[1], height, width)
    left, right = column_strips(acc, edges[2], edges[3])
    up = lax.ppermute(bottom, "gy", ring(along, 1))
    down = lax.ppermute(top, "gy", ring(along, -1))
    near = jnp.concatenate([left, up[1:2, :, 0:128], down[0:1, :, 0:128]], axis=0)
    far = jnp.concatenate([right, up[1:2, :, width - 128 :], down[0:1, :, width - 128 :]], axis=0)
    west = lax.ppermute(far, "gx", ring(across, 1))
    east = lax.ppermute(near, "gx", ring(across, -1))
    once, inner = first_pass(flags, acc, up, down, conduct_x, conduct_y)
    return second_pass(flags, once, inner, up, down, west, east, conduct_x, conduct_y)


def solution(mesh):
    return jax.shard_map(
        body,
        mesh=mesh,
        in_specs=(
            P(("gx", "gy"), None, None),
            P(("gx", "gy"), None),
            P(("gx", "gy"), None),
            P(("gx", "gy")),
            P(("gx", "gy"), None),
            P(("gx", "gy")),
            P("gy", "gx"),
            P("gy", "gx"),
        ),
        out_specs=(P(None, "gy", "gx"), P("gy", "gx")),
        check_vma=False,
    )
```

```python
import functools

import jax
import jax.numpy as jnp
from jax import lax
from jax.experimental import pallas as pl
from jax.experimental.pallas import tpu as pltpu
from jax.sharding import PartitionSpec as P

CAPACITY = 12
SLOTS = CAPACITY + 1
COUNT_LANE = 14
CODES = 16
ENTRIES = 896
GROUP = 96
FIRST_ROWS = 64
ROWS = 32
FLOOR = 0.15
HALO = 2

f32 = jnp.float32
bf16 = jnp.bfloat16
i32 = jnp.int32


def iota(shape, dim):
    return lax.broadcasted_iota(i32, shape, dim)


def ring(count, step):
    return [(i, (i + step) % count) for i in range(count)]


def pack_kernel(
    count_ref,
    owner_ref,
    row_ref,
    swath_ref,
    weight_ref,
    cols_ref,
    out_ref,
    done_ref,
    owner_v,
    row_v,
    swath_v,
    weight_v,
    cols_v,
    rows_f,
    codes_f,
    slot_v,
    slot_s,
    sem,
    load_sems,
):
    bands, blocks, _ = swath_ref.shape
    loads = [
        pltpu.make_async_copy(source, target, load_sems.at[i])
        for i, (source, target) in enumerate(
            (
                (owner_ref, owner_v),
                (row_ref, row_v),
                (weight_ref, weight_v),
                (cols_ref, cols_v),
                (swath_ref, swath_v),
            )
        )
    ]
    for load in loads:
        load.start()
    done_ref[...] = jnp.zeros((8, 128), f32)
    devices = out_ref.shape[0] // SLOTS
    live_count = count_ref[0]
    chunk = iota((128, 256), 1)
    earlier = ((iota((128, 256), 0) < chunk) | (chunk >= 128)).astype(f32).astype(bf16)

    @pl.loop(0, devices // 2)
    def _(t):
        out_ref[pl.ds(t * 2 * SLOTS, 2 * SLOTS)] = jnp.zeros((2 * SLOTS, 8, 128), bf16)

    loads[0].wait()
    owner = owner_v[...]
    live = iota((1, blocks), 1) < live_count
    owner = jnp.where(live, owner, -1)
    named = (iota((devices, blocks), 0) == owner).astype(f32)
    named16 = named.astype(bf16)
    before, seen = [], jnp.zeros((devices, 128), f32)
    for first in range(0, blocks, 128):
        found = jnp.dot(
            named16[:, first : first + 128], earlier, preferred_element_type=f32
        )
        before.append(seen + found[:, 0:128])
        seen = seen + found[:, 128:256]
    before = jnp.concatenate(before, axis=1)
    rank = jnp.sum(named * before, axis=0, keepdims=True).astype(i32)
    slot_v[...] = jnp.where(live, owner * SLOTS + rank, CAPACITY)
    copy = pltpu.make_async_copy(slot_v, slot_s, sem)
    copy.start()
    entry = iota((128, blocks), 0)
    loads[1].wait()
    place = jnp.where(entry == rank, (row_v[...] + 1).astype(f32), 0.0)
    place = jnp.where(entry == COUNT_LANE, 1.0, place).astype(bf16)
    codes_f[...] = lax.dot_general(
        named16, place, (((1,), (1,)), ((), ())), preferred_element_type=f32
    )

    for load in loads[2:]:
        load.wait()

    @pl.loop(0, blocks // 16, unroll=4)
    def _(g):
        near = pl.ds(pl.multiple_of(g * 16, 16), 16)
        weight = weight_v[near, :].astype(f32)
        for c in range(bands):
            rows_f[pl.ds(g * 128 + c, 16, stride=8), :] = swath_v[c, near, :].astype(f32) * weight
        rows_f[pl.ds(g * 128 + bands, 16, stride=8), :] = weight
        rows_f[pl.ds(g * 128 + bands + 1, 16, stride=8), :] = cols_v[near, :].astype(f32)

    copy.wait()

    @pl.loop(0, (live_count + 15) // 16)
    def _(group):
        for i in range(16):
            b = group * 16 + i
            out_ref[slot_s[0, b]] = rows_f[pl.ds(pl.multiple_of(b * 8, 8), 8), :].astype(bf16)

    @pl.loop(0, devices, unroll=4)
    def _(t):
        code = codes_f[pl.ds(t, 1), :]
        out_ref[t * SLOTS + CAPACITY] = jnp.broadcast_to(code, (8, 128)).astype(bf16)


def pack(counts, owners, tile_row, swath, weight, columns, devices):
    blocks = weight.shape[0]
    vmem = pl.BlockSpec(memory_space=pltpu.VMEM)
    return pl.pallas_call(
        pack_kernel,
        out_shape=(
            jax.ShapeDtypeStruct((devices * SLOTS, 8, 128), bf16),
            jax.ShapeDtypeStruct((8, 128), f32),
        ),
        in_specs=[pl.BlockSpec(memory_space=pltpu.SMEM)]
        + [pl.BlockSpec(memory_space=pltpu.HBM)] * 5,
        out_specs=(vmem, vmem),
        scratch_shapes=[
            pltpu.VMEM((1, blocks), i32),
            pltpu.VMEM((1, blocks), i32),
            pltpu.VMEM(swath.shape, bf16),
            pltpu.VMEM(weight.shape, bf16),
            pltpu.VMEM(columns.shape, i32),
            pltpu.VMEM((blocks * 8, 128), f32),
            pltpu.VMEM((devices, 128), f32),
            pltpu.VMEM((1, blocks), i32),
            pltpu.SMEM((1, blocks), i32),
            pltpu.SemaphoreType.DMA,
            pltpu.SemaphoreType.DMA((5,)),
        ],
        compiler_params=pltpu.CompilerParams(vmem_limit_bytes=60 << 20),
        name="pack",
    )(counts, owners, tile_row, swath, weight, columns)


def bin_kernel(
    msg_ref,
    edge_top,
    edge_bottom,
    acc_ref,
    top_ref,
    bottom_ref,
    codes_v,
    lists_v,
    lists_s,
    sem,
):
    sources = msg_ref.shape[0] // SLOTS
    height = acc_ref.shape[0] - 1

    @pl.loop(0, sources // 8)
    def _(g):
        for i in range(8):
            s = g * 8 + i
            tile = msg_ref[s * SLOTS + CAPACITY].astype(f32)
            codes_v[pl.ds(s, 1), :] = tile[0:1, :]

    codes = codes_v[...].T[0:CODES, :]
    pairs = jnp.floor((codes[COUNT_LANE : COUNT_LANE + 1, :] + 1.0) * 0.5)
    earlier = (iota((sources, sources), 0) < iota((sources, sources), 1)).astype(f32).astype(bf16)
    before = jnp.dot(
        jnp.broadcast_to(pairs, (8, sources)).astype(bf16), earlier, preferred_element_type=f32
    )[0:1, :]
    total = (before + pairs)[:, sources - 1 : sources]
    entry = iota((ENTRIES, sources), 0).astype(f32)
    source = iota((1, sources), 1).astype(f32)
    facts, places = [], []
    for p in range(CAPACITY // 2):
        facts.append(
            jnp.concatenate(
                [
                    codes[2 * p : 2 * p + 2, :],
                    source,
                    jnp.full((1, sources), 2.0 * p, f32),
                    jnp.zeros((4, sources), f32),
                ],
                axis=0,
            ).astype(bf16)
        )
        place = jnp.where(pairs > p, before + p, -1.0)
        places.append(jnp.where(entry == place, 1.0, 0.0).astype(bf16))
    found = lax.dot_general(
        jnp.concatenate(facts, axis=1),
        jnp.concatenate(places, axis=1),
        (((1,), (1,)), ((), ())),
        preferred_element_type=f32,
    )
    rows = jnp.where(found[0:2] > 0.0, found[0:2] - 1.0, float(height))
    slots = found[2:3] * SLOTS + found[3:4]
    lists_v[0:1, :] = slots.astype(i32)
    lists_v[1:3, :] = rows.astype(i32)
    lists_v[3:4, :] = jnp.broadcast_to(total, (1, ENTRIES)).astype(i32)
    copy = pltpu.make_async_copy(lists_v, lists_s, sem)
    copy.start()

    @pl.loop(0, height // 16)
    def _(g):
        acc_ref[pl.ds(g * 16, 16)] = jnp.zeros((16, 32, 128), f32)

    acc_ref[height] = jnp.zeros((32, 128), f32)
    copy.wait()
    ids = iota((16, 128), 0).astype(f32)
    low_ids = [(ids + 16.0 * k).astype(bf16) for k in range(4)]
    quarter_ids = [(2.0 * k + jnp.floor(ids * 0.125)).astype(bf16) for k in range(2)]
    one = jnp.ones((16, 128), bf16)
    zero = jnp.zeros((16, 128), bf16)
    empty = jnp.zeros((32, 128), bf16)

    @pl.loop(0, (lists_s[3, 0] + GROUP - 1) // GROUP)
    def _(group):
        for j in range(GROUP):
            slot = lists_s[0, group * GROUP + j]
            values, hits = [], []
            for i in range(2):
                block = msg_ref[slot + i].astype(f32)
                col = jnp.broadcast_to(block[7:8, :], (8, 128))
                quarter = jnp.floor(col * (1.0 / 64.0))
                low = col - 64.0 * quarter
                block, quarter, low = (
                    jnp.concatenate([x, x], axis=0).astype(bf16) for x in (block, quarter, low)
                )
                values.append(
                    jnp.concatenate([jnp.where(q == quarter, block, zero) for q in quarter_ids], axis=0)
                )
                hits.append(
                    jnp.concatenate([jnp.where(k == low, one, zero) for k in low_ids], axis=0)
                )
            values = jnp.concatenate(
                [
                    jnp.concatenate([values[0], empty], axis=1),
                    jnp.concatenate([empty, values[1]], axis=1),
                ],
                axis=0,
            )
            sums = lax.dot_general(
                values,
                jnp.concatenate(hits, axis=1),
                (((1,), (1,)), ((), ())),
                preferred_element_type=f32,
            )
            row_0 = lists_s[1, group * GROUP + j]
            row_1 = lists_s[2, group * GROUP + j]
            shared = jnp.where(row_0 == row_1, sums[0:32], 0.0)
            sum_0 = acc_ref[row_0, :, 0:64] + sums[0:32]
            sum_1 = acc_ref[row_1, :, 0:64] + (sums[32:64] + shared)
            acc_ref[row_0, :, 0:64] = sum_0
            acc_ref[row_1, :, 0:64] = sum_1

    for ref, first, edge in ((top_ref, 0, edge_top), (bottom_ref, height - HALO, edge_bottom)):
        for i in range(HALO):
            for h, half in enumerate(join_quarters(acc_ref[first + i])):
                ref[i, :, 128 * h : 128 * h + 128] = half
        ref[HALO] = edge[...]


def join_quarters(tile):
    quarters = [tile[8 * q : 8 * q + 8] for q in range(4)]
    return [quarters[2 * h] + pltpu.roll(quarters[2 * h + 1], 64, 1) for h in range(2)]


def bin_blocks(message, edge_top, edge_bottom, height, width):
    sources = message.shape[0] // SLOTS
    vmem = pl.BlockSpec(memory_space=pltpu.VMEM)
    shape = lambda *dims: jax.ShapeDtypeStruct(dims, f32)
    return pl.pallas_call(
        bin_kernel,
        out_shape=(
            shape(height + 1, 32, 128),
            shape(HALO + 1, 8, width),
            shape(HALO + 1, 8, width),
        ),
        in_specs=[vmem] * 3,
        out_specs=(vmem,) * 3,
        scratch_shapes=[
            pltpu.VMEM((sources, 128), f32),
            pltpu.VMEM((8, ENTRIES), i32),
            pltpu.SMEM((8, ENTRIES), i32),
            pltpu.SemaphoreType.DMA,
        ],
        compiler_params=pltpu.CompilerParams(vmem_limit_bytes=16 << 20),
        name="bin",
    )(message, edge_top, edge_bottom)


def strip_kernel(acc_ref, edge_left, edge_right, left_ref, right_ref):
    lane = iota((8, 128), 1)
    blank = jnp.zeros((8, 128), f32)

    def take(j, carry):
        here = lane // 2 == j
        result = []
        for q in range(4):
            first = pltpu.roll(acc_ref[q * 64 + j, 0:8], 2 * j, 1)
            last = pltpu.roll(acc_ref[q * 64 + j, 24:32], (2 * j + 66) % 128, 1)
            result.append(jnp.where(here, first, carry[2 * q]))
            result.append(jnp.where(here, last, carry[2 * q + 1]))
        return tuple(result)

    strips = lax.fori_loop(0, 64, take, (blank,) * 8, unroll=8)
    for q in range(4):
        left_ref[q] = strips[2 * q]
        right_ref[q] = strips[2 * q + 1]
    left_ref[4] = edge_left[...]
    right_ref[4] = edge_right[...]


def column_strips(acc, edge_left, edge_right):
    vmem = pl.BlockSpec(memory_space=pltpu.VMEM)
    strip = jax.ShapeDtypeStruct(((acc.shape[0] - 1) // 64 + 1, 8, 128), f32)
    return pl.pallas_call(
        strip_kernel,
        out_shape=(strip, strip),
        in_specs=[vmem] * 3,
        out_specs=(vmem,) * 2,
        compiler_params=pltpu.CompilerParams(vmem_limit_bytes=12 << 20),
        name="column_strips",
    )(acc, edge_left, edge_right)


def relax(current, east_west, north_south, along_x, along_y):
    return current + along_x * (east_west - 2.0 * current) + along_y * (north_south - 2.0 * current)


def smooth_row(above, current, below, near, along_x, along_y):
    lane = iota((8, 128), 1)
    ahead = [pltpu.roll(half, 1, 1) for half in current]
    back = [pltpu.roll(half, 127, 1) for half in current]
    west = [jnp.where(lane == 0, near, ahead[0]), jnp.where(lane == 0, ahead[0], ahead[1])]
    east = [jnp.where(lane == 127, back[1], back[0]), jnp.where(lane == 127, near, back[1])]
    return [
        relax(current[h], east[h] + west[h], below[h] + above[h], along_x[h], along_y[h])
        for h in range(2)
    ]


def halves(ref, row):
    return [ref[row, :, 0:128], ref[row, :, 128:256]]


def keep(flag, parts):
    return [jnp.where(flag, part, 0.0) for part in parts]


def line(ref, row):
    both = ref[pl.ds(row, 1), :]
    return [both[:, 0:128], both[:, 128:256]]


def beyond(ref, flag):
    return [
        keep(flag, [ref[HALO, i : i + 1, h * 128 : h * 128 + 128] for h in range(2)])
        for i in range(2)
    ]


def first_kernel(flags_ref, acc_ref, up_ref, down_ref, cx_ref, cy_ref, once_ref, inner_ref):
    height = inner_ref.shape[0]
    has_up, has_down = flags_ref[0] > 0, flags_ref[1] > 0
    lane = iota((8, 128), 1)
    blank = jnp.zeros((8, 128), f32)
    up = [keep(has_up, halves(up_ref, i)) for i in range(2)]
    down = [keep(has_down, halves(down_ref, i)) for i in range(2)]

    def store(row, parts):
        once_ref[row, :, 0:128] = parts[0]
        once_ref[row, :, 128:256] = parts[1]

    store(0, smooth_row(up[0], up[1], join_quarters(acc_ref[0]), blank, *beyond(up_ref, has_up)))
    store(
        height + 1,
        smooth_row(
            join_quarters(acc_ref[height - 1]),
            down[0],
            down[1],
            blank,
            *beyond(down_ref, has_down),
        ),
    )
    steps = height // FIRST_ROWS

    @pl.loop(0, steps)
    def _(block):
        start = block * FIRST_ROWS
        before = join_quarters(acc_ref[jnp.maximum(start - 1, 0)])
        after = join_quarters(acc_ref[jnp.minimum(start + FIRST_ROWS, height - 1)])
        before = [jnp.where(block == 0, up[1][h], before[h]) for h in range(2)]
        after = [jnp.where(block == steps - 1, down[0][h], after[h]) for h in range(2)]
        lines = [before] + [join_quarters(acc_ref[start + i]) for i in range(FIRST_ROWS)] + [after]
        for i in range(FIRST_ROWS):
            fresh = smooth_row(
                *lines[i : i + 3], blank, line(cx_ref, start + i), line(cy_ref, start + i)
            )
            store(start + i + 1, fresh)
            inner_ref[start + i] = jnp.where(lane < 64, lines[i + 1][0], lines[i + 1][1])


def first_pass(flags, acc, up, down, cx, cy):
    height, width = cx.shape
    vmem = pl.BlockSpec(memory_space=pltpu.VMEM)
    return pl.pallas_call(
        first_kernel,
        out_shape=(
            jax.ShapeDtypeStruct((height + 2, 8, width), f32),
            jax.ShapeDtypeStruct((height, 8, 128), f32),
        ),
        in_specs=[pl.BlockSpec(memory_space=pltpu.SMEM)] + [vmem] * 5,
        out_specs=(vmem, vmem),
        compiler_params=pltpu.CompilerParams(vmem_limit_bytes=20 << 20),
        name="first_pass",
    )(flags, acc, up, down, cx, cy)


def second_kernel(
    flags_ref,
    once_ref,
    inner_ref,
    up_ref,
    down_ref,
    west_ref,
    east_ref,
    cx_ref,
    cy_ref,
    gridded_out,
    coverage_out,
    gridded_ref,
    coverage_ref,
    mix_near,
    mix_far,
    near,
    far,
    twice,
    side_x,
    side_y,
    sems,
):
    height, width = cx_ref.shape
    has_up, has_down = flags_ref[0] > 0, flags_ref[1] > 0
    has_west, has_east = flags_ref[2] > 0, flags_ref[3] > 0
    lane = iota((8, 128), 1)

    for q in range(4):
        west = jnp.where(has_west, west_ref[q], 0.0)
        east = jnp.where(has_east, east_ref[q], 0.0)
        even = lane % 2 == 0
        mix_near[q] = jnp.where(even, pltpu.roll(west, 127, 1), pltpu.roll(east, 127, 1))
        mix_far[q] = jnp.where(even, west, pltpu.roll(east, 126, 1))

    @pl.loop(0, 64, unroll=16)
    def _(j):
        for q in range(4):
            near[q * 64 + j + 1] = pltpu.roll(mix_near[q], 128 - 2 * j, 1)
            far[q * 64 + j] = pltpu.roll(mix_far[q], 128 - 2 * j, 1)

    for tile, row, flag in ((5, 0, has_up), (6, height + 1, has_down)):
        west = jnp.where(has_west & flag, west_ref[tile], 0.0)
        east = jnp.where(has_east & flag, east_ref[tile], 0.0)
        near[row] = jnp.where(lane < 64, pltpu.roll(west, 1, 1), pltpu.roll(east, 127, 1))

    upper = iota((128, 128), 0) < 64
    for i, side in enumerate((side_x, side_y)):
        for half in range(2):
            at = slice(2 * i + half, 2 * i + half + 1)
            west = jnp.where(has_west, west_ref[4, at, :], 0.0)
            east = jnp.where(has_east, east_ref[4, at, :], 0.0)
            both = jnp.where(
                upper, jnp.broadcast_to(west, (128, 128)), jnp.broadcast_to(east, (128, 128))
            )
            side[half * 128 : half * 128 + 128, :] = both.T

    above_x = beyond(up_ref, has_up)[0]
    below_x = beyond(down_ref, has_down)[0]
    steps = height // ROWS

    def completed(row, beside, along_x):
        first, last = halves(once_ref, row)
        return [
            first + jnp.where(lane == 0, along_x[0] * beside, 0.0),
            last + jnp.where(lane == 127, along_x[1] * beside, 0.0),
        ]

    def write_out(block):
        rows = pl.ds(pl.multiple_of(block * ROWS, ROWS), ROWS)
        return (
            pltpu.make_async_copy(
                gridded_ref.at[:, rows, :], gridded_out.at[:, rows, :], sems.at[block, 0]
            ),
            pltpu.make_async_copy(
                coverage_ref.at[rows, :], coverage_out.at[rows, :], sems.at[block, 1]
            ),
        )

    @pl.loop(0, steps + 1)
    def _(g):
        block = jnp.maximum(g - 1, 0)
        for part in range(ROWS // 8):
            base = block * ROWS + part * 8
            rows = pl.ds(pl.multiple_of(base, 8), 8)
            for half in range(width // 128):
                cols = pl.ds(half * 128, 128)
                coverage = twice[half, pl.ds(base * 8 + 6, 8, stride=8), :]
                coverage_ref[rows, cols] = coverage
                scale = 1.0 / jnp.maximum(coverage, FLOOR)
                for c in range(6):
                    gridded_ref[c, rows, cols] = (
                        twice[half, pl.ds(base * 8 + c, 8, stride=8), :] * scale
                    )
        block = jnp.minimum(g, steps - 1)
        start = block * ROWS
        sides = [near[start + i] for i in range(ROWS + 2)]
        along_x = [line(cx_ref, start + i) for i in range(ROWS)]
        along_y = [line(cy_ref, start + i) for i in range(ROWS)]
        before = line(cx_ref, jnp.maximum(start - 1, 0))
        after = line(cx_ref, jnp.minimum(start + ROWS, height - 1))
        before = [jnp.where(block == 0, above_x[h], before[h]) for h in range(2)]
        after = [jnp.where(block == steps - 1, below_x[h], after[h]) for h in range(2)]
        factors = [before] + along_x + [after]
        lines = [completed(start + i, sides[i], factors[i]) for i in range(ROWS + 2)]
        for i in range(ROWS):
            beside = relax(
                sides[i + 1],
                inner_ref[start + i] + far[start + i],
                sides[i + 2] + sides[i],
                side_x[pl.ds(start + i, 1), :],
                side_y[pl.ds(start + i, 1), :],
            )
            fresh = smooth_row(*lines[i : i + 3], beside, along_x[i], along_y[i])
            for half in range(2):
                twice[half, pl.ds(pl.multiple_of((start + i) * 8, 8), 8), :] = fresh[half]

        @pl.when(g > 0)
        def _():
            for copy in write_out(g - 1):
                copy.start()

    for block in range(steps):
        for copy in write_out(block):
            copy.wait()


def second_pass(flags, once, inner, up, down, west, east, cx, cy):
    height, width = cx.shape
    vmem = pl.BlockSpec(memory_space=pltpu.VMEM)
    return pl.pallas_call(
        second_kernel,
        out_shape=(
            jax.ShapeDtypeStruct((6, height, width), f32),
            jax.ShapeDtypeStruct((height, width), f32),
        ),
        in_specs=[pl.BlockSpec(memory_space=pltpu.SMEM)] + [vmem] * 8,
        out_specs=(pl.BlockSpec(memory_space=pltpu.HBM),) * 2,
        scratch_shapes=[
            pltpu.VMEM((6, height, width), f32),
            pltpu.VMEM((height, width), f32),
            pltpu.VMEM((4, 8, 128), f32),
            pltpu.VMEM((4, 8, 128), f32),
            pltpu.VMEM((height + 2, 8, 128), f32),
            pltpu.VMEM((height, 8, 128), f32),
            pltpu.VMEM((width // 128, height * 8, 128), f32),
            pltpu.VMEM((height, 128), f32),
            pltpu.VMEM((height, 128), f32),
            pltpu.SemaphoreType.DMA((height // ROWS, 2)),
        ],
        compiler_params=pltpu.CompilerParams(vmem_limit_bytes=24 << 20),
        name="second_pass",
    )(flags, once, inner, up, down, west, east, cx, cy)


def edge_kernel(after_ref, flags_ref, cx_ref, cy_ref, top_ref, bottom_ref, left_ref, right_ref):
    height, width = cx_ref.shape
    for ref in (top_ref, bottom_ref, left_ref, right_ref):
        ref[...] = jnp.zeros_like(ref)
    for i, block in enumerate((cx_ref, cy_ref)):
        top_ref[i : i + 1, :] = block[0:1, :]
        bottom_ref[i : i + 1, :] = block[height - 1 : height, :]
        first = block[:, 0:128].T
        last = block[:, width - 128 : width].T
        for half in range(2):
            at = slice(2 * i + half, 2 * i + half + 1)
            left_ref[at, :] = first[0:1, half * 128 : half * 128 + 128]
            right_ref[at, :] = last[127:128, half * 128 : half * 128 + 128]


def coefficient_edges(after, flags, cx, cy):
    width = cx.shape[1]
    vmem = pl.BlockSpec(memory_space=pltpu.VMEM)
    row = jax.ShapeDtypeStruct((8, width), f32)
    column = jax.ShapeDtypeStruct((8, 128), f32)
    return pl.pallas_call(
        edge_kernel,
        out_shape=(row, row, column, column),
        in_specs=[vmem, pl.BlockSpec(memory_space=pltpu.SMEM), vmem, vmem],
        out_specs=(vmem,) * 4,
        compiler_params=pltpu.CompilerParams(vmem_limit_bytes=8 << 20),
        name="coefficient_edges",
    )(after, flags, cx, cy)


def body(swath_bands, clear_weight, owners, tile_row, columns, counts, conduct_x, conduct_y):
    blocks = swath_bands.shape[0]
    height, width = conduct_x.shape
    across, along = lax.axis_size("gx"), lax.axis_size("gy")
    devices = across * along
    gx, gy = lax.axis_index("gx"), lax.axis_index("gy")
    flags = jnp.stack([gy > 0, gy < along - 1, gx > 0, gx < across - 1]).astype(i32)
    message, packed = pack(
        counts,
        owners.reshape(1, blocks),
        tile_row.reshape(1, blocks),
        jnp.transpose(swath_bands, (1, 0, 2)),
        clear_weight,
        columns,
        devices,
    )
    arrived = lax.all_to_all(
        message.reshape(devices, SLOTS, 8, 128),
        ("gx", "gy"),
        split_axis=0,
        concat_axis=0,
        tiled=True,
    ).reshape(devices * SLOTS, 8, 128)

    edges = coefficient_edges(packed, flags, conduct_x, conduct_y)
    acc, top, bottom = bin_blocks(arrived, edges[0], edges[1], height, width)
    left, right = column_strips(acc, edges[2], edges[3])
    up = lax.ppermute(bottom, "gy", ring(along, 1))
    down = lax.ppermute(top, "gy", ring(along, -1))
    near = jnp.concatenate([left, up[1:2, :, 0:128], down[0:1, :, 0:128]], axis=0)
    far = jnp.concatenate([right, up[1:2, :, width - 128 :], down[0:1, :, width - 128 :]], axis=0)
    west = lax.ppermute(far, "gx", ring(across, 1))
    east = lax.ppermute(near, "gx", ring(across, -1))
    once, inner = first_pass(flags, acc, up, down, conduct_x, conduct_y)
    return second_pass(flags, once, inner, up, down, west, east, conduct_x, conduct_y)


def solution(mesh):
    return jax.shard_map(
        body,
        mesh=mesh,
        in_specs=(
            P(("gx", "gy"), None, None),
            P(("gx", "gy"), None),
            P(("gx", "gy"), None),
            P(("gx", "gy")),
            P(("gx", "gy"), None),
            P(("gx", "gy")),
            P("gy", "gx"),
            P("gy", "gx"),
        ),
        out_specs=(P(None, "gy", "gx"), P("gy", "gx")),
        check_vma=False,
    )
```

```python
import functools

import jax
import jax.numpy as jnp
from jax import lax
from jax.experimental import pallas as pl
from jax.experimental.pallas import tpu as pltpu
from jax.sharding import PartitionSpec as P

CAPACITY = 12
SLOTS = CAPACITY + 1
COUNT_LANE = 14
CODES = 16
ENTRIES = 896
GROUP = 96
FIRST_ROWS = 64
ROWS = 32
FLOOR = 0.15
HALO = 2

f32 = jnp.float32
bf16 = jnp.bfloat16
i32 = jnp.int32


def iota(shape, dim):
    return lax.broadcasted_iota(i32, shape, dim)


def ring(count, step):
    return [(i, (i + step) % count) for i in range(count)]


def pack_kernel(
    count_ref,
    owner_ref,
    row_ref,
    swath_ref,
    weight_ref,
    cols_ref,
    out_ref,
    done_ref,
    owner_v,
    row_v,
    swath_v,
    weight_v,
    cols_v,
    rows_f,
    codes_f,
    slot_v,
    slot_s,
    sem,
    load_sems,
):
    bands, blocks, _ = swath_ref.shape
    loads = [
        pltpu.make_async_copy(source, target, load_sems.at[i])
        for i, (source, target) in enumerate(
            (
                (owner_ref, owner_v),
                (row_ref, row_v),
                (weight_ref, weight_v),
                (cols_ref, cols_v),
                (swath_ref, swath_v),
            )
        )
    ]
    for load in loads:
        load.start()
    done_ref[...] = jnp.zeros((8, 128), f32)
    devices = out_ref.shape[0] // SLOTS
    live_count = count_ref[0]
    chunk = iota((128, 256), 1)
    earlier = ((iota((128, 256), 0) < chunk) | (chunk >= 128)).astype(f32).astype(bf16)

    @pl.loop(0, devices // 2)
    def _(t):
        out_ref[pl.ds(t * 2 * SLOTS, 2 * SLOTS)] = jnp.zeros((2 * SLOTS, 8, 128), bf16)

    loads[0].wait()
    owner = owner_v[...]
    live = iota((1, blocks), 1) < live_count
    owner = jnp.where(live, owner, -1)
    named = (iota((devices, blocks), 0) == owner).astype(f32)
    named16 = named.astype(bf16)
    before, seen = [], jnp.zeros((devices, 128), f32)
    for first in range(0, blocks, 128):
        found = jnp.dot(
            named16[:, first : first + 128], earlier, preferred_element_type=f32
        )
        before.append(seen + found[:, 0:128])
        seen = seen + found[:, 128:256]
    before = jnp.concatenate(before, axis=1)
    rank = jnp.sum(named * before, axis=0, keepdims=True).astype(i32)
    slot_v[...] = jnp.where(live, owner * SLOTS + rank, CAPACITY)
    copy = pltpu.make_async_copy(slot_v, slot_s, sem)
    copy.start()
    entry = iota((128, blocks), 0)
    loads[1].wait()
    place = jnp.where(entry == rank, (row_v[...] + 1).astype(f32), 0.0)
    place = jnp.where(entry == COUNT_LANE, 1.0, place).astype(bf16)
    codes_f[...] = lax.dot_general(
        named16, place, (((1,), (1,)), ((), ())), preferred_element_type=f32
    )

    for load in loads[2:]:
        load.wait()

    @pl.loop(0, blocks // 16, unroll=8)
    def _(g):
        near = pl.ds(pl.multiple_of(g * 16, 16), 16)
        weight = weight_v[near, :].astype(f32)
        for c in range(bands):
            rows_f[pl.ds(g * 128 + c, 16, stride=8), :] = swath_v[c, near, :].astype(f32) * weight
        rows_f[pl.ds(g * 128 + bands, 16, stride=8), :] = weight
        rows_f[pl.ds(g * 128 + bands + 1, 16, stride=8), :] = cols_v[near, :].astype(f32)

    copy.wait()

    @pl.loop(0, (live_count + 31) // 32)
    def _(group):
        for i in range(32):
            b = group * 32 + i
            out_ref[slot_s[0, b]] = rows_f[pl.ds(pl.multiple_of(b * 8, 8), 8), :].astype(bf16)

    @pl.loop(0, devices, unroll=16)
    def _(t):
        code = codes_f[pl.ds(t, 1), :]
        out_ref[t * SLOTS + CAPACITY] = jnp.broadcast_to(code, (8, 128)).astype(bf16)


def pack(counts, owners, tile_row, swath, weight, columns, devices):
    blocks = weight.shape[0]
    vmem = pl.BlockSpec(memory_space=pltpu.VMEM)
    return pl.pallas_call(
        pack_kernel,
        out_shape=(
            jax.ShapeDtypeStruct((devices * SLOTS, 8, 128), bf16),
            jax.ShapeDtypeStruct((8, 128), f32),
        ),
        in_specs=[pl.BlockSpec(memory_space=pltpu.SMEM)]
        + [pl.BlockSpec(memory_space=pltpu.HBM)] * 5,
        out_specs=(vmem, vmem),
        scratch_shapes=[
            pltpu.VMEM((1, blocks), i32),
            pltpu.VMEM((1, blocks), i32),
            pltpu.VMEM(swath.shape, bf16),
            pltpu.VMEM(weight.shape, bf16),
            pltpu.VMEM(columns.shape, i32),
            pltpu.VMEM((blocks * 8, 128), f32),
            pltpu.VMEM((devices, 128), f32),
            pltpu.VMEM((1, blocks), i32),
            pltpu.SMEM((1, blocks), i32),
            pltpu.SemaphoreType.DMA,
            pltpu.SemaphoreType.DMA((5,)),
        ],
        compiler_params=pltpu.CompilerParams(vmem_limit_bytes=60 << 20),
        name="pack",
    )(counts, owners, tile_row, swath, weight, columns)


def bin_kernel(
    msg_ref,
    edge_top,
    edge_bottom,
    acc_ref,
    top_ref,
    bottom_ref,
    codes_v,
    lists_v,
    lists_s,
    sem,
):
    sources = msg_ref.shape[0] // SLOTS
    height = acc_ref.shape[0] - 1

    @pl.loop(0, sources // 16)
    def _(g):
        for i in range(16):
            s = g * 16 + i
            tile = msg_ref[s * SLOTS + CAPACITY].astype(f32)
            codes_v[pl.ds(s, 1), :] = tile[0:1, :]

    codes = codes_v[...].T[0:CODES, :]
    pairs = jnp.floor((codes[COUNT_LANE : COUNT_LANE + 1, :] + 1.0) * 0.5)
    earlier = (iota((sources, sources), 0) < iota((sources, sources), 1)).astype(f32).astype(bf16)
    before = jnp.dot(
        jnp.broadcast_to(pairs, (8, sources)).astype(bf16), earlier, preferred_element_type=f32
    )[0:1, :]
    total = (before + pairs)[:, sources - 1 : sources]
    entry = iota((ENTRIES, sources), 0).astype(f32)
    source = iota((1, sources), 1).astype(f32)
    facts, places = [], []
    for p in range(CAPACITY // 2):
        facts.append(
            jnp.concatenate(
                [
                    codes[2 * p : 2 * p + 2, :],
                    source,
                    jnp.full((1, sources), 2.0 * p, f32),
                    jnp.zeros((4, sources), f32),
                ],
                axis=0,
            ).astype(bf16)
        )
        place = jnp.where(pairs > p, before + p, -1.0)
        places.append(jnp.where(entry == place, 1.0, 0.0).astype(bf16))
    found = lax.dot_general(
        jnp.concatenate(facts, axis=1),
        jnp.concatenate(places, axis=1),
        (((1,), (1,)), ((), ())),
        preferred_element_type=f32,
    )
    rows = jnp.where(found[0:2] > 0.0, found[0:2] - 1.0, float(height))
    slots = found[2:3] * SLOTS + found[3:4]
    lists_v[0:1, :] = slots.astype(i32)
    lists_v[1:3, :] = rows.astype(i32)
    lists_v[3:4, :] = jnp.broadcast_to(total, (1, ENTRIES)).astype(i32)
    copy = pltpu.make_async_copy(lists_v, lists_s, sem)
    copy.start()

    @pl.loop(0, height // 16)
    def _(g):
        acc_ref[pl.ds(g * 16, 16)] = jnp.zeros((16, 32, 128), f32)

    acc_ref[height] = jnp.zeros((32, 128), f32)
    copy.wait()
    ids = iota((16, 128), 0).astype(f32)
    low_ids = [(ids + 16.0 * k).astype(bf16) for k in range(4)]
    quarter_ids = [(2.0 * k + jnp.floor(ids * 0.125)).astype(bf16) for k in range(2)]
    one = jnp.ones((16, 128), bf16)
    zero = jnp.zeros((16, 128), bf16)
    empty = jnp.zeros((32, 128), bf16)

    @pl.loop(0, (lists_s[3, 0] + GROUP - 1) // GROUP)
    def _(group):
        for j in range(GROUP):
            slot = lists_s[0, group * GROUP + j]
            values, hits = [], []
            for i in range(2):
                block = msg_ref[slot + i].astype(f32)
                col = jnp.broadcast_to(block[7:8, :], (8, 128))
                quarter = jnp.floor(col * (1.0 / 64.0))
                low = col - 64.0 * quarter
                block, quarter, low = (
                    jnp.concatenate([x, x], axis=0).astype(bf16) for x in (block, quarter, low)
                )
                values.append(
                    jnp.concatenate([jnp.where(q == quarter, block, zero) for q in quarter_ids], axis=0)
                )
                hits.append(
                    jnp.concatenate([jnp.where(k == low, one, zero) for k in low_ids], axis=0)
                )
            values = jnp.concatenate(
                [
                    jnp.concatenate([values[0], empty], axis=1),
                    jnp.concatenate([empty, values[1]], axis=1),
                ],
                axis=0,
            )
            sums = lax.dot_general(
                values,
                jnp.concatenate(hits, axis=1),
                (((1,), (1,)), ((), ())),
                preferred_element_type=f32,
            )
            row_0 = lists_s[1, group * GROUP + j]
            row_1 = lists_s[2, group * GROUP + j]
            shared = jnp.where(row_0 == row_1, sums[0:32], 0.0)
            sum_0 = acc_ref[row_0, :, 0:64] + sums[0:32]
            sum_1 = acc_ref[row_1, :, 0:64] + (sums[32:64] + shared)
            acc_ref[row_0, :, 0:64] = sum_0
            acc_ref[row_1, :, 0:64] = sum_1

    for ref, first, edge in ((top_ref, 0, edge_top), (bottom_ref, height - HALO, edge_bottom)):
        for i in range(HALO):
            for h, half in enumerate(join_quarters(acc_ref[first + i])):
                ref[i, :, 128 * h : 128 * h + 128] = half
        ref[HALO] = edge[...]


def join_quarters(tile):
    quarters = [tile[8 * q : 8 * q + 8] for q in range(4)]
    return [quarters[2 * h] + pltpu.roll(quarters[2 * h + 1], 64, 1) for h in range(2)]


def bin_blocks(message, edge_top, edge_bottom, height, width):
    sources = message.shape[0] // SLOTS
    vmem = pl.BlockSpec(memory_space=pltpu.VMEM)
    shape = lambda *dims: jax.ShapeDtypeStruct(dims, f32)
    return pl.pallas_call(
        bin_kernel,
        out_shape=(
            shape(height + 1, 32, 128),
            shape(HALO + 1, 8, width),
            shape(HALO + 1, 8, width),
        ),
        in_specs=[vmem] * 3,
        out_specs=(vmem,) * 3,
        scratch_shapes=[
            pltpu.VMEM((sources, 128), f32),
            pltpu.VMEM((8, ENTRIES), i32),
            pltpu.SMEM((8, ENTRIES), i32),
            pltpu.SemaphoreType.DMA,
        ],
        compiler_params=pltpu.CompilerParams(vmem_limit_bytes=16 << 20),
        name="bin",
    )(message, edge_top, edge_bottom)


def strip_kernel(acc_ref, edge_left, edge_right, left_ref, right_ref):
    lane = iota((8, 128), 1)
    blank = jnp.zeros((8, 128), f32)

    def take(j, carry):
        here = lane // 2 == j
        result = []
        for q in range(4):
            first = pltpu.roll(acc_ref[q * 64 + j, 0:8], 2 * j, 1)
            last = pltpu.roll(acc_ref[q * 64 + j, 24:32], (2 * j + 66) % 128, 1)
            result.append(jnp.where(here, first, carry[2 * q]))
            result.append(jnp.where(here, last, carry[2 * q + 1]))
        return tuple(result)

    strips = lax.fori_loop(0, 64, take, (blank,) * 8, unroll=16)
    for q in range(4):
        left_ref[q] = strips[2 * q]
        right_ref[q] = strips[2 * q + 1]
    left_ref[4] = edge_left[...]
    right_ref[4] = edge_right[...]


def column_strips(acc, edge_left, edge_right):
    vmem = pl.BlockSpec(memory_space=pltpu.VMEM)
    strip = jax.ShapeDtypeStruct(((acc.shape[0] - 1) // 64 + 1, 8, 128), f32)
    return pl.pallas_call(
        strip_kernel,
        out_shape=(strip, strip),
        in_specs=[vmem] * 3,
        out_specs=(vmem,) * 2,
        compiler_params=pltpu.CompilerParams(vmem_limit_bytes=12 << 20),
        name="column_strips",
    )(acc, edge_left, edge_right)


def relax(current, east_west, north_south, along_x, along_y):
    return current + along_x * (east_west - 2.0 * current) + along_y * (north_south - 2.0 * current)


def smooth_row(above, current, below, near, along_x, along_y):
    lane = iota((8, 128), 1)
    ahead = [pltpu.roll(half, 1, 1) for half in current]
    back = [pltpu.roll(half, 127, 1) for half in current]
    west = [jnp.where(lane == 0, near, ahead[0]), jnp.where(lane == 0, ahead[0], ahead[1])]
    east = [jnp.where(lane == 127, back[1], back[0]), jnp.where(lane == 127, near, back[1])]
    return [
        relax(current[h], east[h] + west[h], below[h] + above[h], along_x[h], along_y[h])
        for h in range(2)
    ]


def halves(ref, row):
    return [ref[row, :, 0:128], ref[row, :, 128:256]]


def keep(flag, parts):
    return [jnp.where(flag, part, 0.0) for part in parts]


def line(ref, row):
    both = ref[pl.ds(row, 1), :]
    return [both[:, 0:128], both[:, 128:256]]


def beyond(ref, flag):
    return [
        keep(flag, [ref[HALO, i : i + 1, h * 128 : h * 128 + 128] for h in range(2)])
        for i in range(2)
    ]


def first_kernel(flags_ref, acc_ref, up_ref, down_ref, cx_ref, cy_ref, once_ref, inner_ref):
    height = inner_ref.shape[0]
    has_up, has_down = flags_ref[0] > 0, flags_ref[1] > 0
    lane = iota((8, 128), 1)
    blank = jnp.zeros((8, 128), f32)
    up = [keep(has_up, halves(up_ref, i)) for i in range(2)]
    down = [keep(has_down, halves(down_ref, i)) for i in range(2)]

    def store(row, parts):
        once_ref[row, :, 0:128] = parts[0]
        once_ref[row, :, 128:256] = parts[1]

    store(0, smooth_row(up[0], up[1], join_quarters(acc_ref[0]), blank, *beyond(up_ref, has_up)))
    store(
        height + 1,
        smooth_row(
            join_quarters(acc_ref[height - 1]),
            down[0],
            down[1],
            blank,
            *beyond(down_ref, has_down),
        ),
    )
    steps = height // FIRST_ROWS

    @pl.loop(0, steps)
    def _(block):
        start = block * FIRST_ROWS
        before = join_quarters(acc_ref[jnp.maximum(start - 1, 0)])
        after = join_quarters(acc_ref[jnp.minimum(start + FIRST_ROWS, height - 1)])
        before = [jnp.where(block == 0, up[1][h], before[h]) for h in range(2)]
        after = [jnp.where(block == steps - 1, down[0][h], after[h]) for h in range(2)]
        lines = [before] + [join_quarters(acc_ref[start + i]) for i in range(FIRST_ROWS)] + [after]
        for i in range(FIRST_ROWS):
            fresh = smooth_row(
                *lines[i : i + 3], blank, line(cx_ref, start + i), line(cy_ref, start + i)
            )
            store(start + i + 1, fresh)
            inner_ref[start + i] = jnp.where(lane < 64, lines[i + 1][0], lines[i + 1][1])


def first_pass(flags, acc, up, down, cx, cy):
    height, width = cx.shape
    vmem = pl.BlockSpec(memory_space=pltpu.VMEM)
    return pl.pallas_call(
        first_kernel,
        out_shape=(
            jax.ShapeDtypeStruct((height + 2, 8, width), f32),
            jax.ShapeDtypeStruct((height, 8, 128), f32),
        ),
        in_specs=[pl.BlockSpec(memory_space=pltpu.SMEM)] + [vmem] * 5,
        out_specs=(vmem, vmem),
        compiler_params=pltpu.CompilerParams(vmem_limit_bytes=20 << 20),
        name="first_pass",
    )(flags, acc, up, down, cx, cy)


def second_kernel(
    flags_ref,
    once_ref,
    inner_ref,
    up_ref,
    down_ref,
    west_ref,
    east_ref,
    cx_ref,
    cy_ref,
    gridded_out,
    coverage_out,
    gridded_ref,
    coverage_ref,
    mix_near,
    mix_far,
    near,
    far,
    twice,
    side_x,
    side_y,
    sems,
):
    height, width = cx_ref.shape
    has_up, has_down = flags_ref[0] > 0, flags_ref[1] > 0
    has_west, has_east = flags_ref[2] > 0, flags_ref[3] > 0
    lane = iota((8, 128), 1)

    for q in range(4):
        west = jnp.where(has_west, west_ref[q], 0.0)
        east = jnp.where(has_east, east_ref[q], 0.0)
        even = lane % 2 == 0
        mix_near[q] = jnp.where(even, pltpu.roll(west, 127, 1), pltpu.roll(east, 127, 1))
        mix_far[q] = jnp.where(even, west, pltpu.roll(east, 126, 1))

    @pl.loop(0, 64, unroll=16)
    def _(j):
        for q in range(4):
            near[q * 64 + j + 1] = pltpu.roll(mix_near[q], 128 - 2 * j, 1)
            far[q * 64 + j] = pltpu.roll(mix_far[q], 128 - 2 * j, 1)

    for tile, row, flag in ((5, 0, has_up), (6, height + 1, has_down)):
        west = jnp.where(has_west & flag, west_ref[tile], 0.0)
        east = jnp.where(has_east & flag, east_ref[tile], 0.0)
        near[row] = jnp.where(lane < 64, pltpu.roll(west, 1, 1), pltpu.roll(east, 127, 1))

    upper = iota((128, 128), 0) < 64
    for i, side in enumerate((side_x, side_y)):
        for half in range(2):
            at = slice(2 * i + half, 2 * i + half + 1)
            west = jnp.where(has_west, west_ref[4, at, :], 0.0)
            east = jnp.where(has_east, east_ref[4, at, :], 0.0)
            both = jnp.where(
                upper, jnp.broadcast_to(west, (128, 128)), jnp.broadcast_to(east, (128, 128))
            )
            side[half * 128 : half * 128 + 128, :] = both.T

    above_x = beyond(up_ref, has_up)[0]
    below_x = beyond(down_ref, has_down)[0]
    steps = height // ROWS

    def completed(row, beside, along_x):
        first, last = halves(once_ref, row)
        return [
            first + jnp.where(lane == 0, along_x[0] * beside, 0.0),
            last + jnp.where(lane == 127, along_x[1] * beside, 0.0),
        ]

    def write_out(block):
        rows = pl.ds(pl.multiple_of(block * ROWS, ROWS), ROWS)
        return (
            pltpu.make_async_copy(
                gridded_ref.at[:, rows, :], gridded_out.at[:, rows, :], sems.at[block, 0]
            ),
            pltpu.make_async_copy(
                coverage_ref.at[rows, :], coverage_out.at[rows, :], sems.at[block, 1]
            ),
        )

    @pl.loop(0, steps + 1)
    def _(g):
        block = jnp.maximum(g - 1, 0)
        for part in range(ROWS // 8):
            base = block * ROWS + part * 8
            rows = pl.ds(pl.multiple_of(base, 8), 8)
            for half in range(width // 128):
                cols = pl.ds(half * 128, 128)
                coverage = twice[half, pl.ds(base * 8 + 6, 8, stride=8), :]
                coverage_ref[rows, cols] = coverage
                scale = 1.0 / jnp.maximum(coverage, FLOOR)
                for c in range(6):
                    gridded_ref[c, rows, cols] = (
                        twice[half, pl.ds(base * 8 + c, 8, stride=8), :] * scale
                    )
        block = jnp.minimum(g, steps - 1)
        start = block * ROWS
        sides = [near[start + i] for i in range(ROWS + 2)]
        along_x = [line(cx_ref, start + i) for i in range(ROWS)]
        along_y = [line(cy_ref, start + i) for i in range(ROWS)]
        before = line(cx_ref, jnp.maximum(start - 1, 0))
        after = line(cx_ref, jnp.minimum(start + ROWS, height - 1))
        before = [jnp.where(block == 0, above_x[h], before[h]) for h in range(2)]
        after = [jnp.where(block == steps - 1, below_x[h], after[h]) for h in range(2)]
        factors = [before] + along_x + [after]
        lines = [completed(start + i, sides[i], factors[i]) for i in range(ROWS + 2)]
        for i in range(ROWS):
            beside = relax(
                sides[i + 1],
                inner_ref[start + i] + far[start + i],
                sides[i + 2] + sides[i],
                side_x[pl.ds(start + i, 1), :],
                side_y[pl.ds(start + i, 1), :],
            )
            fresh = smooth_row(*lines[i : i + 3], beside, along_x[i], along_y[i])
            for half in range(2):
                twice[half, pl.ds(pl.multiple_of((start + i) * 8, 8), 8), :] = fresh[half]

        @pl.when(g > 0)
        def _():
            for copy in write_out(g - 1):
                copy.start()

    for block in range(steps):
        for copy in write_out(block):
            copy.wait()


def second_pass(flags, once, inner, up, down, west, east, cx, cy):
    height, width = cx.shape
    vmem = pl.BlockSpec(memory_space=pltpu.VMEM)
    return pl.pallas_call(
        second_kernel,
        out_shape=(
            jax.ShapeDtypeStruct((6, height, width), f32),
            jax.ShapeDtypeStruct((height, width), f32),
        ),
        in_specs=[pl.BlockSpec(memory_space=pltpu.SMEM)] + [vmem] * 8,
        out_specs=(pl.BlockSpec(memory_space=pltpu.HBM),) * 2,
        scratch_shapes=[
            pltpu.VMEM((6, height, width), f32),
            pltpu.VMEM((height, width), f32),
            pltpu.VMEM((4, 8, 128), f32),
            pltpu.VMEM((4, 8, 128), f32),
            pltpu.VMEM((height + 2, 8, 128), f32),
            pltpu.VMEM((height, 8, 128), f32),
            pltpu.VMEM((width // 128, height * 8, 128), f32),
            pltpu.VMEM((height, 128), f32),
            pltpu.VMEM((height, 128), f32),
            pltpu.SemaphoreType.DMA((height // ROWS, 2)),
        ],
        compiler_params=pltpu.CompilerParams(vmem_limit_bytes=24 << 20),
        name="second_pass",
    )(flags, once, inner, up, down, west, east, cx, cy)


def edge_kernel(after_ref, flags_ref, cx_ref, cy_ref, top_ref, bottom_ref, left_ref, right_ref):
    height, width = cx_ref.shape
    for ref in (top_ref, bottom_ref, left_ref, right_ref):
        ref[...] = jnp.zeros_like(ref)
    for i, block in enumerate((cx_ref, cy_ref)):
        top_ref[i : i + 1, :] = block[0:1, :]
        bottom_ref[i : i + 1, :] = block[height - 1 : height, :]
        first = block[:, 0:128].T
        last = block[:, width - 128 : width].T
        for half in range(2):
            at = slice(2 * i + half, 2 * i + half + 1)
            left_ref[at, :] = first[0:1, half * 128 : half * 128 + 128]
            right_ref[at, :] = last[127:128, half * 128 : half * 128 + 128]


def coefficient_edges(after, flags, cx, cy):
    width = cx.shape[1]
    vmem = pl.BlockSpec(memory_space=pltpu.VMEM)
    row = jax.ShapeDtypeStruct((8, width), f32)
    column = jax.ShapeDtypeStruct((8, 128), f32)
    return pl.pallas_call(
        edge_kernel,
        out_shape=(row, row, column, column),
        in_specs=[vmem, pl.BlockSpec(memory_space=pltpu.SMEM), vmem, vmem],
        out_specs=(vmem,) * 4,
        compiler_params=pltpu.CompilerParams(vmem_limit_bytes=8 << 20),
        name="coefficient_edges",
    )(after, flags, cx, cy)


def body(swath_bands, clear_weight, owners, tile_row, columns, counts, conduct_x, conduct_y):
    blocks = swath_bands.shape[0]
    height, width = conduct_x.shape
    across, along = lax.axis_size("gx"), lax.axis_size("gy")
    devices = across * along
    gx, gy = lax.axis_index("gx"), lax.axis_index("gy")
    flags = jnp.stack([gy > 0, gy < along - 1, gx > 0, gx < across - 1]).astype(i32)
    message, packed = pack(
        counts,
        owners.reshape(1, blocks),
        tile_row.reshape(1, blocks),
        jnp.transpose(swath_bands, (1, 0, 2)),
        clear_weight,
        columns,
        devices,
    )
    arrived = lax.all_to_all(
        message.reshape(devices, SLOTS, 8, 128),
        ("gx", "gy"),
        split_axis=0,
        concat_axis=0,
        tiled=True,
    ).reshape(devices * SLOTS, 8, 128)

    edges = coefficient_edges(packed, flags, conduct_x, conduct_y)
    acc, top, bottom = bin_blocks(arrived, edges[0], edges[1], height, width)
    left, right = column_strips(acc, edges[2], edges[3])
    up = lax.ppermute(bottom, "gy", ring(along, 1))
    down = lax.ppermute(top, "gy", ring(along, -1))
    near = jnp.concatenate([left, up[1:2, :, 0:128], down[0:1, :, 0:128]], axis=0)
    far = jnp.concatenate([right, up[1:2, :, width - 128 :], down[0:1, :, width - 128 :]], axis=0)
    west = lax.ppermute(far, "gx", ring(across, 1))
    east = lax.ppermute(near, "gx", ring(across, -1))
    once, inner = first_pass(flags, acc, up, down, conduct_x, conduct_y)
    return second_pass(flags, once, inner, up, down, west, east, conduct_x, conduct_y)


def solution(mesh):
    return jax.shard_map(
        body,
        mesh=mesh,
        in_specs=(
            P(("gx", "gy"), None, None),
            P(("gx", "gy"), None),
            P(("gx", "gy"), None),
            P(("gx", "gy")),
            P(("gx", "gy"), None),
            P(("gx", "gy")),
            P("gy", "gx"),
            P("gy", "gx"),
        ),
        out_specs=(P(None, "gy", "gx"), P("gy", "gx")),
        check_vma=False,
    )
```

```python
import functools

import jax
import jax.numpy as jnp
from jax import lax
from jax.experimental import pallas as pl
from jax.experimental.pallas import tpu as pltpu
from jax.sharding import PartitionSpec as P

CAPACITY = 12
SLOTS = CAPACITY + 1
COUNT_LANE = 14
CODES = 16
ENTRIES = 896
GROUP = 96
FIRST_ROWS = 64
ROWS = 32
FLOOR = 0.15
HALO = 2

f32 = jnp.float32
bf16 = jnp.bfloat16
i32 = jnp.int32


def iota(shape, dim):
    return lax.broadcasted_iota(i32, shape, dim)


def ring(count, step):
    return [(i, (i + step) % count) for i in range(count)]


def pack_kernel(
    count_ref,
    owner_ref,
    row_ref,
    swath_ref,
    weight_ref,
    cols_ref,
    out_ref,
    done_ref,
    owner_v,
    row_v,
    swath_v,
    weight_v,
    cols_v,
    rows_f,
    codes_f,
    slot_v,
    slot_s,
    sem,
    load_sems,
):
    bands, blocks, _ = swath_ref.shape
    loads = [
        pltpu.make_async_copy(source, target, load_sems.at[i])
        for i, (source, target) in enumerate(
            (
                (owner_ref, owner_v),
                (row_ref, row_v),
                (weight_ref, weight_v),
                (cols_ref, cols_v),
                (swath_ref, swath_v),
            )
        )
    ]
    for load in loads:
        load.start()
    done_ref[...] = jnp.zeros((8, 128), f32)
    devices = out_ref.shape[0] // SLOTS
    live_count = count_ref[0]
    chunk = iota((128, 256), 1)
    earlier = ((iota((128, 256), 0) < chunk) | (chunk >= 128)).astype(f32).astype(bf16)

    @pl.loop(0, devices // 2)
    def _(t):
        out_ref[pl.ds(t * 2 * SLOTS, 2 * SLOTS)] = jnp.zeros((2 * SLOTS, 8, 128), bf16)

    loads[0].wait()
    owner = owner_v[...]
    live = iota((1, blocks), 1) < live_count
    owner = jnp.where(live, owner, -1)
    named = (iota((devices, blocks), 0) == owner).astype(f32)
    named16 = named.astype(bf16)
    before, seen = [], jnp.zeros((devices, 128), f32)
    for first in range(0, blocks, 128):
        found = jnp.dot(
            named16[:, first : first + 128], earlier, preferred_element_type=f32
        )
        before.append(seen + found[:, 0:128])
        seen = seen + found[:, 128:256]
    before = jnp.concatenate(before, axis=1)
    rank = jnp.sum(named * before, axis=0, keepdims=True).astype(i32)
    slot_v[...] = jnp.where(live, owner * SLOTS + rank, CAPACITY)
    copy = pltpu.make_async_copy(slot_v, slot_s, sem)
    copy.start()
    entry = iota((128, blocks), 0)
    loads[1].wait()
    place = jnp.where(entry == rank, (row_v[...] + 1).astype(f32), 0.0)
    place = jnp.where(entry == COUNT_LANE, 1.0, place).astype(bf16)
    codes_f[...] = lax.dot_general(
        named16, place, (((1,), (1,)), ((), ())), preferred_element_type=f32
    )

    for load in loads[2:]:
        load.wait()

    @pl.loop(0, blocks // 16, unroll=8)
    def _(g):
        near = pl.ds(pl.multiple_of(g * 16, 16), 16)
        weight = weight_v[near, :].astype(f32)
        for c in range(bands):
            rows_f[pl.ds(g * 128 + c, 16, stride=8), :] = swath_v[c, near, :].astype(f32) * weight
        rows_f[pl.ds(g * 128 + bands, 16, stride=8), :] = weight
        rows_f[pl.ds(g * 128 + bands + 1, 16, stride=8), :] = cols_v[near, :].astype(f32)

    copy.wait()

    @pl.loop(0, (live_count + 31) // 32)
    def _(group):
        for i in range(32):
            b = group * 32 + i
            out_ref[slot_s[0, b]] = rows_f[pl.ds(pl.multiple_of(b * 8, 8), 8), :].astype(bf16)

    @pl.loop(0, devices, unroll=16)
    def _(t):
        code = codes_f[pl.ds(t, 1), :]
        out_ref[t * SLOTS + CAPACITY] = jnp.broadcast_to(code, (8, 128)).astype(bf16)


def pack(counts, owners, tile_row, swath, weight, columns, devices):
    blocks = weight.shape[0]
    vmem = pl.BlockSpec(memory_space=pltpu.VMEM)
    return pl.pallas_call(
        pack_kernel,
        out_shape=(
            jax.ShapeDtypeStruct((devices * SLOTS, 8, 128), bf16),
            jax.ShapeDtypeStruct((8, 128), f32),
        ),
        in_specs=[pl.BlockSpec(memory_space=pltpu.SMEM)]
        + [pl.BlockSpec(memory_space=pltpu.HBM)] * 5,
        out_specs=(vmem, vmem),
        scratch_shapes=[
            pltpu.VMEM((1, blocks), i32),
            pltpu.VMEM((1, blocks), i32),
            pltpu.VMEM(swath.shape, bf16),
            pltpu.VMEM(weight.shape, bf16),
            pltpu.VMEM(columns.shape, i32),
            pltpu.VMEM((blocks * 8, 128), f32),
            pltpu.VMEM((devices, 128), f32),
            pltpu.VMEM((1, blocks), i32),
            pltpu.SMEM((1, blocks), i32),
            pltpu.SemaphoreType.DMA,
            pltpu.SemaphoreType.DMA((5,)),
        ],
        compiler_params=pltpu.CompilerParams(vmem_limit_bytes=60 << 20),
        name="pack",
    )(counts, owners, tile_row, swath, weight, columns)


def bin_kernel(
    msg_ref,
    edge_top,
    edge_bottom,
    acc_ref,
    top_ref,
    bottom_ref,
    codes_v,
    lists_v,
    lists_s,
    sem,
):
    sources = msg_ref.shape[0] // SLOTS
    height = acc_ref.shape[0] - 1

    @pl.loop(0, sources // 16)
    def _(g):
        for i in range(16):
            s = g * 16 + i
            tile = msg_ref[s * SLOTS + CAPACITY].astype(f32)
            codes_v[pl.ds(s, 1), :] = tile[0:1, :]

    codes = codes_v[...].T[0:CODES, :]
    pairs = jnp.floor((codes[COUNT_LANE : COUNT_LANE + 1, :] + 1.0) * 0.5)
    earlier = (iota((sources, sources), 0) < iota((sources, sources), 1)).astype(f32).astype(bf16)
    before = jnp.dot(
        jnp.broadcast_to(pairs, (8, sources)).astype(bf16), earlier, preferred_element_type=f32
    )[0:1, :]
    total = (before + pairs)[:, sources - 1 : sources]
    entry = iota((ENTRIES, sources), 0).astype(f32)
    source = iota((1, sources), 1).astype(f32)
    facts, places = [], []
    for p in range(CAPACITY // 2):
        facts.append(
            jnp.concatenate(
                [
                    codes[2 * p : 2 * p + 2, :],
                    source,
                    jnp.full((1, sources), 2.0 * p, f32),
                    jnp.zeros((4, sources), f32),
                ],
                axis=0,
            ).astype(bf16)
        )
        place = jnp.where(pairs > p, before + p, -1.0)
        places.append(jnp.where(entry == place, 1.0, 0.0).astype(bf16))
    found = lax.dot_general(
        jnp.concatenate(facts, axis=1),
        jnp.concatenate(places, axis=1),
        (((1,), (1,)), ((), ())),
        preferred_element_type=f32,
    )
    rows = jnp.where(found[0:2] > 0.0, found[0:2] - 1.0, float(height))
    slots = found[2:3] * SLOTS + found[3:4]
    lists_v[0:1, :] = slots.astype(i32)
    lists_v[1:3, :] = rows.astype(i32)
    lists_v[3:4, :] = jnp.broadcast_to(total, (1, ENTRIES)).astype(i32)
    copy = pltpu.make_async_copy(lists_v, lists_s, sem)
    copy.start()

    @pl.loop(0, height // 16)
    def _(g):
        acc_ref[pl.ds(g * 16, 16)] = jnp.zeros((16, 32, 128), f32)

    acc_ref[height] = jnp.zeros((32, 128), f32)
    copy.wait()
    ids = iota((16, 128), 0).astype(f32)
    low_ids = [(ids + 16.0 * k).astype(bf16) for k in range(4)]
    quarter_ids = [(2.0 * k + jnp.floor(ids * 0.125)).astype(bf16) for k in range(2)]
    one = jnp.ones((16, 128), bf16)
    zero = jnp.zeros((16, 128), bf16)
    empty = jnp.zeros((32, 128), bf16)

    @pl.loop(0, (lists_s[3, 0] + GROUP - 1) // GROUP)
    def _(group):
        for j in range(GROUP):
            slot = lists_s[0, group * GROUP + j]
            values, hits = [], []
            for i in range(2):
                block = msg_ref[slot + i].astype(f32)
                col = jnp.broadcast_to(block[7:8, :], (8, 128))
                quarter = jnp.floor(col * (1.0 / 64.0))
                low = col - 64.0 * quarter
                block, quarter, low = (
                    jnp.concatenate([x, x], axis=0).astype(bf16) for x in (block, quarter, low)
                )
                values.append(
                    jnp.concatenate([jnp.where(q == quarter, block, zero) for q in quarter_ids], axis=0)
                )
                hits.append(
                    jnp.concatenate([jnp.where(k == low, one, zero) for k in low_ids], axis=0)
                )
            values = jnp.concatenate(
                [
                    jnp.concatenate([values[0], empty], axis=1),
                    jnp.concatenate([empty, values[1]], axis=1),
                ],
                axis=0,
            )
            sums = lax.dot_general(
                values,
                jnp.concatenate(hits, axis=1),
                (((1,), (1,)), ((), ())),
                preferred_element_type=f32,
            )
            row_0 = lists_s[1, group * GROUP + j]
            row_1 = lists_s[2, group * GROUP + j]
            shared = jnp.where(row_0 == row_1, sums[0:32], 0.0)
            sum_0 = acc_ref[row_0, :, 0:64] + sums[0:32]
            sum_1 = acc_ref[row_1, :, 0:64] + (sums[32:64] + shared)
            acc_ref[row_0, :, 0:64] = sum_0
            acc_ref[row_1, :, 0:64] = sum_1

    for ref, first, edge in ((top_ref, 0, edge_top), (bottom_ref, height - HALO, edge_bottom)):
        for i in range(HALO):
            for h, half in enumerate(join_quarters(acc_ref[first + i])):
                ref[i, :, 128 * h : 128 * h + 128] = half
        ref[HALO] = edge[...]


def join_quarters(tile):
    quarters = [tile[8 * q : 8 * q + 8] for q in range(4)]
    return [quarters[2 * h] + pltpu.roll(quarters[2 * h + 1], 64, 1) for h in range(2)]


def bin_blocks(message, edge_top, edge_bottom, height, width):
    sources = message.shape[0] // SLOTS
    vmem = pl.BlockSpec(memory_space=pltpu.VMEM)
    shape = lambda *dims: jax.ShapeDtypeStruct(dims, f32)
    return pl.pallas_call(
        bin_kernel,
        out_shape=(
            shape(height + 1, 32, 128),
            shape(HALO + 1, 8, width),
            shape(HALO + 1, 8, width),
        ),
        in_specs=[vmem] * 3,
        out_specs=(vmem,) * 3,
        scratch_shapes=[
            pltpu.VMEM((sources, 128), f32),
            pltpu.VMEM((8, ENTRIES), i32),
            pltpu.SMEM((8, ENTRIES), i32),
            pltpu.SemaphoreType.DMA,
        ],
        compiler_params=pltpu.CompilerParams(vmem_limit_bytes=16 << 20),
        name="bin",
    )(message, edge_top, edge_bottom)


def strip_kernel(acc_ref, edge_left, edge_right, left_ref, right_ref):
    lane = iota((8, 128), 1)
    blank = jnp.zeros((8, 128), f32)

    def take(j, carry):
        here = lane // 2 == j
        result = []
        for q in range(4):
            first = pltpu.roll(acc_ref[q * 64 + j, 0:8], 2 * j, 1)
            last = pltpu.roll(acc_ref[q * 64 + j, 24:32], (2 * j + 66) % 128, 1)
            result.append(jnp.where(here, first, carry[2 * q]))
            result.append(jnp.where(here, last, carry[2 * q + 1]))
        return tuple(result)

    strips = lax.fori_loop(0, 64, take, (blank,) * 8, unroll=16)
    for q in range(4):
        left_ref[q] = strips[2 * q]
        right_ref[q] = strips[2 * q + 1]
    left_ref[4] = edge_left[...]
    right_ref[4] = edge_right[...]


def column_strips(acc, edge_left, edge_right):
    vmem = pl.BlockSpec(memory_space=pltpu.VMEM)
    strip = jax.ShapeDtypeStruct(((acc.shape[0] - 1) // 64 + 1, 8, 128), f32)
    return pl.pallas_call(
        strip_kernel,
        out_shape=(strip, strip),
        in_specs=[vmem] * 3,
        out_specs=(vmem,) * 2,
        compiler_params=pltpu.CompilerParams(vmem_limit_bytes=12 << 20),
        name="column_strips",
    )(acc, edge_left, edge_right)


def relax(current, east_west, north_south, along_x, along_y):
    return current + along_x * (east_west - 2.0 * current) + along_y * (north_south - 2.0 * current)


def smooth_row(above, current, below, near, along_x, along_y):
    lane = iota((8, 128), 1)
    ahead = [pltpu.roll(half, 1, 1) for half in current]
    back = [pltpu.roll(half, 127, 1) for half in current]
    west = [jnp.where(lane == 0, near, ahead[0]), jnp.where(lane == 0, ahead[0], ahead[1])]
    east = [jnp.where(lane == 127, back[1], back[0]), jnp.where(lane == 127, near, back[1])]
    return [
        relax(current[h], east[h] + west[h], below[h] + above[h], along_x[h], along_y[h])
        for h in range(2)
    ]


def halves(ref, row):
    return [ref[row, :, 0:128], ref[row, :, 128:256]]


def keep(flag, parts):
    return [jnp.where(flag, part, 0.0) for part in parts]


def line(ref, row):
    both = ref[pl.ds(row, 1), :]
    return [both[:, 0:128], both[:, 128:256]]


def beyond(ref, flag):
    return [
        keep(flag, [ref[HALO, i : i + 1, h * 128 : h * 128 + 128] for h in range(2)])
        for i in range(2)
    ]


def first_kernel(flags_ref, acc_ref, up_ref, down_ref, cx_ref, cy_ref, once_ref, inner_ref):
    height = inner_ref.shape[0]
    has_up, has_down = flags_ref[0] > 0, flags_ref[1] > 0
    lane = iota((8, 128), 1)
    blank = jnp.zeros((8, 128), f32)
    up = [keep(has_up, halves(up_ref, i)) for i in range(2)]
    down = [keep(has_down, halves(down_ref, i)) for i in range(2)]

    def store(row, parts):
        once_ref[row, :, 0:128] = parts[0]
        once_ref[row, :, 128:256] = parts[1]

    store(0, smooth_row(up[0], up[1], join_quarters(acc_ref[0]), blank, *beyond(up_ref, has_up)))
    store(
        height + 1,
        smooth_row(
            join_quarters(acc_ref[height - 1]),
            down[0],
            down[1],
            blank,
            *beyond(down_ref, has_down),
        ),
    )
    steps = height // FIRST_ROWS

    @pl.loop(0, steps)
    def _(block):
        start = block * FIRST_ROWS
        before = join_quarters(acc_ref[jnp.maximum(start - 1, 0)])
        after = join_quarters(acc_ref[jnp.minimum(start + FIRST_ROWS, height - 1)])
        before = [jnp.where(block == 0, up[1][h], before[h]) for h in range(2)]
        after = [jnp.where(block == steps - 1, down[0][h], after[h]) for h in range(2)]
        lines = [before] + [join_quarters(acc_ref[start + i]) for i in range(FIRST_ROWS)] + [after]
        for i in range(FIRST_ROWS):
            fresh = smooth_row(
                *lines[i : i + 3], blank, line(cx_ref, start + i), line(cy_ref, start + i)
            )
            store(start + i + 1, fresh)
            inner_ref[start + i] = jnp.where(lane < 64, lines[i + 1][0], lines[i + 1][1])


def first_pass(flags, acc, up, down, cx, cy):
    height, width = cx.shape
    vmem = pl.BlockSpec(memory_space=pltpu.VMEM)
    return pl.pallas_call(
        first_kernel,
        out_shape=(
            jax.ShapeDtypeStruct((height + 2, 8, width), f32),
            jax.ShapeDtypeStruct((height, 8, 128), f32),
        ),
        in_specs=[pl.BlockSpec(memory_space=pltpu.SMEM)] + [vmem] * 5,
        out_specs=(vmem, vmem),
        compiler_params=pltpu.CompilerParams(vmem_limit_bytes=20 << 20),
        name="first_pass",
    )(flags, acc, up, down, cx, cy)


def second_kernel(
    flags_ref,
    once_ref,
    inner_ref,
    up_ref,
    down_ref,
    west_ref,
    east_ref,
    cx_ref,
    cy_ref,
    gridded_out,
    coverage_out,
    gridded_ref,
    coverage_ref,
    mix_near,
    mix_far,
    near,
    far,
    twice,
    side_x,
    side_y,
    sems,
):
    height, width = cx_ref.shape
    has_up, has_down = flags_ref[0] > 0, flags_ref[1] > 0
    has_west, has_east = flags_ref[2] > 0, flags_ref[3] > 0
    lane = iota((8, 128), 1)

    for q in range(4):
        west = jnp.where(has_west, west_ref[q], 0.0)
        east = jnp.where(has_east, east_ref[q], 0.0)
        even = lane % 2 == 0
        mix_near[q] = jnp.where(even, pltpu.roll(west, 127, 1), pltpu.roll(east, 127, 1))
        mix_far[q] = jnp.where(even, west, pltpu.roll(east, 126, 1))

    @pl.loop(0, 64, unroll=64)
    def _(j):
        for q in range(4):
            near[q * 64 + j + 1] = pltpu.roll(mix_near[q], 128 - 2 * j, 1)
            far[q * 64 + j] = pltpu.roll(mix_far[q], 128 - 2 * j, 1)

    for tile, row, flag in ((5, 0, has_up), (6, height + 1, has_down)):
        west = jnp.where(has_west & flag, west_ref[tile], 0.0)
        east = jnp.where(has_east & flag, east_ref[tile], 0.0)
        near[row] = jnp.where(lane < 64, pltpu.roll(west, 1, 1), pltpu.roll(east, 127, 1))

    upper = iota((128, 128), 0) < 64
    for i, side in enumerate((side_x, side_y)):
        for half in range(2):
            at = slice(2 * i + half, 2 * i + half + 1)
            west = jnp.where(has_west, west_ref[4, at, :], 0.0)
            east = jnp.where(has_east, east_ref[4, at, :], 0.0)
            both = jnp.where(
                upper, jnp.broadcast_to(west, (128, 128)), jnp.broadcast_to(east, (128, 128))
            )
            side[half * 128 : half * 128 + 128, :] = both.T

    above_x = beyond(up_ref, has_up)[0]
    below_x = beyond(down_ref, has_down)[0]
    steps = height // ROWS

    def completed(row, beside, along_x):
        first, last = halves(once_ref, row)
        return [
            first + jnp.where(lane == 0, along_x[0] * beside, 0.0),
            last + jnp.where(lane == 127, along_x[1] * beside, 0.0),
        ]

    def write_out(block):
        rows = pl.ds(pl.multiple_of(block * ROWS, ROWS), ROWS)
        return (
            pltpu.make_async_copy(
                gridded_ref.at[:, rows, :], gridded_out.at[:, rows, :], sems.at[block, 0]
            ),
            pltpu.make_async_copy(
                coverage_ref.at[rows, :], coverage_out.at[rows, :], sems.at[block, 1]
            ),
        )

    @pl.loop(0, steps + 1)
    def _(g):
        block = jnp.maximum(g - 1, 0)
        for part in range(ROWS // 8):
            base = block * ROWS + part * 8
            rows = pl.ds(pl.multiple_of(base, 8), 8)
            for half in range(width // 128):
                cols = pl.ds(half * 128, 128)
                coverage = twice[half, pl.ds(base * 8 + 6, 8, stride=8), :]
                coverage_ref[rows, cols] = coverage
                scale = 1.0 / jnp.maximum(coverage, FLOOR)
                for c in range(6):
                    gridded_ref[c, rows, cols] = (
                        twice[half, pl.ds(base * 8 + c, 8, stride=8), :] * scale
                    )
        block = jnp.minimum(g, steps - 1)
        start = block * ROWS
        sides = [near[start + i] for i in range(ROWS + 2)]
        along_x = [line(cx_ref, start + i) for i in range(ROWS)]
        along_y = [line(cy_ref, start + i) for i in range(ROWS)]
        before = line(cx_ref, jnp.maximum(start - 1, 0))
        after = line(cx_ref, jnp.minimum(start + ROWS, height - 1))
        before = [jnp.where(block == 0, above_x[h], before[h]) for h in range(2)]
        after = [jnp.where(block == steps - 1, below_x[h], after[h]) for h in range(2)]
        factors = [before] + along_x + [after]
        lines = [completed(start + i, sides[i], factors[i]) for i in range(ROWS + 2)]
        for i in range(ROWS):
            beside = relax(
                sides[i + 1],
                inner_ref[start + i] + far[start + i],
                sides[i + 2] + sides[i],
                side_x[pl.ds(start + i, 1), :],
                side_y[pl.ds(start + i, 1), :],
            )
            fresh = smooth_row(*lines[i : i + 3], beside, along_x[i], along_y[i])
            for half in range(2):
                twice[half, pl.ds(pl.multiple_of((start + i) * 8, 8), 8), :] = fresh[half]

        @pl.when(g > 0)
        def _():
            for copy in write_out(g - 1):
                copy.start()

    for block in range(steps):
        for copy in write_out(block):
            copy.wait()


def second_pass(flags, once, inner, up, down, west, east, cx, cy):
    height, width = cx.shape
    vmem = pl.BlockSpec(memory_space=pltpu.VMEM)
    return pl.pallas_call(
        second_kernel,
        out_shape=(
            jax.ShapeDtypeStruct((6, height, width), f32),
            jax.ShapeDtypeStruct((height, width), f32),
        ),
        in_specs=[pl.BlockSpec(memory_space=pltpu.SMEM)] + [vmem] * 8,
        out_specs=(pl.BlockSpec(memory_space=pltpu.HBM),) * 2,
        scratch_shapes=[
            pltpu.VMEM((6, height, width), f32),
            pltpu.VMEM((height, width), f32),
            pltpu.VMEM((4, 8, 128), f32),
            pltpu.VMEM((4, 8, 128), f32),
            pltpu.VMEM((height + 2, 8, 128), f32),
            pltpu.VMEM((height, 8, 128), f32),
            pltpu.VMEM((width // 128, height * 8, 128), f32),
            pltpu.VMEM((height, 128), f32),
            pltpu.VMEM((height, 128), f32),
            pltpu.SemaphoreType.DMA((height // ROWS, 2)),
        ],
        compiler_params=pltpu.CompilerParams(vmem_limit_bytes=24 << 20),
        name="second_pass",
    )(flags, once, inner, up, down, west, east, cx, cy)


def edge_kernel(after_ref, flags_ref, cx_ref, cy_ref, top_ref, bottom_ref, left_ref, right_ref):
    height, width = cx_ref.shape
    for ref in (top_ref, bottom_ref, left_ref, right_ref):
        ref[...] = jnp.zeros_like(ref)
    for i, block in enumerate((cx_ref, cy_ref)):
        top_ref[i : i + 1, :] = block[0:1, :]
        bottom_ref[i : i + 1, :] = block[height - 1 : height, :]
        first = block[:, 0:128].T
        last = block[:, width - 128 : width].T
        for half in range(2):
            at = slice(2 * i + half, 2 * i + half + 1)
            left_ref[at, :] = first[0:1, half * 128 : half * 128 + 128]
            right_ref[at, :] = last[127:128, half * 128 : half * 128 + 128]


def coefficient_edges(after, flags, cx, cy):
    width = cx.shape[1]
    vmem = pl.BlockSpec(memory_space=pltpu.VMEM)
    row = jax.ShapeDtypeStruct((8, width), f32)
    column = jax.ShapeDtypeStruct((8, 128), f32)
    return pl.pallas_call(
        edge_kernel,
        out_shape=(row, row, column, column),
        in_specs=[vmem, pl.BlockSpec(memory_space=pltpu.SMEM), vmem, vmem],
        out_specs=(vmem,) * 4,
        compiler_params=pltpu.CompilerParams(vmem_limit_bytes=8 << 20),
        name="coefficient_edges",
    )(after, flags, cx, cy)


def body(swath_bands, clear_weight, owners, tile_row, columns, counts, conduct_x, conduct_y):
    blocks = swath_bands.shape[0]
    height, width = conduct_x.shape
    across, along = lax.axis_size("gx"), lax.axis_size("gy")
    devices = across * along
    gx, gy = lax.axis_index("gx"), lax.axis_index("gy")
    flags = jnp.stack([gy > 0, gy < along - 1, gx > 0, gx < across - 1]).astype(i32)
    message, packed = pack(
        counts,
        owners.reshape(1, blocks),
        tile_row.reshape(1, blocks),
        jnp.transpose(swath_bands, (1, 0, 2)),
        clear_weight,
        columns,
        devices,
    )
    arrived = lax.all_to_all(
        message.reshape(devices, SLOTS, 8, 128),
        ("gx", "gy"),
        split_axis=0,
        concat_axis=0,
        tiled=True,
    ).reshape(devices * SLOTS, 8, 128)

    edges = coefficient_edges(packed, flags, conduct_x, conduct_y)
    acc, top, bottom = bin_blocks(arrived, edges[0], edges[1], height, width)
    left, right = column_strips(acc, edges[2], edges[3])
    up = lax.ppermute(bottom, "gy", ring(along, 1))
    down = lax.ppermute(top, "gy", ring(along, -1))
    near = jnp.concatenate([left, up[1:2, :, 0:128], down[0:1, :, 0:128]], axis=0)
    far = jnp.concatenate([right, up[1:2, :, width - 128 :], down[0:1, :, width - 128 :]], axis=0)
    west = lax.ppermute(far, "gx", ring(across, 1))
    east = lax.ppermute(near, "gx", ring(across, -1))
    once, inner = first_pass(flags, acc, up, down, conduct_x, conduct_y)
    return second_pass(flags, once, inner, up, down, west, east, conduct_x, conduct_y)


def solution(mesh):
    return jax.shard_map(
        body,
        mesh=mesh,
        in_specs=(
            P(("gx", "gy"), None, None),
            P(("gx", "gy"), None),
            P(("gx", "gy"), None),
            P(("gx", "gy")),
            P(("gx", "gy"), None),
            P(("gx", "gy")),
            P("gy", "gx"),
            P("gy", "gx"),
        ),
        out_specs=(P(None, "gy", "gx"), P("gy", "gx")),
        check_vma=False,
    )
```

```python
import functools

import jax
import jax.numpy as jnp
from jax import lax
from jax.experimental import pallas as pl
from jax.experimental.pallas import tpu as pltpu
from jax.sharding import PartitionSpec as P

CAPACITY = 12
SLOTS = CAPACITY + 1
COUNT_LANE = 14
CODES = 16
ENTRIES = 896
GROUP = 96
FIRST_ROWS = 128
ROWS = 32
FLOOR = 0.15
HALO = 2

f32 = jnp.float32
bf16 = jnp.bfloat16
i32 = jnp.int32


def iota(shape, dim):
    return lax.broadcasted_iota(i32, shape, dim)


def ring(count, step):
    return [(i, (i + step) % count) for i in range(count)]


def pack_kernel(
    count_ref,
    owner_ref,
    row_ref,
    swath_ref,
    weight_ref,
    cols_ref,
    out_ref,
    done_ref,
    owner_v,
    row_v,
    swath_v,
    weight_v,
    cols_v,
    rows_f,
    codes_f,
    slot_v,
    slot_s,
    sem,
    load_sems,
):
    bands, blocks, _ = swath_ref.shape
    loads = [
        pltpu.make_async_copy(source, target, load_sems.at[i])
        for i, (source, target) in enumerate(
            (
                (owner_ref, owner_v),
                (row_ref, row_v),
                (weight_ref, weight_v),
                (cols_ref, cols_v),
                (swath_ref, swath_v),
            )
        )
    ]
    for load in loads:
        load.start()
    done_ref[...] = jnp.zeros((8, 128), f32)
    devices = out_ref.shape[0] // SLOTS
    live_count = count_ref[0]
    chunk = iota((128, 256), 1)
    earlier = ((iota((128, 256), 0) < chunk) | (chunk >= 128)).astype(f32).astype(bf16)

    @pl.loop(0, devices // 2)
    def _(t):
        out_ref[pl.ds(t * 2 * SLOTS, 2 * SLOTS)] = jnp.zeros((2 * SLOTS, 8, 128), bf16)

    loads[0].wait()
    owner = owner_v[...]
    live = iota((1, blocks), 1) < live_count
    owner = jnp.where(live, owner, -1)
    named = (iota((devices, blocks), 0) == owner).astype(f32)
    named16 = named.astype(bf16)
    before, seen = [], jnp.zeros((devices, 128), f32)
    for first in range(0, blocks, 128):
        found = jnp.dot(
            named16[:, first : first + 128], earlier, preferred_element_type=f32
        )
        before.append(seen + found[:, 0:128])
        seen = seen + found[:, 128:256]
    before = jnp.concatenate(before, axis=1)
    rank = jnp.sum(named * before, axis=0, keepdims=True).astype(i32)
    slot_v[...] = jnp.where(live, owner * SLOTS + rank, CAPACITY)
    copy = pltpu.make_async_copy(slot_v, slot_s, sem)
    copy.start()
    entry = iota((128, blocks), 0)
    loads[1].wait()
    place = jnp.where(entry == rank, (row_v[...] + 1).astype(f32), 0.0)
    place = jnp.where(entry == COUNT_LANE, 1.0, place).astype(bf16)
    codes_f[...] = lax.dot_general(
        named16, place, (((1,), (1,)), ((), ())), preferred_element_type=f32
    )

    for load in loads[2:]:
        load.wait()

    @pl.loop(0, blocks // 16, unroll=8)
    def _(g):
        near = pl.ds(pl.multiple_of(g * 16, 16), 16)
        weight = weight_v[near, :].astype(f32)
        for c in range(bands):
            rows_f[pl.ds(g * 128 + c, 16, stride=8), :] = swath_v[c, near, :].astype(f32) * weight
        rows_f[pl.ds(g * 128 + bands, 16, stride=8), :] = weight
        rows_f[pl.ds(g * 128 + bands + 1, 16, stride=8), :] = cols_v[near, :].astype(f32)

    copy.wait()

    @pl.loop(0, (live_count + 31) // 32)
    def _(group):
        for i in range(32):
            b = group * 32 + i
            out_ref[slot_s[0, b]] = rows_f[pl.ds(pl.multiple_of(b * 8, 8), 8), :].astype(bf16)

    @pl.loop(0, devices, unroll=16)
    def _(t):
        code = codes_f[pl.ds(t, 1), :]
        out_ref[t * SLOTS + CAPACITY] = jnp.broadcast_to(code, (8, 128)).astype(bf16)


def pack(counts, owners, tile_row, swath, weight, columns, devices):
    blocks = weight.shape[0]
    vmem = pl.BlockSpec(memory_space=pltpu.VMEM)
    return pl.pallas_call(
        pack_kernel,
        out_shape=(
            jax.ShapeDtypeStruct((devices * SLOTS, 8, 128), bf16),
            jax.ShapeDtypeStruct((8, 128), f32),
        ),
        in_specs=[pl.BlockSpec(memory_space=pltpu.SMEM)]
        + [pl.BlockSpec(memory_space=pltpu.HBM)] * 5,
        out_specs=(vmem, vmem),
        scratch_shapes=[
            pltpu.VMEM((1, blocks), i32),
            pltpu.VMEM((1, blocks), i32),
            pltpu.VMEM(swath.shape, bf16),
            pltpu.VMEM(weight.shape, bf16),
            pltpu.VMEM(columns.shape, i32),
            pltpu.VMEM((blocks * 8, 128), f32),
            pltpu.VMEM((devices, 128), f32),
            pltpu.VMEM((1, blocks), i32),
            pltpu.SMEM((1, blocks), i32),
            pltpu.SemaphoreType.DMA,
            pltpu.SemaphoreType.DMA((5,)),
        ],
        compiler_params=pltpu.CompilerParams(vmem_limit_bytes=60 << 20),
        name="pack",
    )(counts, owners, tile_row, swath, weight, columns)


def bin_kernel(
    msg_ref,
    edge_top,
    edge_bottom,
    acc_ref,
    top_ref,
    bottom_ref,
    codes_v,
    lists_v,
    lists_s,
    sem,
):
    sources = msg_ref.shape[0] // SLOTS
    height = acc_ref.shape[0] - 1

    @pl.loop(0, sources // 16)
    def _(g):
        for i in range(16):
            s = g * 16 + i
            tile = msg_ref[s * SLOTS + CAPACITY].astype(f32)
            codes_v[pl.ds(s, 1), :] = tile[0:1, :]

    codes = codes_v[...].T[0:CODES, :]
    pairs = jnp.floor((codes[COUNT_LANE : COUNT_LANE + 1, :] + 1.0) * 0.5)
    earlier = (iota((sources, sources), 0) < iota((sources, sources), 1)).astype(f32).astype(bf16)
    before = jnp.dot(
        jnp.broadcast_to(pairs, (8, sources)).astype(bf16), earlier, preferred_element_type=f32
    )[0:1, :]
    total = (before + pairs)[:, sources - 1 : sources]
    entry = iota((ENTRIES, sources), 0).astype(f32)
    source = iota((1, sources), 1).astype(f32)
    facts, places = [], []
    for p in range(CAPACITY // 2):
        facts.append(
            jnp.concatenate(
                [
                    codes[2 * p : 2 * p + 2, :],
                    source,
                    jnp.full((1, sources), 2.0 * p, f32),
                    jnp.zeros((4, sources), f32),
                ],
                axis=0,
            ).astype(bf16)
        )
        place = jnp.where(pairs > p, before + p, -1.0)
        places.append(jnp.where(entry == place, 1.0, 0.0).astype(bf16))
    found = lax.dot_general(
        jnp.concatenate(facts, axis=1),
        jnp.concatenate(places, axis=1),
        (((1,), (1,)), ((), ())),
        preferred_element_type=f32,
    )
    rows = jnp.where(found[0:2] > 0.0, found[0:2] - 1.0, float(height))
    slots = found[2:3] * SLOTS + found[3:4]
    lists_v[0:1, :] = slots.astype(i32)
    lists_v[1:3, :] = rows.astype(i32)
    lists_v[3:4, :] = jnp.broadcast_to(total, (1, ENTRIES)).astype(i32)
    copy = pltpu.make_async_copy(lists_v, lists_s, sem)
    copy.start()

    @pl.loop(0, height // 16)
    def _(g):
        acc_ref[pl.ds(g * 16, 16)] = jnp.zeros((16, 32, 128), f32)

    acc_ref[height] = jnp.zeros((32, 128), f32)
    copy.wait()
    ids = iota((16, 128), 0).astype(f32)
    low_ids = [(ids + 16.0 * k).astype(bf16) for k in range(4)]
    quarter_ids = [(2.0 * k + jnp.floor(ids * 0.125)).astype(bf16) for k in range(2)]
    one = jnp.ones((16, 128), bf16)
    zero = jnp.zeros((16, 128), bf16)
    empty = jnp.zeros((32, 128), bf16)

    @pl.loop(0, (lists_s[3, 0] + GROUP - 1) // GROUP)
    def _(group):
        for j in range(GROUP):
            slot = lists_s[0, group * GROUP + j]
            values, hits = [], []
            for i in range(2):
                block = msg_ref[slot + i].astype(f32)
                col = jnp.broadcast_to(block[7:8, :], (8, 128))
                quarter = jnp.floor(col * (1.0 / 64.0))
                low = col - 64.0 * quarter
                block, quarter, low = (
                    jnp.concatenate([x, x], axis=0).astype(bf16) for x in (block, quarter, low)
                )
                values.append(
                    jnp.concatenate([jnp.where(q == quarter, block, zero) for q in quarter_ids], axis=0)
                )
                hits.append(
                    jnp.concatenate([jnp.where(k == low, one, zero) for k in low_ids], axis=0)
                )
            values = jnp.concatenate(
                [
                    jnp.concatenate([values[0], empty], axis=1),
                    jnp.concatenate([empty, values[1]], axis=1),
                ],
                axis=0,
            )
            sums = lax.dot_general(
                values,
                jnp.concatenate(hits, axis=1),
                (((1,), (1,)), ((), ())),
                preferred_element_type=f32,
            )
            row_0 = lists_s[1, group * GROUP + j]
            row_1 = lists_s[2, group * GROUP + j]
            shared = jnp.where(row_0 == row_1, sums[0:32], 0.0)
            sum_0 = acc_ref[row_0, :, 0:64] + sums[0:32]
            sum_1 = acc_ref[row_1, :, 0:64] + (sums[32:64] + shared)
            acc_ref[row_0, :, 0:64] = sum_0
            acc_ref[row_1, :, 0:64] = sum_1

    for ref, first, edge in ((top_ref, 0, edge_top), (bottom_ref, height - HALO, edge_bottom)):
        for i in range(HALO):
            for h, half in enumerate(join_quarters(acc_ref[first + i])):
                ref[i, :, 128 * h : 128 * h + 128] = half
        ref[HALO] = edge[...]


def join_quarters(tile):
    quarters = [tile[8 * q : 8 * q + 8] for q in range(4)]
    return [quarters[2 * h] + pltpu.roll(quarters[2 * h + 1], 64, 1) for h in range(2)]


def bin_blocks(message, edge_top, edge_bottom, height, width):
    sources = message.shape[0] // SLOTS
    vmem = pl.BlockSpec(memory_space=pltpu.VMEM)
    shape = lambda *dims: jax.ShapeDtypeStruct(dims, f32)
    return pl.pallas_call(
        bin_kernel,
        out_shape=(
            shape(height + 1, 32, 128),
            shape(HALO + 1, 8, width),
            shape(HALO + 1, 8, width),
        ),
        in_specs=[vmem] * 3,
        out_specs=(vmem,) * 3,
        scratch_shapes=[
            pltpu.VMEM((sources, 128), f32),
            pltpu.VMEM((8, ENTRIES), i32),
            pltpu.SMEM((8, ENTRIES), i32),
            pltpu.SemaphoreType.DMA,
        ],
        compiler_params=pltpu.CompilerParams(vmem_limit_bytes=16 << 20),
        name="bin",
    )(message, edge_top, edge_bottom)


def strip_kernel(acc_ref, edge_left, edge_right, left_ref, right_ref):
    lane = iota((8, 128), 1)
    blank = jnp.zeros((8, 128), f32)

    def take(j, carry):
        here = lane // 2 == j
        result = []
        for q in range(4):
            first = pltpu.roll(acc_ref[q * 64 + j, 0:8], 2 * j, 1)
            last = pltpu.roll(acc_ref[q * 64 + j, 24:32], (2 * j + 66) % 128, 1)
            result.append(jnp.where(here, first, carry[2 * q]))
            result.append(jnp.where(here, last, carry[2 * q + 1]))
        return tuple(result)

    strips = lax.fori_loop(0, 64, take, (blank,) * 8, unroll=16)
    for q in range(4):
        left_ref[q] = strips[2 * q]
        right_ref[q] = strips[2 * q + 1]
    left_ref[4] = edge_left[...]
    right_ref[4] = edge_right[...]


def column_strips(acc, edge_left, edge_right):
    vmem = pl.BlockSpec(memory_space=pltpu.VMEM)
    strip = jax.ShapeDtypeStruct(((acc.shape[0] - 1) // 64 + 1, 8, 128), f32)
    return pl.pallas_call(
        strip_kernel,
        out_shape=(strip, strip),
        in_specs=[vmem] * 3,
        out_specs=(vmem,) * 2,
        compiler_params=pltpu.CompilerParams(vmem_limit_bytes=12 << 20),
        name="column_strips",
    )(acc, edge_left, edge_right)


def relax(current, east_west, north_south, along_x, along_y):
    return current + along_x * (east_west - 2.0 * current) + along_y * (north_south - 2.0 * current)


def smooth_row(above, current, below, near, along_x, along_y):
    lane = iota((8, 128), 1)
    ahead = [pltpu.roll(half, 1, 1) for half in current]
    back = [pltpu.roll(half, 127, 1) for half in current]
    west = [jnp.where(lane == 0, near, ahead[0]), jnp.where(lane == 0, ahead[0], ahead[1])]
    east = [jnp.where(lane == 127, back[1], back[0]), jnp.where(lane == 127, near, back[1])]
    return [
        relax(current[h], east[h] + west[h], below[h] + above[h], along_x[h], along_y[h])
        for h in range(2)
    ]


def halves(ref, row):
    return [ref[row, :, 0:128], ref[row, :, 128:256]]


def keep(flag, parts):
    return [jnp.where(flag, part, 0.0) for part in parts]


def line(ref, row):
    both = ref[pl.ds(row, 1), :]
    return [both[:, 0:128], both[:, 128:256]]


def beyond(ref, flag):
    return [
        keep(flag, [ref[HALO, i : i + 1, h * 128 : h * 128 + 128] for h in range(2)])
        for i in range(2)
    ]


def first_kernel(flags_ref, acc_ref, up_ref, down_ref, cx_ref, cy_ref, once_ref, inner_ref):
    height = inner_ref.shape[0]
    has_up, has_down = flags_ref[0] > 0, flags_ref[1] > 0
    lane = iota((8, 128), 1)
    blank = jnp.zeros((8, 128), f32)
    up = [keep(has_up, halves(up_ref, i)) for i in range(2)]
    down = [keep(has_down, halves(down_ref, i)) for i in range(2)]

    def store(row, parts):
        once_ref[row, :, 0:128] = parts[0]
        once_ref[row, :, 128:256] = parts[1]

    store(0, smooth_row(up[0], up[1], join_quarters(acc_ref[0]), blank, *beyond(up_ref, has_up)))
    store(
        height + 1,
        smooth_row(
            join_quarters(acc_ref[height - 1]),
            down[0],
            down[1],
            blank,
            *beyond(down_ref, has_down),
        ),
    )
    steps = height // FIRST_ROWS

    @pl.loop(0, steps)
    def _(block):
        start = block * FIRST_ROWS
        before = join_quarters(acc_ref[jnp.maximum(start - 1, 0)])
        after = join_quarters(acc_ref[jnp.minimum(start + FIRST_ROWS, height - 1)])
        before = [jnp.where(block == 0, up[1][h], before[h]) for h in range(2)]
        after = [jnp.where(block == steps - 1, down[0][h], after[h]) for h in range(2)]
        lines = [before] + [join_quarters(acc_ref[start + i]) for i in range(FIRST_ROWS)] + [after]
        for i in range(FIRST_ROWS):
            fresh = smooth_row(
                *lines[i : i + 3], blank, line(cx_ref, start + i), line(cy_ref, start + i)
            )
            store(start + i + 1, fresh)
            inner_ref[start + i] = jnp.where(lane < 64, lines[i + 1][0], lines[i + 1][1])


def first_pass(flags, acc, up, down, cx, cy):
    height, width = cx.shape
    vmem = pl.BlockSpec(memory_space=pltpu.VMEM)
    return pl.pallas_call(
        first_kernel,
        out_shape=(
            jax.ShapeDtypeStruct((height + 2, 8, width), f32),
            jax.ShapeDtypeStruct((height, 8, 128), f32),
        ),
        in_specs=[pl.BlockSpec(memory_space=pltpu.SMEM)] + [vmem] * 5,
        out_specs=(vmem, vmem),
        compiler_params=pltpu.CompilerParams(vmem_limit_bytes=20 << 20),
        name="first_pass",
    )(flags, acc, up, down, cx, cy)


def second_kernel(
    flags_ref,
    once_ref,
    inner_ref,
    up_ref,
    down_ref,
    west_ref,
    east_ref,
    cx_ref,
    cy_ref,
    gridded_out,
    coverage_out,
    gridded_ref,
    coverage_ref,
    mix_near,
    mix_far,
    near,
    far,
    twice,
    side_x,
    side_y,
    sems,
):
    height, width = cx_ref.shape
    has_up, has_down = flags_ref[0] > 0, flags_ref[1] > 0
    has_west, has_east = flags_ref[2] > 0, flags_ref[3] > 0
    lane = iota((8, 128), 1)

    for q in range(4):
        west = jnp.where(has_west, west_ref[q], 0.0)
        east = jnp.where(has_east, east_ref[q], 0.0)
        even = lane % 2 == 0
        mix_near[q] = jnp.where(even, pltpu.roll(west, 127, 1), pltpu.roll(east, 127, 1))
        mix_far[q] = jnp.where(even, west, pltpu.roll(east, 126, 1))

    @pl.loop(0, 64, unroll=64)
    def _(j):
        for q in range(4):
            near[q * 64 + j + 1] = pltpu.roll(mix_near[q], 128 - 2 * j, 1)
            far[q * 64 + j] = pltpu.roll(mix_far[q], 128 - 2 * j, 1)

    for tile, row, flag in ((5, 0, has_up), (6, height + 1, has_down)):
        west = jnp.where(has_west & flag, west_ref[tile], 0.0)
        east = jnp.where(has_east & flag, east_ref[tile], 0.0)
        near[row] = jnp.where(lane < 64, pltpu.roll(west, 1, 1), pltpu.roll(east, 127, 1))

    upper = iota((128, 128), 0) < 64
    for i, side in enumerate((side_x, side_y)):
        for half in range(2):
            at = slice(2 * i + half, 2 * i + half + 1)
            west = jnp.where(has_west, west_ref[4, at, :], 0.0)
            east = jnp.where(has_east, east_ref[4, at, :], 0.0)
            both = jnp.where(
                upper, jnp.broadcast_to(west, (128, 128)), jnp.broadcast_to(east, (128, 128))
            )
            side[half * 128 : half * 128 + 128, :] = both.T

    above_x = beyond(up_ref, has_up)[0]
    below_x = beyond(down_ref, has_down)[0]
    steps = height // ROWS

    def completed(row, beside, along_x):
        first, last = halves(once_ref, row)
        return [
            first + jnp.where(lane == 0, along_x[0] * beside, 0.0),
            last + jnp.where(lane == 127, along_x[1] * beside, 0.0),
        ]

    def write_out(block):
        rows = pl.ds(pl.multiple_of(block * ROWS, ROWS), ROWS)
        return (
            pltpu.make_async_copy(
                gridded_ref.at[:, rows, :], gridded_out.at[:, rows, :], sems.at[block, 0]
            ),
            pltpu.make_async_copy(
                coverage_ref.at[rows, :], coverage_out.at[rows, :], sems.at[block, 1]
            ),
        )

    @pl.loop(0, steps + 1)
    def _(g):
        block = jnp.maximum(g - 1, 0)
        for part in range(ROWS // 8):
            base = block * ROWS + part * 8
            rows = pl.ds(pl.multiple_of(base, 8), 8)
            for half in range(width // 128):
                cols = pl.ds(half * 128, 128)
                coverage = twice[half, pl.ds(base * 8 + 6, 8, stride=8), :]
                coverage_ref[rows, cols] = coverage
                scale = 1.0 / jnp.maximum(coverage, FLOOR)
                for c in range(6):
                    gridded_ref[c, rows, cols] = (
                        twice[half, pl.ds(base * 8 + c, 8, stride=8), :] * scale
                    )
        block = jnp.minimum(g, steps - 1)
        start = block * ROWS
        sides = [near[start + i] for i in range(ROWS + 2)]
        along_x = [line(cx_ref, start + i) for i in range(ROWS)]
        along_y = [line(cy_ref, start + i) for i in range(ROWS)]
        before = line(cx_ref, jnp.maximum(start - 1, 0))
        after = line(cx_ref, jnp.minimum(start + ROWS, height - 1))
        before = [jnp.where(block == 0, above_x[h], before[h]) for h in range(2)]
        after = [jnp.where(block == steps - 1, below_x[h], after[h]) for h in range(2)]
        factors = [before] + along_x + [after]
        lines = [completed(start + i, sides[i], factors[i]) for i in range(ROWS + 2)]
        for i in range(ROWS):
            beside = relax(
                sides[i + 1],
                inner_ref[start + i] + far[start + i],
                sides[i + 2] + sides[i],
                side_x[pl.ds(start + i, 1), :],
                side_y[pl.ds(start + i, 1), :],
            )
            fresh = smooth_row(*lines[i : i + 3], beside, along_x[i], along_y[i])
            for half in range(2):
                twice[half, pl.ds(pl.multiple_of((start + i) * 8, 8), 8), :] = fresh[half]

        @pl.when(g > 0)
        def _():
            for copy in write_out(g - 1):
                copy.start()

    for block in range(steps):
        for copy in write_out(block):
            copy.wait()


def second_pass(flags, once, inner, up, down, west, east, cx, cy):
    height, width = cx.shape
    vmem = pl.BlockSpec(memory_space=pltpu.VMEM)
    return pl.pallas_call(
        second_kernel,
        out_shape=(
            jax.ShapeDtypeStruct((6, height, width), f32),
            jax.ShapeDtypeStruct((height, width), f32),
        ),
        in_specs=[pl.BlockSpec(memory_space=pltpu.SMEM)] + [vmem] * 8,
        out_specs=(pl.BlockSpec(memory_space=pltpu.HBM),) * 2,
        scratch_shapes=[
            pltpu.VMEM((6, height, width), f32),
            pltpu.VMEM((height, width), f32),
            pltpu.VMEM((4, 8, 128), f32),
            pltpu.VMEM((4, 8, 128), f32),
            pltpu.VMEM((height + 2, 8, 128), f32),
            pltpu.VMEM((height, 8, 128), f32),
            pltpu.VMEM((width // 128, height * 8, 128), f32),
            pltpu.VMEM((height, 128), f32),
            pltpu.VMEM((height, 128), f32),
            pltpu.SemaphoreType.DMA((height // ROWS, 2)),
        ],
        compiler_params=pltpu.CompilerParams(vmem_limit_bytes=24 << 20),
        name="second_pass",
    )(flags, once, inner, up, down, west, east, cx, cy)


def edge_kernel(after_ref, flags_ref, cx_ref, cy_ref, top_ref, bottom_ref, left_ref, right_ref):
    height, width = cx_ref.shape
    for ref in (top_ref, bottom_ref, left_ref, right_ref):
        ref[...] = jnp.zeros_like(ref)
    for i, block in enumerate((cx_ref, cy_ref)):
        top_ref[i : i + 1, :] = block[0:1, :]
        bottom_ref[i : i + 1, :] = block[height - 1 : height, :]
        first = block[:, 0:128].T
        last = block[:, width - 128 : width].T
        for half in range(2):
            at = slice(2 * i + half, 2 * i + half + 1)
            left_ref[at, :] = first[0:1, half * 128 : half * 128 + 128]
            right_ref[at, :] = last[127:128, half * 128 : half * 128 + 128]


def coefficient_edges(after, flags, cx, cy):
    width = cx.shape[1]
    vmem = pl.BlockSpec(memory_space=pltpu.VMEM)
    row = jax.ShapeDtypeStruct((8, width), f32)
    column = jax.ShapeDtypeStruct((8, 128), f32)
    return pl.pallas_call(
        edge_kernel,
        out_shape=(row, row, column, column),
        in_specs=[vmem, pl.BlockSpec(memory_space=pltpu.SMEM), vmem, vmem],
        out_specs=(vmem,) * 4,
        compiler_params=pltpu.CompilerParams(vmem_limit_bytes=8 << 20),
        name="coefficient_edges",
    )(after, flags, cx, cy)


def body(swath_bands, clear_weight, owners, tile_row, columns, counts, conduct_x, conduct_y):
    blocks = swath_bands.shape[0]
    height, width = conduct_x.shape
    across, along = lax.axis_size("gx"), lax.axis_size("gy")
    devices = across * along
    gx, gy = lax.axis_index("gx"), lax.axis_index("gy")
    flags = jnp.stack([gy > 0, gy < along - 1, gx > 0, gx < across - 1]).astype(i32)
    message, packed = pack(
        counts,
        owners.reshape(1, blocks),
        tile_row.reshape(1, blocks),
        jnp.transpose(swath_bands, (1, 0, 2)),
        clear_weight,
        columns,
        devices,
    )
    arrived = lax.all_to_all(
        message.reshape(devices, SLOTS, 8, 128),
        ("gx", "gy"),
        split_axis=0,
        concat_axis=0,
        tiled=True,
    ).reshape(devices * SLOTS, 8, 128)

    edges = coefficient_edges(packed, flags, conduct_x, conduct_y)
    acc, top, bottom = bin_blocks(arrived, edges[0], edges[1], height, width)
    left, right = column_strips(acc, edges[2], edges[3])
    up = lax.ppermute(bottom, "gy", ring(along, 1))
    down = lax.ppermute(top, "gy", ring(along, -1))
    near = jnp.concatenate([left, up[1:2, :, 0:128], down[0:1, :, 0:128]], axis=0)
    far = jnp.concatenate([right, up[1:2, :, width - 128 :], down[0:1, :, width - 128 :]], axis=0)
    west = lax.ppermute(far, "gx", ring(across, 1))
    east = lax.ppermute(near, "gx", ring(across, -1))
    once, inner = first_pass(flags, acc, up, down, conduct_x, conduct_y)
    return second_pass(flags, once, inner, up, down, west, east, conduct_x, conduct_y)


def solution(mesh):
    return jax.shard_map(
        body,
        mesh=mesh,
        in_specs=(
            P(("gx", "gy"), None, None),
            P(("gx", "gy"), None),
            P(("gx", "gy"), None),
            P(("gx", "gy")),
            P(("gx", "gy"), None),
            P(("gx", "gy")),
            P("gy", "gx"),
            P("gy", "gx"),
        ),
        out_specs=(P(None, "gy", "gx"), P("gy", "gx")),
        check_vma=False,
    )
```
